256 devices in a mesh: step: 4 (over y), tile: 64 (over z, x, core).
Axes of the slice: x: 4, y: 4, z: 8, core: 2. Of those that a mesh axis runs over, the one named last changes fastest.
Arguments:
- start_state: float32 [4, 512, 128], P(None, 'tile'), may hold values from -6 to 6
- covariates: bfloat16 [12, 512, 128], P(None, 'tile'), may hold values from -6 to 6
- noise: float32 [8, 4, 512, 128], P('step', None, 'tile'), may hold values from -6 to 6
- embedding: float32 [8, 128], P('step'), may hold values from -4 to 4
- w_in: bfloat16 [9, 128, 16], replicated, may hold values from -0.5 to 0.5
- w_first: bfloat16 [9, 128, 128], replicated, may hold values from -0.1875 to 0.1875
- w_second: bfloat16 [9, 128, 128], replicated, may hold values from -0.1875 to 0.1875
- w_out: bfloat16 [4, 128], replicated, may hold values from -0.5 to 0.5
Outputs:
- states: float32 [8, 4, 512, 128], P('step', None, 'tile')
The draws below stay inside these ranges and needn't reach their ends.
All inputs are finite; a program needn't handle non-finite values.
Results may differ from the reference program's by a relative error of at most 0.0013.
Values may be sent and summed in bfloat16 or wider, within the bound.
A program may use at most 64 MiB of HBM per device.

```python
import jax
import jax.numpy as jnp

CH = 4
COV = 12
IN_CH = 16
HID = 128
STEPS = 8
SWEEPS = 2
ROWS = 128
NC = 512


def block_scale(rng, extent, pieces, low, top_value):
    def one(axis_at, blocks):
        draws = jax.random.uniform(jax.random.fold_in(jax.random.fold_in(rng, 6), axis_at), (blocks,), jnp.float32, low / len(pieces), top_value / len(pieces))
        return jnp.repeat(jnp.exp(draws), extent[axis_at] // blocks).reshape((-1,) + (1,) * (len(extent) - axis_at - 1))

    gain = one(*pieces[0])
    for cut in pieces[1:]:
        gain = gain * one(*cut)
    return gain


def gaussian(stream_key, dims, spread, most, shards=(), kind=jnp.bfloat16):
    result = spread * jax.random.normal(stream_key, dims, jnp.float32)
    if shards:
        result = result * block_scale(stream_key, dims, shards, -0.22, 0.18)
    return jnp.clip(result, -most, most).astype(kind)


def setup_inputs(seed: int = 0) -> dict:
    key_of = jax.random.split(jax.random.key(seed), 9)
    return {
        "start_state": gaussian(key_of[0], (CH, NC, ROWS), 1.0, 6.0, ((1, 64),), jnp.float32),
        "covariates": gaussian(key_of[1], (COV, NC, ROWS), 1.0, 6.0, ((1, 64),)),
        "noise": gaussian(key_of[2], (STEPS, CH, NC, ROWS), 1.0, 6.0, ((0, 4), (2, 64)), jnp.float32),
        "embedding": gaussian(key_of[3], (STEPS, HID), 0.7, 4.0, ((0, 4),), jnp.float32),
        "w_in": gaussian(key_of[4], (9, HID, IN_CH), (9 * IN_CH) ** -0.5, 0.5),
        "w_first": gaussian(key_of[5], (9, HID, HID), (9 * HID) ** -0.5, 0.1875),
        "w_second": gaussian(key_of[6], (9, HID, HID), (9 * HID) ** -0.5, 0.1875),
        "w_out": gaussian(key_of[7], (CH, HID), HID ** -0.5, 0.5),
    }


def conv_field(field, weight):
    channels, columns, rows = field.shape
    padded = jnp.pad(field.astype(jnp.float32), ((0, 0), (1, 1), (1, 1)))
    total = jnp.zeros((weight.shape[1], columns, rows), jnp.float32)
    for col_off in range(3):
        for row_off in range(3):
            piece = padded[:, col_off:col_off + columns, row_off:row_off + rows]
            total = total + jnp.einsum("oi,icr->ocr", weight[3 * col_off + row_off].astype(jnp.float32), piece)
    return total


def drift_of(state, step_noise, step_embed, covariates, w_in, w_first, w_second, w_out):
    inputs = jnp.concatenate([state.astype(jnp.bfloat16), covariates], axis=0)
    first_hidden = jax.nn.silu(conv_field(inputs, w_in) + step_embed[:, None, None]).astype(jnp.bfloat16)
    second_hidden = jax.nn.silu(conv_field(first_hidden, w_first)).astype(jnp.bfloat16)
    block_out = (jax.nn.silu(conv_field(second_hidden, w_second)) + first_hidden.astype(jnp.float32)).astype(jnp.bfloat16)
    projected = jnp.einsum("oi,icr->ocr", w_out.astype(jnp.float32), block_out.astype(jnp.float32))
    return projected / STEPS + 0.3 * step_noise


def reference(start_state, covariates, noise, embedding, w_in, w_first, w_second, w_out):
    guesses = [start_state for step_index in range(STEPS)]
    results = []
    for sweep_index in range(SWEEPS):
        drifts = [drift_of(guesses[k], noise[k], embedding[k], covariates, w_in, w_first, w_second, w_out) for k in range(STEPS)]
        running = start_state
        results = []
        for k in range(STEPS):
            running = running + drifts[k]
            results.append(running)
        guesses = [start_state] + results[:-1]
    return jnp.stack(results, axis=0)
```

```python
import jax
import jax.numpy as jnp
from jax import lax
from jax.experimental import pallas as pl
from jax.experimental.pallas import tpu as pltpu
from jax.sharding import PartitionSpec as P

STEPS = 8
SWEEPS = 2
HALO = 3
BF = jnp.bfloat16
F32 = jnp.float32
MESH = pl.DeviceIdType.MESH


def silu(v):
    h = 0.5 * v
    return h * jnp.tanh(h) + h


def kernel(
    groups,
    tiles,
    start_ref,
    cov_ref,
    noise_ref,
    embed_ref,
    win_hbm,
    wfirst_hbm,
    wsecond_hbm,
    wout_ref,
    out_ref,
    x_ref,
    covf_ref,
    xs_ref,
    win_ref,
    w1_ref,
    w2_ref,
    w3_ref,
    wo_ref,
    eb_ref,
    nz_ref,
    fh_ref,
    sh_ref,
    bo_ref,
    part_ref,
    part_a,
    part_g,
    rx_ref,
    rxs_ref,
    rxf_ref,
    w_sem,
    halo_send,
    halo_recv,
    full_send,
    full_recv,
    edge_send,
    edge_recv,
    near_send,
    near_recv,
    last_send,
    last_recv,
):
    k = lax.axis_index("step")
    t = lax.axis_index("tile")
    cols = start_ref.shape[1]
    wide = cols + 2 * HALO
    rows = 128
    edge = HALO * rows
    has_left = t > 0
    has_right = t < tiles - 1

    win_copy = pltpu.make_async_copy(win_hbm, win_ref, w_sem.at[0])
    win_copy.start()
    copies = []
    for n, (src, dst) in enumerate(((wfirst_hbm, w2_ref), (wsecond_hbm, w3_ref))):
        group = []
        for tap in range(9):
            c = pltpu.make_async_copy(
                src.at[tap], dst.at[:, pl.ds(tap * 128, 128)], w_sem.at[1 + 9 * n + tap]
            )
            c.start()
            group.append(c)
        copies.append(group)

    barrier = pltpu.get_barrier_semaphore()

    def signal(step, tile):
        pl.semaphore_signal(barrier, inc=1, device_id=(step, tile), device_id_type=MESH)

    for side, there in ((-1, has_left), (1, has_right)):

        @pl.when(there)
        def _():
            signal(k, t + side)

        for d in range(1, groups):

            @pl.when(there & (k >= d))
            def _():
                signal(k - d, t + side)

    for d in range(1, groups):

        @pl.when(k >= d)
        def _():
            signal(k - d, t)

    sides = has_left.astype(jnp.int32) + has_right.astype(jnp.int32)
    later = groups - 1 - k

    covf_ref[...] = cov_ref[...].astype(F32)
    for c in range(cols):
        at = pl.ds((HALO + c) * rows, rows)
        x_ref[0:4, at] = start_ref[:, c, :]
        x_ref[4:16, at] = covf_ref[:, c, :]

    pl.semaphore_wait(barrier, sides + later * (1 + sides))

    def remote(src, dst, send, recv, step, tile):
        return pltpu.make_async_remote_copy(
            src_ref=src,
            dst_ref=dst,
            send_sem=send,
            recv_sem=recv,
            device_id=(step, tile),
            device_id_type=MESH,
        )

    own = pl.ds(HALO * rows, cols * rows)
    own_first = pl.ds(HALO * rows, edge)
    own_last = pl.ds(cols * rows, edge)
    left_halo = pl.ds(0, edge)
    right_halo = pl.ds((HALO + cols) * rows, edge)
    first_edge = pl.ds(0, edge)
    last_edge = pl.ds((cols - HALO) * rows, edge)

    def halo_left():
        return remote(
            x_ref.at[:, own_first], x_ref.at[:, right_halo], halo_send.at[0], halo_recv.at[0], k, t - 1
        )

    def halo_right():
        return remote(
            x_ref.at[:, own_last], x_ref.at[:, left_halo], halo_send.at[1], halo_recv.at[1], k, t + 1
        )

    @pl.when(has_left)
    def _():
        halo_left().start()

    @pl.when(has_right)
    def _():
        halo_right().start()

    @pl.when(jnp.logical_not(has_left))
    def _():
        x_ref[:, left_halo] = jnp.zeros((16, edge), F32)

    @pl.when(jnp.logical_not(has_right))
    def _():
        x_ref[:, right_halo] = jnp.zeros((16, edge), F32)

    win_copy.wait()
    w1_ref[...] = jnp.concatenate([win_ref[tap] for tap in range(9)], axis=1)
    wo = wout_ref[...]
    zero_wo = jnp.zeros_like(wo)
    wo_ref[0:4, 0:128] = wo
    wo_ref[0:4, 128:256] = zero_wo
    wo_ref[4:8, 0:128] = wo
    wo_ref[4:8, 128:256] = wo
    et = jnp.transpose(jnp.concatenate([embed_ref[...], jnp.zeros((6, 128), F32)], axis=0))
    for s in range(2):
        eb_ref[s] = jnp.broadcast_to(et[:, s : s + 1], (128, 128))
    for c in range(cols):
        at = pl.ds(c * rows, rows)
        n0 = 0.3 * noise_ref[0, :, c, :]
        nz_ref[0:4, at] = n0
        nz_ref[4:8, at] = n0 + 0.3 * noise_ref[1, :, c, :]

    @pl.when(has_left)
    def _():
        halo_left().wait_send()

    @pl.when(has_right)
    def _():
        halo_right().wait_send()

    @pl.when(has_left)
    def _():
        halo_right().wait_recv()

    @pl.when(has_right)
    def _():
        halo_left().wait_recv()

    lane = lax.broadcasted_iota(jnp.int32, (1, 2 * rows), 1) % rows
    keep_first = (lane > 0).astype(F32)
    keep_last = (lane < rows - 1).astype(F32)

    def store_taps(ref, value, lo, width):
        n = value.shape[0]
        for part in range(width):
            v = value[:, part * rows : (part + 1) * rows]
            at = pl.ds(lo + part * rows, rows)
            ref[0:n, at] = (pltpu.roll(v, 1, 1) * keep_first[:, :rows]).astype(BF)
            ref[n : 2 * n, at] = v.astype(BF)
            ref[2 * n : 3 * n, at] = (pltpu.roll(v, rows - 1, 1) * keep_last[:, :rows]).astype(BF)

    def taps_of(ref, lo):
        return jnp.concatenate(
            [ref[:, pl.ds(lo + a * rows, 2 * rows)] for a in range(3)], axis=0
        )

    left_one = has_left.astype(F32)
    right_one = has_right.astype(F32)

    def masked(v, pair, first_real, last_real):
        if pair < first_real:
            return v * left_one
        if pair >= last_real:
            return v * right_one
        return v

    half = HALO - 1
    for sweep in range(SWEEPS):
        for s in range(2):
            if sweep == 0 and s == 1:
                continue
            for c in range(wide):
                at = pl.ds(c * rows, rows)
                v = x_ref[:, at]
                if sweep == 1:
                    base = jnp.zeros((4, rows), F32)
                    for d in range(1, groups):
                        base = base + jnp.where(k >= d, rx_ref[d - 1, :, at], 0.0)
                    if s == 1:
                        base = base + rxs_ref[:, at]
                    state = v[0:4] + base
                    if c < HALO:
                        state = state * left_one
                    if c >= HALO + cols:
                        state = state * right_one
                    v = jnp.concatenate([state, v[4:16]], axis=0)
                store_taps(xs_ref.at[s], v, c * rows, 1)

        for pair in range((wide - 2) // 2):
            lo = pair * 2 * rows
            for s in range(2):
                if s == 0 or sweep == 1:
                    pre = jnp.dot(w1_ref[...], taps_of(xs_ref.at[s], lo), preferred_element_type=F32)
                e = eb_ref[s]
                h = silu(pre + jnp.concatenate([e, e], axis=1))
                h = masked(h, pair, 1, 1 + cols // 2)
                store_taps(fh_ref.at[s], h, lo, 2)

        if sweep == 0:
            for c in copies[0]:
                c.wait()
        for pair in range((cols + 2) // 2):
            lo = pair * 2 * rows
            for s in range(2):
                h = silu(jnp.dot(w2_ref[...], taps_of(fh_ref.at[s], lo), preferred_element_type=F32))
                if pair == 0:
                    h = jnp.concatenate([h[:, :rows] * left_one, h[:, rows:]], axis=1)
                if pair == cols // 2:
                    h = jnp.concatenate([h[:, :rows], h[:, rows:] * right_one], axis=1)
                store_taps(sh_ref.at[s], h, lo, 2)

        if sweep == 0:
            for c in copies[1]:
                c.wait()
        for pair in range(cols // 2):
            lo = pair * 2 * rows
            at = pl.ds(lo, 2 * rows)
            for s in range(2):
                h = silu(jnp.dot(w3_ref[...], taps_of(sh_ref.at[s], lo), preferred_element_type=F32))
                first = fh_ref[s, 128:256, pl.ds(lo + half * rows, 2 * rows)].astype(F32)
                bo_ref[128 * s : 128 * (s + 1), at] = (h + first).astype(BF)
            sums = jnp.dot(wo_ref[...], bo_ref[:, at], preferred_element_type=F32)
            sums = sums * (1.0 / STEPS) + nz_ref[:, at]
            part_ref[:, at] = sums
            part_a[:, at] = sums[0:4]
            part_g[sweep, :, at] = sums[4:8]

        if sweep == 0:
            rxs_ref[:, own] = part_a[...]

            def near_left():
                return remote(
                    part_a.at[:, first_edge], rxs_ref.at[:, right_halo], near_send.at[0], near_recv.at[0], k, t - 1
                )

            def near_right():
                return remote(
                    part_a.at[:, last_edge], rxs_ref.at[:, left_halo], near_send.at[1], near_recv.at[1], k, t + 1
                )

            def full(d):
                return remote(
                    part_g.at[0],
                    rx_ref.at[d - 1, :, own],
                    full_send.at[d - 1],
                    full_recv.at[d - 1],
                    k + d,
                    t,
                )

            def edge_left(d):
                return remote(
                    part_g.at[0, :, first_edge],
                    rx_ref.at[d - 1, :, right_halo],
                    edge_send.at[d - 1, 0],
                    edge_recv.at[d - 1, 0],
                    k + d,
                    t - 1,
                )

            def edge_right(d):
                return remote(
                    part_g.at[0, :, last_edge],
                    rx_ref.at[d - 1, :, left_halo],
                    edge_send.at[d - 1, 1],
                    edge_recv.at[d - 1, 1],
                    k + d,
                    t + 1,
                )

            def each(act_near_l, act_near_r, act_full, act_l, act_r, sending):
                for d in range(groups - 1, 0, -1):
                    reach = (k + d < groups) if sending else (k >= d)
                    pl.when(reach & has_left)(lambda d=d: act_l(d))
                    pl.when(reach & has_right)(lambda d=d: act_r(d))
                    pl.when(reach)(lambda d=d: act_full(d))
                pl.when(has_left)(act_near_l)
                pl.when(has_right)(act_near_r)

            each(
                lambda: near_left().start(),
                lambda: near_right().start(),
                lambda d: full(d).start(),
                lambda d: edge_left(d).start(),
                lambda d: edge_right(d).start(),
                True,
            )
            each(
                lambda: near_right().wait_recv(),
                lambda: near_left().wait_recv(),
                lambda d: full(d).wait_recv(),
                lambda d: edge_right(d).wait_recv(),
                lambda d: edge_left(d).wait_recv(),
                False,
            )
            each(
                lambda: near_left().wait_send(),
                lambda: near_right().wait_send(),
                lambda d: full(d).wait_send(),
                lambda d: edge_left(d).wait_send(),
                lambda d: edge_right(d).wait_send(),
                True,
            )

    def last(d):
        return remote(
            part_g.at[1], rxf_ref.at[d - 1], last_send.at[d - 1], last_recv.at[d - 1], k + d, t
        )

    for d in range(groups - 1, 0, -1):
        pl.when(k + d < groups)(lambda d=d: last(d).start())
    for d in range(1, groups):
        pl.when(k >= d)(lambda d=d: last(d).wait_recv())
    for c in range(cols):
        at = pl.ds(c * rows, rows)
        base = start_ref[:, c, :]
        for d in range(1, groups):
            base = base + jnp.where(k >= d, rxf_ref[d - 1, :, at], 0.0)
        out_ref[0, :, c, :] = base + part_ref[0:4, at]
        out_ref[1, :, c, :] = base + part_ref[4:8, at]
    for d in range(groups - 1, 0, -1):
        pl.when(k + d < groups)(lambda d=d: last(d).wait_send())


def solution(mesh):
    groups, tiles = mesh.shape["step"], mesh.shape["tile"]

    def local(start_state, covariates, noise, embedding, w_in, w_first, w_second, w_out):
        cols = start_state.shape[1]
        wide = cols + 2 * HALO
        cells = cols * 128
        vmem = pl.BlockSpec(memory_space=pltpu.VMEM)
        hbm = pl.BlockSpec(memory_space=pl.ANY)
        dma = pltpu.SemaphoreType.DMA

        def body(*refs):
            kernel(groups, tiles, *refs)

        return pl.pallas_call(
            body,
            out_shape=jax.ShapeDtypeStruct((2, 4, cols, 128), F32),
            in_specs=[vmem, vmem, vmem, vmem, hbm, hbm, hbm, vmem],
            out_specs=vmem,
            scratch_shapes=[
                pltpu.VMEM((16, wide * 128), F32),
                pltpu.VMEM((12, cols, 128), F32),
                pltpu.VMEM((2, 48, wide * 128), BF),
                pltpu.VMEM((9, 128, 16), BF),
                pltpu.VMEM((128, 144), BF),
                pltpu.VMEM((128, 1152), BF),
                pltpu.VMEM((128, 1152), BF),
                pltpu.VMEM((8, 256), BF),
                pltpu.VMEM((2, 128, 128), F32),
                pltpu.VMEM((8, cells), F32),
                pltpu.VMEM((2, 384, (wide - 2) * 128), BF),
                pltpu.VMEM((2, 384, (wide - 4) * 128), BF),
                pltpu.VMEM((256, cells), BF),
                pltpu.VMEM((8, cells), F32),
                pltpu.VMEM((4, cells), F32),
                pltpu.VMEM((2, 4, cells), F32),
                pltpu.VMEM((groups - 1, 4, wide * 128), F32),
                pltpu.VMEM((4, wide * 128), F32),
                pltpu.VMEM((groups - 1, 4, cells), F32),
                dma((19,)),
                dma((2,)),
                dma((2,)),
                dma((groups - 1,)),
                dma((groups - 1,)),
                dma((groups - 1, 2)),
                dma((groups - 1, 2)),
                dma((2,)),
                dma((2,)),
                dma((groups - 1,)),
                dma((groups - 1,)),
            ],
            compiler_params=pltpu.CompilerParams(
                collective_id=0, has_side_effects=True, vmem_limit_bytes=40 << 20
            ),
        )(start_state, covariates, noise, embedding, w_in, w_first, w_second, w_out)

    in_specs = (
        P(None, "tile", None),
        P(None, "tile", None),
        P("step", None, "tile", None),
        P("step", None),
        P(),
        P(),
        P(),
        P(),
    )
    out_specs = P("step", None, "tile", None)
    return jax.shard_map(local, mesh=mesh, in_specs=in_specs, out_specs=out_specs, check_vma=False)
```

```python
import jax
import jax.numpy as jnp
from jax import lax
from jax.experimental import pallas as pl
from jax.experimental.pallas import tpu as pltpu
from jax.sharding import PartitionSpec as P

STEPS = 8
SWEEPS = 2
HALO = 3
ROWS = 128
BF = jnp.bfloat16
F32 = jnp.float32
MESH = pl.DeviceIdType.MESH


def silu_of_half(h):
    return h * jnp.tanh(h) + h


def kernel(
    groups,
    tiles,
    start_hbm,
    cov_hbm,
    noise_hbm,
    embed_hbm,
    win_hbm,
    wfirst_hbm,
    wsecond_hbm,
    wout_hbm,
    out_ref,
    start_ref,
    cov_ref,
    noise_ref,
    embed_ref,
    win_ref,
    wout_ref,
    covf_ref,
    st_ref,
    xb_ref,
    xs_ref,
    w1_ref,
    w2_ref,
    w3_ref,
    wo_ref,
    eb_ref,
    nz_ref,
    fh_ref,
    sh_ref,
    bo_ref,
    part_ref,
    part_a,
    part_g,
    rx_ref,
    rxs_ref,
    rxf_ref,
    in_sem,
    w_sem,
    halo_send,
    halo_recv,
    rim_send,
    rim_recv,
    full_send,
    full_recv,
    edge_send,
    edge_recv,
    near_send,
    near_recv,
    last_send,
    last_recv,
):
    k = lax.axis_index("step")
    t = lax.axis_index("tile")
    cols = start_ref.shape[1]
    wide = cols + 2 * HALO
    edge = HALO * ROWS
    has_left = t > 0
    has_right = t < tiles - 1

    local = [
        pltpu.make_async_copy(src, dst, in_sem.at[n])
        for n, (src, dst) in enumerate(
            (
                (start_hbm, start_ref),
                (cov_hbm, cov_ref),
                (win_hbm, win_ref),
                (embed_hbm, embed_ref),
                (noise_hbm, noise_ref),
                (wout_hbm, wout_ref),
            )
        )
    ]
    get_start, get_cov, get_win, get_embed, get_noise, get_wout = local
    weights = []
    for n, (src, dst) in enumerate(((wfirst_hbm, w2_ref), (wsecond_hbm, w3_ref))):
        weights.append(
            [
                pltpu.make_async_copy(src.at[tap], dst.at[:, pl.ds(tap * 128, 128)], w_sem.at[n, tap])
                for tap in range(9)
            ]
        )

    barrier = pltpu.get_barrier_semaphore()

    def signal(step, tile):
        pl.semaphore_signal(barrier, inc=1, device_id=(step, tile), device_id_type=MESH)

    get_start.start()
    get_cov.start()
    for side, there in ((-1, has_left), (1, has_right)):

        @pl.when(there)
        def _():
            signal(k, t + side)

    for d in range(1, groups):

        @pl.when(k >= d)
        def _():
            signal(k - d, t)

    for d in range(1, groups):
        for side, there in ((-1, has_left), (1, has_right)):

            @pl.when(there & (k >= d))
            def _():
                signal(k - d, t + side)

    for c in (get_win, get_embed, get_noise, get_wout, *weights[0], *weights[1]):
        c.start()

    get_cov.wait()
    covf_ref[...] = cov_ref[...].astype(F32)
    get_start.wait()
    for c in range(cols):
        at = pl.ds((HALO + c) * ROWS, ROWS)
        state = start_ref[:, c, :]
        st_ref[:, at] = state
        xb_ref[:, at] = jnp.concatenate([state, covf_ref[:, c, :]], axis=0).astype(BF)

    sides = has_left.astype(jnp.int32) + has_right.astype(jnp.int32)
    pl.semaphore_wait(barrier, sides + (groups - 1 - k) * (1 + sides))

    def remote(src, dst, send, recv, step, tile):
        return pltpu.make_async_remote_copy(
            src_ref=src,
            dst_ref=dst,
            send_sem=send,
            recv_sem=recv,
            device_id=(step, tile),
            device_id_type=MESH,
        )

    own = pl.ds(HALO * ROWS, cols * ROWS)
    own_first = pl.ds(HALO * ROWS, edge)
    own_last = pl.ds(cols * ROWS, edge)
    left_halo = pl.ds(0, edge)
    right_halo = pl.ds((HALO + cols) * ROWS, edge)
    first_edge = pl.ds(0, edge)
    last_edge = pl.ds((cols - HALO) * ROWS, edge)

    def to_left(ref, send, recv):
        return remote(ref.at[:, own_first], ref.at[:, right_halo], send.at[0], recv.at[0], k, t - 1)

    def to_right(ref, send, recv):
        return remote(ref.at[:, own_last], ref.at[:, left_halo], send.at[1], recv.at[1], k, t + 1)

    halo = (xb_ref, halo_send, halo_recv)
    rim = (st_ref, rim_send, rim_recv)
    pl.when(has_left)(lambda: to_left(*halo).start())
    pl.when(has_right)(lambda: to_right(*halo).start())
    pl.when(has_left)(lambda: to_left(*rim).start())
    pl.when(has_right)(lambda: to_right(*rim).start())

    @pl.when(jnp.logical_not(has_left))
    def _():
        xb_ref[:, left_halo] = jnp.zeros((16, edge), BF)

    @pl.when(jnp.logical_not(has_right))
    def _():
        xb_ref[:, right_halo] = jnp.zeros((16, edge), BF)

    get_win.wait()
    w1_ref[...] = jnp.transpose(win_ref[...].astype(F32) * 0.5).astype(BF)
    get_embed.wait()
    et = 0.5 * jnp.transpose(jnp.concatenate([embed_ref[...], jnp.zeros((6, 128), F32)], axis=0))
    for s in range(2):
        eb_ref[s] = jnp.broadcast_to(et[:, s : s + 1], (128, 128))

    lane = lax.broadcasted_iota(jnp.int32, (1, ROWS), 1)
    keep_first = (lane > 0).astype(F32).astype(BF)
    keep_last = (lane < ROWS - 1).astype(F32).astype(BF)
    left_one = has_left.astype(F32)
    right_one = has_right.astype(F32)
    ones = jnp.ones((1, ROWS), F32)
    outside = jnp.concatenate([ones * left_one, ones * right_one], axis=1)

    def store_taps(ref, v, slot):
        n = v.shape[0]
        at = pl.ds(slot * ROWS, ROWS)
        ref[0:n, at] = pltpu.roll(v, 1, 1) * keep_first
        ref[n : 2 * n, at] = v
        ref[2 * n : 3 * n, at] = pltpu.roll(v, ROWS - 1, 1) * keep_last

    def taps_of(ref, pair):
        return jnp.concatenate(
            [
                jnp.concatenate([ref[:, pl.ds((c + a) * ROWS, ROWS)] for c in pair], axis=1)
                for a in range(3)
            ],
            axis=0,
        )

    def first_pre(s, pair):
        return jnp.dot(
            w1_ref[...], taps_of(xs_ref.at[s], [c + 2 for c in pair]), preferred_element_type=F32
        )

    def first_store(s, pair, pre):
        e = eb_ref[s]
        h = silu_of_half(pre + jnp.concatenate([e, e], axis=1))
        if pair[0] < 0:
            h = h * outside
        h = h.astype(BF)
        for n, c in enumerate(pair):
            store_taps(fh_ref.at[s], h[:, n * ROWS : (n + 1) * ROWS], c + 2)

    def second(s, pair):
        h = jnp.dot(
            w2_ref[...], taps_of(fh_ref.at[s], [c + 1 for c in pair]), preferred_element_type=F32
        )
        h = silu_of_half(h)
        if pair[0] < 0:
            h = h * outside
        h = h.astype(BF)
        for n, c in enumerate(pair):
            store_taps(sh_ref.at[s], h[:, n * ROWS : (n + 1) * ROWS], c + 1)

    def block(s, pair):
        h = jnp.dot(
            w3_ref[...], taps_of(sh_ref.at[s], list(pair)), preferred_element_type=F32
        )
        h = silu_of_half(h)
        for n, c in enumerate(pair):
            first = fh_ref[s, 128:256, pl.ds((c + 2) * ROWS, ROWS)].astype(F32)
            at = pl.ds(c * ROWS, ROWS)
            bo_ref[128 * s : 128 * (s + 1), at] = (h[:, n * ROWS : (n + 1) * ROWS] + first).astype(BF)

    def project(sweep, pair):
        ats = [pl.ds(c * ROWS, ROWS) for c in pair]
        sums = jnp.dot(
            wo_ref[...],
            jnp.concatenate([bo_ref[:, at] for at in ats], axis=1),
            preferred_element_type=F32,
        )
        for n, at in enumerate(ats):
            v = sums[:, n * ROWS : (n + 1) * ROWS] * (1.0 / STEPS) + nz_ref[:, at]
            part_ref[:, at] = v
            if sweep == 0:
                part_a[:, at] = v[0:4]
            part_g[sweep, :, at] = v[4:8]

    mid = cols // 2
    first_in = [(c, c + 1) for c in range(1, cols - 1, 2)]
    first_out = [(c, cols - 1 - c) for c in (-2, -1, 0)]
    second_in = [(c, c + 1) for c in range(2, cols - 2, 2)]
    second_out = [(c, cols - 1 - c) for c in (1, 0, -1)]
    block_in = [(c, c + 1) for c in range(3, cols - 3, 2)]
    block_out = [(c, cols - 1 - c) for c in (2, 1, 0)]

    def inputs_first(c):
        store_taps(xs_ref.at[0], xb_ref[:, pl.ds((c + HALO) * ROWS, ROWS)], c + HALO)

    for c in range(cols):
        inputs_first(c)
    for pair in first_in:
        pre = first_pre(0, pair)
        for s in range(2):
            first_store(s, pair, pre)
    for c in weights[0]:
        c.wait()
    w2_ref[...] = w2_ref[...] * BF(0.5)
    for s in range(2):
        for pair in second_in:
            second(s, pair)
    for c in weights[1]:
        c.wait()
    w3_ref[...] = w3_ref[...] * BF(0.5)
    for s in range(2):
        for pair in block_in:
            block(s, pair)
    get_wout.wait()
    wo = wout_ref[...]
    zero_wo = jnp.zeros_like(wo)
    wo_ref[0:4, 0:128] = wo
    wo_ref[0:4, 128:256] = zero_wo
    wo_ref[4:8, 0:128] = wo
    wo_ref[4:8, 128:256] = wo
    get_noise.wait()
    for c in range(cols):
        at = pl.ds(c * ROWS, ROWS)
        n0 = 0.3 * noise_ref[0, :, c, :]
        nz_ref[0:4, at] = n0
        nz_ref[4:8, at] = n0 + 0.3 * noise_ref[1, :, c, :]
    for pair in block_in:
        project(0, pair)

    pl.when(has_left)(lambda: to_right(*halo).wait_recv())
    pl.when(has_right)(lambda: to_left(*halo).wait_recv())

    for c in (*range(-HALO, 0), *range(cols, cols + HALO)):
        inputs_first(c)
    pres = [first_pre(0, pair) for pair in first_out]
    for s in range(2):
        for pair, pre in zip(first_out, pres):
            first_store(s, pair, pre)
    for s in range(2):
        for pair in second_out:
            second(s, pair)
    for s in range(2):
        for pair in block_out:
            block(s, pair)
    for pair in block_out:
        project(0, pair)

    def near_left():
        return remote(
            part_a.at[:, first_edge], rxs_ref.at[:, right_halo], near_send.at[0], near_recv.at[0], k, t - 1
        )

    def near_right():
        return remote(
            part_a.at[:, last_edge], rxs_ref.at[:, left_halo], near_send.at[1], near_recv.at[1], k, t + 1
        )

    def full(d):
        return remote(
            part_g.at[0], rx_ref.at[d - 1, :, own], full_send.at[d - 1], full_recv.at[d - 1], k + d, t
        )

    def edge_left(d):
        return remote(
            part_g.at[0, :, first_edge],
            rx_ref.at[d - 1, :, right_halo],
            edge_send.at[d - 1, 0],
            edge_recv.at[d - 1, 0],
            k + d,
            t - 1,
        )

    def edge_right(d):
        return remote(
            part_g.at[0, :, last_edge],
            rx_ref.at[d - 1, :, left_halo],
            edge_send.at[d - 1, 1],
            edge_recv.at[d - 1, 1],
            k + d,
            t + 1,
        )

    for d in range(groups - 1, 0, -1):
        pl.when((k + d < groups) & has_left)(lambda d=d: edge_left(d).start())
        pl.when((k + d < groups) & has_right)(lambda d=d: edge_right(d).start())
    for d in range(groups - 1, 0, -1):
        pl.when(k + d < groups)(lambda d=d: full(d).start())
    pl.when(has_left)(lambda: near_left().start())
    pl.when(has_right)(lambda: near_right().start())
    rxs_ref[:, own] = part_a[...]

    pl.when(has_left)(lambda: to_right(*rim).wait_recv())
    pl.when(has_right)(lambda: to_left(*rim).wait_recv())
    pl.when(has_left)(lambda: near_right().wait_recv())
    pl.when(has_right)(lambda: near_left().wait_recv())
    for d in range(1, groups):
        pl.when(k >= d)(lambda d=d: full(d).wait_recv())
        pl.when((k >= d) & has_left)(lambda d=d: edge_right(d).wait_recv())
        pl.when((k >= d) & has_right)(lambda d=d: edge_left(d).wait_recv())

    for c in range(-HALO, cols + HALO):
        at = pl.ds((c + HALO) * ROWS, ROWS)
        base = st_ref[:, at]
        for d in range(1, groups):
            base = base + jnp.where(k >= d, rx_ref[d - 1, :, at], 0.0)
        cov = xb_ref[:, at].astype(F32)[4:16]
        for s in range(2):
            state = base + rxs_ref[:, at] if s == 1 else base
            if c < 0:
                state = jnp.where(has_left, state, 0.0)
            if c >= cols:
                state = jnp.where(has_right, state, 0.0)
            v = jnp.concatenate([state, cov], axis=0).astype(BF)
            store_taps(xs_ref.at[s], v, c + HALO)
    for s in range(2):
        for pair in first_out + first_in:
            first_store(s, pair, first_pre(s, pair))
    for s in range(2):
        for pair in second_out + second_in:
            second(s, pair)
    for s in range(2):
        for pair in block_out + block_in:
            block(s, pair)
    for pair in block_out + block_in:
        project(1, pair)

    def last(d):
        return remote(
            part_g.at[1], rxf_ref.at[d - 1], last_send.at[d - 1], last_recv.at[d - 1], k + d, t
        )

    for d in range(groups - 1, 0, -1):
        pl.when(k + d < groups)(lambda d=d: last(d).start())

    pl.when(has_left)(lambda: to_left(*halo).wait_send())
    pl.when(has_right)(lambda: to_right(*halo).wait_send())
    pl.when(has_left)(lambda: to_left(*rim).wait_send())
    pl.when(has_right)(lambda: to_right(*rim).wait_send())
    pl.when(has_left)(lambda: near_left().wait_send())
    pl.when(has_right)(lambda: near_right().wait_send())
    for d in range(1, groups):
        pl.when(k + d < groups)(lambda d=d: full(d).wait_send())
        pl.when((k + d < groups) & has_left)(lambda d=d: edge_left(d).wait_send())
        pl.when((k + d < groups) & has_right)(lambda d=d: edge_right(d).wait_send())

    for d in range(1, groups):
        pl.when(k >= d)(lambda d=d: last(d).wait_recv())
    for c in range(cols):
        at = pl.ds(c * ROWS, ROWS)
        base = start_ref[:, c, :]
        for d in range(1, groups):
            base = base + jnp.where(k >= d, rxf_ref[d - 1, :, at], 0.0)
        out_ref[0, :, c, :] = base + part_ref[0:4, at]
        out_ref[1, :, c, :] = base + part_ref[4:8, at]
    for d in range(1, groups):
        pl.when(k + d < groups)(lambda d=d: last(d).wait_send())


def solution(mesh):
    groups, tiles = mesh.shape["step"], mesh.shape["tile"]

    def local(start_state, covariates, noise, embedding, w_in, w_first, w_second, w_out):
        cols = start_state.shape[1]
        wide = cols + 2 * HALO
        cells = cols * ROWS
        vmem = pl.BlockSpec(memory_space=pltpu.VMEM)
        hbm = pl.BlockSpec(memory_space=pltpu.HBM)
        dma = pltpu.SemaphoreType.DMA
        w_in = jnp.swapaxes(w_in, 1, 2).reshape(144, 128)

        def body(*refs):
            kernel(groups, tiles, *refs)

        args = [
            pltpu.with_memory_space_constraint(v, pltpu.HBM)
            for v in (start_state, covariates, noise, embedding, w_in, w_first, w_second, w_out)
        ]

        return pl.pallas_call(
            body,
            out_shape=pltpu.VMEM((2, 4, cols, ROWS), F32),
            in_specs=[hbm] * 8,
            out_specs=vmem,
            scratch_shapes=[
                pltpu.VMEM((4, cols, ROWS), F32),
                pltpu.VMEM((12, cols, ROWS), BF),
                pltpu.VMEM((2, 4, cols, ROWS), F32),
                pltpu.VMEM((2, 128), F32),
                pltpu.VMEM((144, 128), BF),
                pltpu.VMEM((4, 128), BF),
                pltpu.VMEM((12, cols, ROWS), F32),
                pltpu.VMEM((4, wide * ROWS), F32),
                pltpu.VMEM((16, wide * ROWS), BF),
                pltpu.VMEM((2, 48, wide * ROWS), BF),
                pltpu.VMEM((128, 144), BF),
                pltpu.VMEM((128, 1152), BF),
                pltpu.VMEM((128, 1152), BF),
                pltpu.VMEM((8, 256), BF),
                pltpu.VMEM((2, 128, ROWS), F32),
                pltpu.VMEM((8, cells), F32),
                pltpu.VMEM((2, 384, (wide - 2) * ROWS), BF),
                pltpu.VMEM((2, 384, (wide - 4) * ROWS), BF),
                pltpu.VMEM((256, cells), BF),
                pltpu.VMEM((8, cells), F32),
                pltpu.VMEM((4, cells), F32),
                pltpu.VMEM((2, 4, cells), F32),
                pltpu.VMEM((groups - 1, 4, wide * ROWS), F32),
                pltpu.VMEM((4, wide * ROWS), F32),
                pltpu.VMEM((groups - 1, 4, cells), F32),
                dma((6,)),
                dma((2, 9)),
                dma((2,)),
                dma((2,)),
                dma((2,)),
                dma((2,)),
                dma((groups - 1,)),
                dma((groups - 1,)),
                dma((groups - 1, 2)),
                dma((groups - 1, 2)),
                dma((2,)),
                dma((2,)),
                dma((groups - 1,)),
                dma((groups - 1,)),
            ],
            compiler_params=pltpu.CompilerParams(
                collective_id=0, has_side_effects=True, vmem_limit_bytes=40 << 20
            ),
        )(*args)

    in_specs = (
        P(None, "tile", None),
        P(None, "tile", None),
        P("step", None, "tile", None),
        P("step", None),
        P(),
        P(),
        P(),
        P(),
    )
    out_specs = P("step", None, "tile", None)
    return jax.shard_map(local, mesh=mesh, in_specs=in_specs, out_specs=out_specs, check_vma=False)
```

```python
import jax
import jax.numpy as jnp
from jax import lax
from jax.experimental import pallas as pl
from jax.experimental.pallas import tpu as pltpu
from jax.sharding import PartitionSpec as P

STEPS = 8
SWEEPS = 2
HALO = 3
ROWS = 128
BF = jnp.bfloat16
F32 = jnp.float32
MESH = pl.DeviceIdType.MESH


def silu_of_half(h):
    return h * jnp.tanh(h) + h


def kernel(
    groups,
    tiles,
    start_hbm,
    cov_hbm,
    noise_hbm,
    embed_hbm,
    win_hbm,
    wfirst_hbm,
    wsecond_hbm,
    wout_hbm,
    out_ref,
    start_ref,
    cov_ref,
    noise_ref,
    embed_ref,
    win_ref,
    wout_ref,
    covf_ref,
    st_ref,
    xb_ref,
    xs_ref,
    w1_ref,
    w2_ref,
    w3_ref,
    wo_ref,
    eb_ref,
    nz_ref,
    fh_ref,
    sh_ref,
    part_ref,
    part_a,
    part_g,
    rx_ref,
    rxs_ref,
    rxf_ref,
    in_sem,
    w_sem,
    halo_send,
    halo_recv,
    rim_send,
    rim_recv,
    near_send,
    near_recv,
    mid_send,
    mid_recv,
    last_send,
    last_recv,
    chain,
):
    k = lax.axis_index("step")
    t = lax.axis_index("tile")
    cols = start_ref.shape[1]
    wide = cols + 2 * HALO

    even = t % 2 == 0
    fast = jnp.where(even, t + 1, t - 1)
    slow = jnp.where(even, t - 1, t + 1)
    has_slow = (slow >= 0) & (slow < tiles)
    slow_one = has_slow.astype(F32)

    def col(i):
        return jnp.where(even, cols - 1 - i, i)

    def lanes(at, width, unit=ROWS):
        return pl.ds(pl.multiple_of(at * unit, ROWS), width * unit)

    local = [
        pltpu.make_async_copy(src, dst, in_sem.at[n])
        for n, (src, dst) in enumerate(
            (
                (start_hbm, start_ref),
                (cov_hbm, cov_ref),
                (win_hbm, win_ref),
                (embed_hbm, embed_ref),
                (noise_hbm, noise_ref),
                (wout_hbm, wout_ref),
            )
        )
    ]
    get_start, get_cov, get_win, get_embed, get_noise, get_wout = local
    weights = []
    for n, (src, dst) in enumerate(((wfirst_hbm, w2_ref), (wsecond_hbm, w3_ref))):
        weights.append(
            [
                pltpu.make_async_copy(src.at[tap], dst.at[:, pl.ds(tap * 128, 128)], w_sem.at[n, tap])
                for tap in range(9)
            ]
        )
    get_start.start()
    get_cov.start()

    st_ref[...] = jnp.zeros_like(st_ref)
    xb_ref[...] = jnp.zeros_like(xb_ref)
    rx_ref[...] = jnp.zeros_like(rx_ref)
    rxs_ref[...] = jnp.zeros_like(rxs_ref)
    rxf_ref[...] = jnp.zeros_like(rxf_ref)

    barrier = pltpu.get_barrier_semaphore()

    def signal(sem, step, tile):
        pl.semaphore_signal(sem, inc=1, device_id=(step, tile), device_id_type=MESH)

    pl.when(has_slow)(lambda: signal(barrier, k, slow))
    pl.when(k > 0)(lambda: signal(barrier, k - 1, t))
    pl.when(k < groups - 1)(lambda: signal(barrier, k + 1, t))
    signal(barrier, k, fast)

    for c in (get_win, get_embed, *weights[0], *weights[1], get_noise, get_wout):
        c.start()

    get_cov.wait()
    covf_ref[...] = cov_ref[...].astype(F32)
    get_start.wait()
    for c in range(cols):
        at = pl.ds((HALO + c) * ROWS, ROWS)
        state = start_ref[:, c, :]
        st_ref[:, at] = state
        xb_ref[:, at] = jnp.concatenate([state, covf_ref[:, c, :]], axis=0).astype(BF)

    def one(p):
        return p.astype(jnp.int32)

    pl.semaphore_wait(barrier, 1 + one(has_slow) + one(k > 0) + one(k < groups - 1))

    def remote(src, dst, send, recv, step, tile):
        return pltpu.make_async_remote_copy(
            src_ref=src,
            dst_ref=dst,
            send_sem=send,
            recv_sem=recv,
            device_id=(step, tile),
            device_id_type=MESH,
        )

    to_fast = lanes(jnp.where(even, cols - HALO, 0), HALO)
    to_slow = lanes(jnp.where(even, 0, cols - HALO), HALO)
    own_to_fast = lanes(jnp.where(even, cols, HALO), HALO)
    own_to_slow = lanes(jnp.where(even, HALO, cols), HALO)
    at_fast = lanes(jnp.where(even, 0, HALO + cols), HALO)
    at_slow = lanes(jnp.where(even, HALO + cols, 0), HALO)
    early = lanes(jnp.where(even, HALO, 0), cols - HALO)
    own_early = lanes(jnp.where(even, 2 * HALO, HALO), cols - HALO)

    def to_sides(ref, send, recv):
        f = remote(ref.at[:, own_to_fast], ref.at[:, at_fast], send.at[0], recv.at[0], k, fast)
        s = remote(ref.at[:, own_to_slow], ref.at[:, at_slow], send.at[1], recv.at[1], k, slow)
        return f, s

    halo_fast, halo_slow = to_sides(xb_ref, halo_send, halo_recv)
    rim_fast, rim_slow = to_sides(st_ref, rim_send, rim_recv)
    pl.when(has_slow)(halo_slow.start)
    halo_fast.start()
    pl.when(has_slow)(rim_slow.start)
    rim_fast.start()

    def pass_on(n):
        if n < groups - 1:
            pl.when((k > 0) & (k < groups - n))(lambda: signal(chain.at[n], k - 1, t))

    def hear(n):
        pl.when(k < groups - 1 - n)(lambda: pl.semaphore_wait(chain.at[n], 1))

    pass_on(0)

    get_win.wait()
    w1_ref[...] = jnp.transpose(win_ref[...].astype(F32) * 0.5).astype(BF)
    get_embed.wait()
    et = 0.5 * jnp.transpose(jnp.concatenate([embed_ref[...], jnp.zeros((6, 128), F32)], axis=0))
    for s in range(2):
        eb_ref[:, pl.ds(s * ROWS, ROWS)] = jnp.broadcast_to(et[:, s : s + 1], (128, ROWS))

    lane = lax.broadcasted_iota(jnp.int32, (1, ROWS), 1)
    keep_first = (lane > 0).astype(F32).astype(BF)
    keep_last = (lane < ROWS - 1).astype(F32).astype(BF)

    def store_taps(ref, v, slot):
        n = v.shape[0]
        for s in range(2):
            at = pl.ds(pl.multiple_of((2 * slot + s) * ROWS, ROWS), ROWS)
            x = v[:, s * ROWS : (s + 1) * ROWS]
            ref[0:n, at] = pltpu.roll(x, 1, 1) * keep_first
            ref[n : 2 * n, at] = x
            ref[2 * n : 3 * n, at] = pltpu.roll(x, ROWS - 1, 1) * keep_last

    def taps_of(ref, slot):
        return jnp.concatenate([ref[:, lanes(slot + a, 1, 2 * ROWS)] for a in range(3)], axis=0)

    def first(c, may_be_outside):
        pre = jnp.dot(w1_ref[...], taps_of(xs_ref, c + 2), preferred_element_type=F32)
        h = silu_of_half(pre + eb_ref[...])
        if may_be_outside:
            h = h * slow_one
        store_taps(fh_ref, h.astype(BF), c + 2)

    def second(c, may_be_outside):
        h = jnp.dot(w2_ref[...], taps_of(fh_ref, c + 1), preferred_element_type=F32)
        h = silu_of_half(h)
        if may_be_outside:
            h = h * slow_one
        store_taps(sh_ref, h.astype(BF), c + 1)

    def block(c):
        h = silu_of_half(jnp.dot(w3_ref[...], taps_of(sh_ref, c), preferred_element_type=F32))
        h = (h + fh_ref[128:256, lanes(c + 2, 1, 2 * ROWS)].astype(F32)).astype(BF)
        return jnp.concatenate([h[:, :ROWS], h[:, ROWS:]], axis=0)

    def project(sweep, cs, blocks):
        sums = jnp.dot(wo_ref[...], jnp.concatenate(blocks, axis=1), preferred_element_type=F32)
        for n, c in enumerate(cs):
            at = lanes(c, 1)
            v = sums[:, n * ROWS : (n + 1) * ROWS] + nz_ref[:, at]
            if sweep == 0:
                part_a[:, at] = v[0:4]
            else:
                part_ref[:, at] = v
            part_g[sweep, :, at] = v[4:8]

    def inputs_first(c):
        x = xb_ref[:, lanes(c + HALO, 1)]
        store_taps(xs_ref, jnp.concatenate([x, x], axis=1), c + HALO)

    def inputs_next(c):
        at = lanes(c + HALO, 1)
        base = st_ref[:, at]
        for d in range(groups - 1):
            base = base + rx_ref[d, :, at]
        cov = xb_ref[:, at].astype(F32)[4:16]
        v = jnp.concatenate(
            [
                jnp.concatenate([base, base + rxs_ref[:, at]], axis=1),
                jnp.concatenate([cov, cov], axis=1),
            ],
            axis=0,
        )
        store_taps(xs_ref, v.astype(BF), c + HALO)

    inner_x = range(cols)
    inner_1, inner_2, inner_3 = range(1, cols - 1), range(2, cols - 2), range(3, cols - 3)
    fast_x, fast_1, fast_2, fast_3 = (-1, -2, -3), (0, -1, -2), (1, 0, -1), (2, 1, 0)

    def other(group):
        return [cols - 1 - i for i in group]

    slow_x, slow_1, slow_2, slow_3 = other(fast_x), other(fast_1), other(fast_2), other(fast_3)

    def stages(sweep, group_1, group_2, group_3, between=lambda n: None):
        for i in group_1:
            first(col(i), i >= cols)
        between(0)
        for i in group_2:
            second(col(i), i >= cols)
        between(1)
        cs = [col(i) for i in group_3]
        blocks = [block(c) for c in cs]
        between(2)
        project(sweep, cs, blocks)

    for i in inner_x:
        inputs_first(col(i))

    def ready(n):
        if n < 2:
            for c in weights[n]:
                c.wait()
            ref = (w2_ref, w3_ref)[n]
            ref[...] = ref[...] * BF(0.5)
            hear(n)
            pass_on(n + 1)
        else:
            get_wout.wait()
            wo = wout_ref[...] * BF(1.0 / STEPS)
            zero_wo = jnp.zeros_like(wo)
            wo_ref[0:4, 0:128] = wo
            wo_ref[0:4, 128:256] = zero_wo
            wo_ref[4:8, 0:128] = wo
            wo_ref[4:8, 128:256] = wo
            get_noise.wait()
            for c in range(cols):
                at = pl.ds(c * ROWS, ROWS)
                n0 = 0.3 * noise_ref[0, :, c, :]
                nz_ref[0:4, at] = n0
                nz_ref[4:8, at] = n0 + 0.3 * noise_ref[1, :, c, :]

    stages(0, inner_1, inner_2, inner_3, ready)

    halo_fast.wait_recv()
    for i in fast_x:
        inputs_first(col(i))
    stages(0, fast_1, fast_2, fast_3)
    for n in range(2, groups - 1):
        hear(n)
        pass_on(n + 1)

    def mids(d):
        g = part_g.at[0]
        r = rx_ref.at[d - 1]

        def send(n, src, dst, tile):
            return remote(
                g.at[:, src], r.at[:, dst], mid_send.at[d - 1, n], mid_recv.at[d - 1, n], k + d, tile
            )

        return (
            send(0, early, own_early, t),
            send(1, to_fast, at_fast, fast),
            send(2, to_slow, own_to_slow, t),
            send(3, to_slow, at_slow, slow),
        )

    mid = {d: mids(d) for d in range(1, groups)}
    near_fast = remote(
        part_a.at[:, to_fast], rxs_ref.at[:, at_fast], near_send.at[0], near_recv.at[0], k, fast
    )
    near_slow = remote(
        part_a.at[:, to_slow], rxs_ref.at[:, at_slow], near_send.at[1], near_recv.at[1], k, slow
    )
    far = range(groups - 1, 0, -1)

    for d in far:

        @pl.when(k + d < groups)
        def _():
            mid[d][1].start()
            mid[d][0].start()

    near_fast.start()

    pl.when(has_slow)(halo_slow.wait_recv)
    for i in slow_x:
        inputs_first(col(i))
    stages(0, slow_1, slow_2, slow_3)

    for d in far:
        pl.when((k + d < groups) & has_slow)(mid[d][3].start)
    for d in far:
        pl.when(k + d < groups)(mid[d][2].start)
    pl.when(has_slow)(near_slow.start)
    rxs_ref[:, pl.ds(HALO * ROWS, cols * ROWS)] = part_a[...]

    rim_fast.wait_recv()
    near_fast.wait_recv()
    for d in range(1, groups):

        @pl.when(k >= d)
        def _():
            mid[d][0].wait_recv()
            mid[d][1].wait_recv()
            mid[d][2].wait_recv()

    for i in (*inner_x, *fast_x):
        inputs_next(col(i))
    stages(1, (*inner_1, *fast_1), (*inner_2, *fast_2), (*inner_3, *fast_3))

    def lasts(d):
        def send(n, at):
            return remote(
                part_g.at[1, :, at],
                rxf_ref.at[d - 1, :, at],
                last_send.at[d - 1, n],
                last_recv.at[d - 1, n],
                k + d,
                t,
            )

        return send(0, early), send(1, to_slow)

    last = {d: lasts(d) for d in range(1, groups)}
    for d in far:
        pl.when(k + d < groups)(last[d][0].start)

    @pl.when(has_slow)
    def _():
        rim_slow.wait_recv()
        near_slow.wait_recv()

    for d in range(1, groups):
        pl.when((k >= d) & has_slow)(mid[d][3].wait_recv)
    for i in slow_x:
        inputs_next(col(i))
    stages(1, slow_1, slow_2, slow_3)
    for d in far:
        pl.when(k + d < groups)(last[d][1].start)

    halo_fast.wait_send()
    rim_fast.wait_send()
    near_fast.wait_send()

    @pl.when(has_slow)
    def _():
        halo_slow.wait_send()
        rim_slow.wait_send()
        near_slow.wait_send()

    for d in range(1, groups):

        @pl.when(k + d < groups)
        def _():
            mid[d][0].wait_send()
            mid[d][1].wait_send()
            mid[d][2].wait_send()

        pl.when((k + d < groups) & has_slow)(mid[d][3].wait_send)

    for d in range(1, groups):

        @pl.when(k >= d)
        def _():
            last[d][0].wait_recv()
            last[d][1].wait_recv()

    for c in range(cols):
        at = pl.ds(c * ROWS, ROWS)
        base = start_ref[:, c, :]
        for d in range(groups - 1):
            base = base + rxf_ref[d, :, at]
        out_ref[0, :, c, :] = base + part_ref[0:4, at]
        out_ref[1, :, c, :] = base + part_ref[4:8, at]
    for d in range(1, groups):

        @pl.when(k + d < groups)
        def _():
            last[d][0].wait_send()
            last[d][1].wait_send()


def solution(mesh):
    groups, tiles = mesh.shape["step"], mesh.shape["tile"]

    def local(start_state, covariates, noise, embedding, w_in, w_first, w_second, w_out):
        cols = start_state.shape[1]
        wide = cols + 2 * HALO
        cells = cols * ROWS
        hbm = pl.BlockSpec(memory_space=pltpu.HBM)
        dma = pltpu.SemaphoreType.DMA
        w_in = jnp.swapaxes(w_in, 1, 2).reshape(144, 128)

        def body(*refs):
            kernel(groups, tiles, *refs)

        args = [
            pltpu.with_memory_space_constraint(v, pltpu.HBM)
            for v in (start_state, covariates, noise, embedding, w_in, w_first, w_second, w_out)
        ]
        return pl.pallas_call(
            body,
            out_shape=pltpu.VMEM((2, 4, cols, ROWS), F32),
            in_specs=[hbm] * 8,
            out_specs=pl.BlockSpec(memory_space=pltpu.VMEM),
            scratch_shapes=[
                pltpu.VMEM((4, cols, ROWS), F32),
                pltpu.VMEM((12, cols, ROWS), BF),
                pltpu.VMEM((2, 4, cols, ROWS), F32),
                pltpu.VMEM((2, 128), F32),
                pltpu.VMEM((144, 128), BF),
                pltpu.VMEM((4, 128), BF),
                pltpu.VMEM((12, cols, ROWS), F32),
                pltpu.VMEM((4, wide * ROWS), F32),
                pltpu.VMEM((16, wide * ROWS), BF),
                pltpu.VMEM((48, wide * 2 * ROWS), BF),
                pltpu.VMEM((128, 144), BF),
                pltpu.VMEM((128, 1152), BF),
                pltpu.VMEM((128, 1152), BF),
                pltpu.VMEM((8, 256), BF),
                pltpu.VMEM((128, 2 * ROWS), F32),
                pltpu.VMEM((8, cells), F32),
                pltpu.VMEM((384, (wide - 2) * 2 * ROWS), BF),
                pltpu.VMEM((384, (wide - 4) * 2 * ROWS), BF),
                pltpu.VMEM((8, cells), F32),
                pltpu.VMEM((4, cells), F32),
                pltpu.VMEM((2, 4, cells), F32),
                pltpu.VMEM((groups - 1, 4, wide * ROWS), F32),
                pltpu.VMEM((4, wide * ROWS), F32),
                pltpu.VMEM((groups - 1, 4, cells), F32),
                dma((6,)),
                dma((2, 9)),
                dma((2,)),
                dma((2,)),
                dma((2,)),
                dma((2,)),
                dma((2,)),
                dma((2,)),
                dma((groups - 1, 4)),
                dma((groups - 1, 4)),
                dma((groups - 1, 2)),
                dma((groups - 1, 2)),
                pltpu.SemaphoreType.REGULAR((groups - 1,)),
            ],
            compiler_params=pltpu.CompilerParams(
                collective_id=0, has_side_effects=True, vmem_limit_bytes=40 << 20
            ),
        )(*args)

    in_specs = (
        P(None, "tile", None),
        P(None, "tile", None),
        P("step", None, "tile", None),
        P("step", None),
        P(),
        P(),
        P(),
        P(),
    )
    out_specs = P("step", None, "tile", None)
    return jax.shard_map(local, mesh=mesh, in_specs=in_specs, out_specs=out_specs, check_vma=False)
```

```python
import jax
import jax.numpy as jnp
from jax import lax
from jax.experimental import pallas as pl
from jax.experimental.pallas import tpu as pltpu
from jax.sharding import PartitionSpec as P

STEPS = 8
SWEEPS = 2
CH = 4
HALO = 3
ROWS = 128
BF = jnp.bfloat16
F32 = jnp.float32
MESH = pl.DeviceIdType.MESH


def silu_of_half(h):
    return h * jnp.tanh(h) + h


def kernel(
    groups,
    tiles,
    start_hbm,
    cov_hbm,
    noise_hbm,
    embed_hbm,
    win_hbm,
    wfirst_hbm,
    wsecond_hbm,
    wout_hbm,
    out_ref,
    start_ref,
    cov_ref,
    noise_ref,
    embed_ref,
    win_ref,
    wout_ref,
    covf_ref,
    st_ref,
    base_ref,
    xb_ref,
    x1_ref,
    x2_ref,
    w1_ref,
    w2_ref,
    w3_ref,
    wo_ref,
    eb_ref,
    nz_ref,
    fh_ref,
    sh_ref,
    bo_ref,
    pa_ref,
    pg_ref,
    pd_ref,
    rx_ref,
    rxs_ref,
    rxf_ref,
    in_sem,
    w_sem,
    halo_send,
    halo_recv,
    rim_send,
    rim_recv,
    near_send,
    near_recv,
    mid_send,
    mid_recv,
    last_send,
    last_recv,
    chain,
):
    k = lax.axis_index("step")
    t = lax.axis_index("tile")
    cols = start_ref.shape[1]
    half = cols // 2
    rim = CH * half
    has_left = t > 0
    has_right = t < tiles - 1

    local = [
        pltpu.make_async_copy(src, dst, in_sem.at[n])
        for n, (src, dst) in enumerate(
            (
                (start_hbm, start_ref),
                (cov_hbm, cov_ref),
                (win_hbm, win_ref),
                (embed_hbm, embed_ref),
                (noise_hbm, noise_ref),
                (wout_hbm, wout_ref),
            )
        )
    ]
    get_start, get_cov, get_win, get_embed, get_noise, get_wout = local
    weights = []
    for n, (src, dst) in enumerate(((wfirst_hbm, w2_ref), (wsecond_hbm, w3_ref))):
        weights.append(
            [
                pltpu.make_async_copy(src.at[tap], dst.at[:, pl.ds(tap * 128, 128)], w_sem.at[n, tap])
                for tap in range(9)
            ]
        )
    get_start.start()
    get_cov.start()

    for ref in (st_ref, xb_ref, rx_ref, rxs_ref, rxf_ref):
        ref[...] = jnp.zeros_like(ref)

    barrier = pltpu.get_barrier_semaphore()

    def signal(sem, step, tile):
        pl.semaphore_signal(sem, inc=1, device_id=(step, tile), device_id_type=MESH)

    pl.when(has_left)(lambda: signal(barrier, k, t - 1))
    pl.when(has_right)(lambda: signal(barrier, k, t + 1))
    pl.when(k > 0)(lambda: signal(barrier, k - 1, t))
    pl.when(k < groups - 1)(lambda: signal(barrier, k + 1, t))

    for c in (get_win, get_embed, *weights[0], *weights[1], get_noise, get_wout):
        c.start()

    def slot(c):
        return pl.ds((c + HALO) * ROWS, ROWS)

    get_cov.wait()
    covf_ref[...] = cov_ref[...].astype(F32)
    get_start.wait()
    for c in range(cols):
        xb_ref[:, slot(c)] = jnp.concatenate([start_ref[:, c, :], covf_ref[:, c, :]], axis=0).astype(BF)

    def one(p):
        return p.astype(jnp.int32)

    pl.semaphore_wait(barrier, one(has_left) + one(has_right) + one(k > 0) + one(k < groups - 1))

    def remote(src, dst, send, recv, step, tile):
        return pltpu.make_async_remote_copy(
            src_ref=src,
            dst_ref=dst,
            send_sem=send,
            recv_sem=recv,
            device_id=(step, tile),
            device_id_type=MESH,
        )

    def strip(c):
        return pl.ds((c + HALO) * ROWS, HALO * ROWS)

    halo_left = remote(
        xb_ref.at[:, strip(0)], xb_ref.at[:, strip(cols)], halo_send.at[0], halo_recv.at[0], k, t - 1
    )
    halo_right = remote(
        xb_ref.at[:, strip(cols - HALO)], xb_ref.at[:, strip(-HALO)], halo_send.at[1], halo_recv.at[1], k, t + 1
    )
    pl.when(has_left)(halo_left.start)
    pl.when(has_right)(halo_right.start)

    at_left, own_left, own_right, at_right = [pl.ds(n * rim, rim) for n in range(4)]
    first_half, second_half = pl.ds(0, rim), pl.ds(rim, rim)
    own = pl.ds(rim, 2 * rim)

    for ch in range(CH):
        st_ref[pl.ds(rim + ch, cols, stride=CH), :] = start_ref[ch]
    rim_left = remote(st_ref.at[own_left], st_ref.at[at_right], rim_send.at[0], rim_recv.at[0], k, t - 1)
    rim_right = remote(st_ref.at[own_right], st_ref.at[at_left], rim_send.at[1], rim_recv.at[1], k, t + 1)
    pl.when(has_left)(rim_left.start)
    pl.when(has_right)(rim_right.start)

    def pass_on(n):
        if n < groups - 1:
            pl.when((k > 0) & (k < groups - n))(lambda: signal(chain.at[n], k - 1, t))

    def hear(n):
        pl.when(k < groups - 1 - n)(lambda: pl.semaphore_wait(chain.at[n], 1))

    pass_on(0)

    get_win.wait()
    w1_ref[...] = jnp.transpose(win_ref[...].astype(F32) * 0.5).astype(BF)
    get_embed.wait()
    et = 0.5 * jnp.transpose(jnp.concatenate([embed_ref[...], jnp.zeros((6, 128), F32)], axis=0))
    for s in range(2):
        eb_ref[:, pl.ds(s * ROWS, ROWS)] = jnp.broadcast_to(et[:, s : s + 1], (128, ROWS))

    lane = lax.broadcasted_iota(jnp.int32, (1, ROWS), 1)
    keep_first = (lane > 0).astype(F32).astype(BF)
    keep_last = (lane < ROWS - 1).astype(F32).astype(BF)
    left_one = has_left.astype(F32)
    right_one = has_right.astype(F32)

    def store_taps(ref, x, at):
        n = x.shape[0]
        at = pl.ds(at * ROWS, ROWS)
        ref[0:n, at] = pltpu.roll(x, 1, 1) * keep_first
        ref[n : 2 * n, at] = x
        ref[2 * n : 3 * n, at] = pltpu.roll(x, ROWS - 1, 1) * keep_last

    def store_both(ref, h, at):
        for s in range(2):
            store_taps(ref, h[:, s * ROWS : (s + 1) * ROWS], 2 * at + s)

    def taps_of(ref, at):
        return jnp.concatenate(
            [ref[:, pl.ds((at + a) * 2 * ROWS, 2 * ROWS)] for a in range(3)], axis=0
        )

    def inside(h, c):
        if c < 0:
            return h * left_one
        if c >= cols:
            return h * right_one
        return h

    def first_done(pre, c):
        h = inside(silu_of_half(pre + eb_ref[...]), c)
        store_both(fh_ref, h.astype(BF), c + 2)

    def first(c):
        first_done(jnp.dot(w1_ref[...], taps_of(x2_ref, c + 2), preferred_element_type=F32), c)

    def first_pair(pair):
        taps = jnp.concatenate(
            [
                jnp.concatenate([x1_ref[:, pl.ds((c + 2 + a) * ROWS, ROWS)] for c in pair], axis=1)
                for a in range(3)
            ],
            axis=0,
        )
        pre = jnp.dot(w1_ref[...], taps, preferred_element_type=F32)
        for n, c in enumerate(pair):
            p = pre[:, n * ROWS : (n + 1) * ROWS]
            first_done(jnp.concatenate([p, p], axis=1), c)

    def second(c):
        h = jnp.dot(w2_ref[...], taps_of(fh_ref, c + 1), preferred_element_type=F32)
        store_both(sh_ref, inside(silu_of_half(h), c).astype(BF), c + 1)

    def block(c):
        h = silu_of_half(jnp.dot(w3_ref[...], taps_of(sh_ref, c), preferred_element_type=F32))
        h = (h + fh_ref[128:256, pl.ds((c + 2) * 2 * ROWS, 2 * ROWS)].astype(F32)).astype(BF)
        for s in range(2):
            at = (s * half + c % half) * 128
            bo_ref[at : at + 128, pl.ds((c // half) * ROWS, ROWS)] = h[:, s * ROWS : (s + 1) * ROWS]

    def project():
        p = jnp.dot(wo_ref[...], bo_ref[...], preferred_element_type=F32)
        p = jnp.concatenate([p[:, :ROWS], p[:, ROWS:]], axis=0)
        a = jnp.concatenate([p[0:rim], p[2 * rim : 3 * rim]], axis=0) + nz_ref[0]
        g = jnp.concatenate([p[rim : 2 * rim], p[3 * rim : 4 * rim]], axis=0) + nz_ref[1]
        return a, g

    def inputs_first(c):
        store_taps(x1_ref, xb_ref[:, slot(c)], c + HALO)

    for c in range(cols):
        inputs_first(c)
    for c in range(1, cols - 1, 2):
        first_pair((c, c + 1))
    hear(0)
    pass_on(1)
    for c in weights[0]:
        c.wait()
    w2_ref[...] = w2_ref[...] * BF(0.5)
    for c in range(2, cols - 2):
        second(c)
    hear(1)
    pass_on(2)
    for c in weights[1]:
        c.wait()
    w3_ref[...] = w3_ref[...] * BF(0.5)
    for c in range(3, cols - 3):
        block(c)
    get_wout.wait()
    wo = wout_ref[...].astype(F32) * (1.0 / STEPS)
    none = jnp.zeros((CH, 128), F32)
    lhs = []
    for sums in range(2):
        for j in range(half):
            parts = [wo if s <= sums and i == j else none for s in range(2) for i in range(half)]
            lhs.append(jnp.concatenate(parts, axis=1))
    wo_ref[...] = jnp.concatenate(lhs, axis=0).astype(BF)
    get_noise.wait()
    for ch in range(CH):
        at = pl.ds(ch, cols, stride=CH)
        n0 = 0.3 * noise_ref[0, ch]
        nz_ref[0, at, :] = n0
        nz_ref[1, at, :] = n0 + 0.3 * noise_ref[1, ch]
    for n in range(2, groups - 1):
        hear(n)
        pass_on(n + 1)

    pl.when(has_left)(halo_right.wait_recv)
    pl.when(has_right)(halo_left.wait_recv)
    for c in (-1, cols, -2, cols + 1, -3, cols + 2):
        inputs_first(c)
    for c in (0, -1, -2):
        first_pair((c, cols - 1 - c))
    for c in (1, 0, -1):
        second(c)
        second(cols - 1 - c)
    for c in (2, 1, 0):
        block(c)
        block(cols - 1 - c)
    a, g = project()
    pg_ref[...] = g.astype(BF)
    pa_ref[...] = a.astype(BF)

    def mids(d):
        def send(n, src, dst, tile):
            return remote(
                pg_ref.at[src],
                rx_ref.at[d - 1, dst],
                mid_send.at[d - 1, n],
                mid_recv.at[d - 1, n],
                k + d,
                tile,
            )

        return (
            send(0, first_half, at_right, t - 1),
            send(1, second_half, at_left, t + 1),
            send(2, pl.ds(0, 2 * rim), own, t),
        )

    mid = {d: mids(d) for d in range(1, groups)}
    near_left = remote(
        pa_ref.at[first_half], rxs_ref.at[at_right], near_send.at[0], near_recv.at[0], k, t - 1
    )
    near_right = remote(
        pa_ref.at[second_half], rxs_ref.at[at_left], near_send.at[1], near_recv.at[1], k, t + 1
    )
    far = sorted(range(1, groups), key=lambda d: -min(d, groups - d))
    for d in far:
        pl.when((k + d < groups) & has_left)(mid[d][0].start)
        pl.when((k + d < groups) & has_right)(mid[d][1].start)
    for d in far:
        pl.when(k + d < groups)(mid[d][2].start)
    pl.when(has_left)(near_left.start)
    pl.when(has_right)(near_right.start)

    @pl.when(has_left)
    def _():
        rim_right.wait_recv()
        near_right.wait_recv()

    @pl.when(has_right)
    def _():
        rim_left.wait_recv()
        near_left.wait_recv()

    for d in range(1, groups):
        pl.when(k >= d)(mid[d][2].wait_recv)
        pl.when((k >= d) & has_left)(mid[d][1].wait_recv)
        pl.when((k >= d) & has_right)(mid[d][0].wait_recv)

    base = st_ref[...]
    for d in range(groups - 1):
        base = base + rx_ref[d].astype(F32)
    base_ref[...] = base[rim : 3 * rim]
    step = jnp.concatenate(
        [rxs_ref[at_left].astype(F32), a, rxs_ref[at_right].astype(F32)], axis=0
    )
    states = (base, base + step)
    for c in range(-HALO, cols + HALO):
        at = CH * (c + half)
        cov = xb_ref[:, slot(c)].astype(F32)[CH:]
        for s in range(2):
            v = jnp.concatenate([states[s][at : at + CH], cov], axis=0)
            store_taps(x2_ref, v.astype(BF), 2 * (c + HALO) + s)
    for c in range(-2, cols + 2):
        first(c)
    for c in range(-1, cols + 1):
        second(c)
    for c in range(cols):
        block(c)
    a, g = project()
    pd_ref[...] = (g - pg_ref[...].astype(F32)).astype(BF)
    last = {
        d: remote(pd_ref, rxf_ref.at[d - 1], last_send.at[d - 1], last_recv.at[d - 1], k + d, t)
        for d in range(1, groups)
    }
    for d in far:
        pl.when(k + d < groups)(last[d].start)

    @pl.when(has_left)
    def _():
        halo_left.wait_send()
        rim_left.wait_send()
        near_left.wait_send()

    @pl.when(has_right)
    def _():
        halo_right.wait_send()
        rim_right.wait_send()
        near_right.wait_send()

    for d in range(1, groups):
        pl.when(k + d < groups)(mid[d][2].wait_send)
        pl.when((k + d < groups) & has_left)(mid[d][0].wait_send)
        pl.when((k + d < groups) & has_right)(mid[d][1].wait_send)

    for d in range(1, groups):
        pl.when(k >= d)(last[d].wait_recv)
    base = base_ref[...]
    for d in range(groups - 1):
        base = base + rxf_ref[d].astype(F32)
    for s, v in enumerate((a, g)):
        base_ref[...] = base + v
        for ch in range(CH):
            out_ref[s, ch] = base_ref[pl.ds(ch, cols, stride=CH), :]
    for d in range(1, groups):
        pl.when(k + d < groups)(last[d].wait_send)


def solution(mesh):
    groups, tiles = mesh.shape["step"], mesh.shape["tile"]

    def local(start_state, covariates, noise, embedding, w_in, w_first, w_second, w_out):
        cols = start_state.shape[1]
        wide = cols + 2 * HALO
        hbm = pl.BlockSpec(memory_space=pltpu.HBM)
        dma = pltpu.SemaphoreType.DMA
        w_in = jnp.swapaxes(w_in, 1, 2).reshape(144, 128)

        def body(*refs):
            kernel(groups, tiles, *refs)

        args = [
            pltpu.with_memory_space_constraint(v, pltpu.HBM)
            for v in (start_state, covariates, noise, embedding, w_in, w_first, w_second, w_out)
        ]
        return pl.pallas_call(
            body,
            out_shape=pltpu.VMEM((2, 4, cols, ROWS), F32),
            in_specs=[hbm] * 8,
            out_specs=pl.BlockSpec(memory_space=pltpu.VMEM),
            scratch_shapes=[
                pltpu.VMEM((CH, cols, ROWS), F32),
                pltpu.VMEM((12, cols, ROWS), BF),
                pltpu.VMEM((2, CH, cols, ROWS), F32),
                pltpu.VMEM((2, 128), F32),
                pltpu.VMEM((144, 128), BF),
                pltpu.VMEM((CH, 128), BF),
                pltpu.VMEM((12, cols, ROWS), F32),
                pltpu.VMEM((2 * CH * cols, ROWS), F32),
                pltpu.VMEM((CH * cols, ROWS), F32),
                pltpu.VMEM((16, wide * ROWS), BF),
                pltpu.VMEM((48, wide * ROWS), BF),
                pltpu.VMEM((48, wide * 2 * ROWS), BF),
                pltpu.VMEM((128, 144), BF),
                pltpu.VMEM((128, 1152), BF),
                pltpu.VMEM((128, 1152), BF),
                pltpu.VMEM((CH * cols, 128 * cols), BF),
                pltpu.VMEM((128, 2 * ROWS), F32),
                pltpu.VMEM((2, CH * cols, ROWS), F32),
                pltpu.VMEM((384, (wide - 2) * 2 * ROWS), BF),
                pltpu.VMEM((384, (wide - 4) * 2 * ROWS), BF),
                pltpu.VMEM((128 * cols, 2 * ROWS), BF),
                pltpu.VMEM((CH * cols, ROWS), BF),
                pltpu.VMEM((CH * cols, ROWS), BF),
                pltpu.VMEM((CH * cols, ROWS), BF),
                pltpu.VMEM((groups - 1, 2 * CH * cols, ROWS), BF),
                pltpu.VMEM((2 * CH * cols, ROWS), BF),
                pltpu.VMEM((groups - 1, CH * cols, ROWS), BF),
                dma((6,)),
                dma((2, 9)),
                dma((2,)),
                dma((2,)),
                dma((2,)),
                dma((2,)),
                dma((2,)),
                dma((2,)),
                dma((groups - 1, 3)),
                dma((groups - 1, 3)),
                dma((groups - 1,)),
                dma((groups - 1,)),
                pltpu.SemaphoreType.REGULAR((groups - 1,)),
            ],
            compiler_params=pltpu.CompilerParams(
                collective_id=0, has_side_effects=True, vmem_limit_bytes=40 << 20
            ),
        )(*args)

    in_specs = (
        P(None, "tile", None),
        P(None, "tile", None),
        P("step", None, "tile", None),
        P("step", None),
        P(),
        P(),
        P(),
        P(),
    )
    out_specs = P("step", None, "tile", None)
    return jax.shard_map(local, mesh=mesh, in_specs=in_specs, out_specs=out_specs, check_vma=False)
```

```python
import jax
import jax.numpy as jnp
from jax import lax
from jax.experimental import pallas as pl
from jax.experimental.pallas import tpu as pltpu
from jax.sharding import PartitionSpec as P

STEPS = 8
SWEEPS = 2
CH = 4
HALO = 3
ROWS = 128
BF = jnp.bfloat16
F32 = jnp.float32
MESH = pl.DeviceIdType.MESH


def silu_of_half(h):
    return h * jnp.tanh(h) + h


def kernel(
    groups,
    tiles,
    start_hbm,
    cov_hbm,
    noise_hbm,
    embed_hbm,
    win_hbm,
    wfirst_hbm,
    wsecond_hbm,
    wout_hbm,
    out_ref,
    start_ref,
    cov_ref,
    noise_ref,
    embed_ref,
    win_ref,
    wout_ref,
    covf_ref,
    st_ref,
    base_ref,
    xb_ref,
    x1_ref,
    x2_ref,
    w1_ref,
    w2_ref,
    w3_ref,
    wo_ref,
    eb_ref,
    nz_ref,
    fh_ref,
    sh_ref,
    bo_ref,
    pa_ref,
    pg_ref,
    pd_ref,
    rx_ref,
    rxs_ref,
    rxf_ref,
    in_sem,
    win_sem,
    w_sem,
    halo_send,
    halo_recv,
    rim_send,
    rim_recv,
    near_send,
    near_recv,
    mid_send,
    mid_recv,
    last_send,
    last_recv,
    chain,
):
    k = lax.axis_index("step")
    t = lax.axis_index("tile")
    cols = start_ref.shape[1]
    half = cols // 2
    rim = CH * half

    even = t % 2 == 0
    fast = jnp.where(even, t + 1, t - 1)
    slow = jnp.where(even, t - 1, t + 1)
    has_slow = (slow >= 0) & (slow < tiles)

    def turned(n, count):
        return jnp.where(even, count - 1 - n, n)

    def either_way(f):
        @pl.when(even)
        def _():
            for c in range(cols):
                f(c, cols - 1 - c)

        @pl.when(jnp.logical_not(even))
        def _():
            for c in range(cols):
                f(c, c)

    get_start, get_cov, get_embed, get_noise, get_wout = [
        pltpu.make_async_copy(src, dst, in_sem.at[n])
        for n, (src, dst) in enumerate(
            (
                (start_hbm, start_ref),
                (cov_hbm, cov_ref),
                (embed_hbm, embed_ref),
                (noise_hbm, noise_ref),
                (wout_hbm, wout_ref),
            )
        )
    ]
    get_win = [
        pltpu.make_async_copy(
            win_hbm.at[pl.ds(a * 48, 48)],
            win_ref.at[pl.ds(pl.multiple_of(turned(a, 3) * 48, 48), 48)],
            win_sem.at[a],
        )
        for a in range(3)
    ]
    weights = []
    for n, (src, dst) in enumerate(((wfirst_hbm, w2_ref), (wsecond_hbm, w3_ref))):
        weights.append(
            [
                pltpu.make_async_copy(
                    src.at[3 * a + b],
                    dst.at[:, pl.ds(pl.multiple_of((3 * turned(a, 3) + b) * 128, 128), 128)],
                    w_sem.at[n, 3 * a + b],
                )
                for a in range(3)
                for b in range(3)
            ]
        )
    get_start.start()
    get_cov.start()

    for ref in (st_ref, xb_ref, rx_ref, rxs_ref, rxf_ref):
        ref[...] = jnp.zeros_like(ref)

    barrier = pltpu.get_barrier_semaphore()

    def signal(sem, step, tile):
        pl.semaphore_signal(sem, inc=1, device_id=(step, tile), device_id_type=MESH)

    pl.when(has_slow)(lambda: signal(barrier, k, slow))
    pl.when(k > 0)(lambda: signal(barrier, k - 1, t))
    pl.when(k < groups - 1)(lambda: signal(barrier, k + 1, t))
    signal(barrier, k, fast)

    for c in (*get_win, get_embed, *weights[0], *weights[1], get_noise, get_wout):
        c.start()

    def lanes(n, width=1):
        return pl.ds(n * ROWS, width * ROWS)

    def place(i):
        if i < 0:
            return -1 - i
        if i >= cols:
            return HALO + cols + HALO - 1 - (i - cols)
        return HALO + i

    def row_of(i):
        if i < 0:
            return CH * (-1 - i)
        if i >= cols:
            return 3 * rim + CH * (half - 1 - (i - cols))
        return rim + CH * i

    get_cov.wait()
    covf_ref[...] = cov_ref[...].astype(F32)
    get_start.wait()

    def put_inputs(c, i):
        x = jnp.concatenate([start_ref[:, c, :], covf_ref[:, c, :]], axis=0)
        xb_ref[:, lanes(place(i))] = x.astype(BF)

    either_way(put_inputs)

    def one(p):
        return p.astype(jnp.int32)

    pl.semaphore_wait(barrier, 1 + one(has_slow) + one(k > 0) + one(k < groups - 1))

    def remote(src, dst, send, recv, step, tile):
        return pltpu.make_async_remote_copy(
            src_ref=src,
            dst_ref=dst,
            send_sem=send,
            recv_sem=recv,
            device_id=(step, tile),
            device_id_type=MESH,
        )

    def to_sides(ref, parts, send, recv):
        at_fast, own_fast, own_slow, at_slow = parts
        return (
            remote(ref.at[own_fast], ref.at[at_fast], send.at[0], recv.at[0], k, fast),
            remote(ref.at[own_slow], ref.at[at_slow], send.at[1], recv.at[1], k, slow),
        )

    strips = [(slice(None), lanes(n, HALO)) for n in (0, HALO, cols, cols + HALO)]
    halo_fast, halo_slow = to_sides(xb_ref, strips, halo_send, halo_recv)
    pl.when(has_slow)(halo_slow.start)
    halo_fast.start()

    at_fast, own_fast, own_slow, at_slow = quarters = [pl.ds(n * rim, rim) for n in range(4)]
    halves = (pl.ds(0, rim), pl.ds(rim, rim))

    def put_state(c, i):
        st_ref[row_of(i) : row_of(i) + CH, :] = start_ref[:, c, :]

    either_way(put_state)
    rim_fast, rim_slow = to_sides(st_ref, quarters, rim_send, rim_recv)
    pl.when(has_slow)(rim_slow.start)
    rim_fast.start()

    def pass_on(n):
        if n < groups - 1:
            pl.when((k > 0) & (k < groups - n))(lambda: signal(chain.at[n], k - 1, t))

    def hear(n):
        pl.when(k < groups - 1 - n)(lambda: pl.semaphore_wait(chain.at[n], 1))

    pass_on(0)

    for c in get_win:
        c.wait()
    w1_ref[...] = jnp.transpose(win_ref[...].astype(F32) * 0.5).astype(BF)
    get_embed.wait()
    et = 0.5 * jnp.transpose(jnp.concatenate([embed_ref[...], jnp.zeros((6, 128), F32)], axis=0))
    for s in range(2):
        eb_ref[:, pl.ds(s * ROWS, ROWS)] = jnp.broadcast_to(et[:, s : s + 1], (128, ROWS))

    lane = lax.broadcasted_iota(jnp.int32, (1, ROWS), 1)
    keep_first = (lane > 0).astype(F32).astype(BF)
    keep_last = (lane < ROWS - 1).astype(F32).astype(BF)
    slow_one = has_slow.astype(F32)

    def store_taps(ref, x, at):
        n = x.shape[0]
        at = pl.ds(at * ROWS, ROWS)
        ref[0:n, at] = pltpu.roll(x, 1, 1) * keep_first
        ref[n : 2 * n, at] = x
        ref[2 * n : 3 * n, at] = pltpu.roll(x, ROWS - 1, 1) * keep_last

    def store_both(ref, h, at):
        for s in range(2):
            store_taps(ref, h[:, s * ROWS : (s + 1) * ROWS], 2 * at + s)

    def taps_of(ref, at):
        return jnp.concatenate(
            [ref[:, pl.ds((at + a) * 2 * ROWS, 2 * ROWS)] for a in range(3)], axis=0
        )

    def inside(h, c):
        return h * slow_one if c >= cols else h

    def first_done(pre, c):
        h = inside(silu_of_half(pre + eb_ref[...]), c)
        store_both(fh_ref, h.astype(BF), c + 2)

    def first(c):
        first_done(jnp.dot(w1_ref[...], taps_of(x2_ref, c + 2), preferred_element_type=F32), c)

    def first_pair(pair):
        taps = jnp.concatenate(
            [
                jnp.concatenate([x1_ref[:, lanes(c + 2 + a)] for c in pair], axis=1)
                for a in range(3)
            ],
            axis=0,
        )
        pre = jnp.dot(w1_ref[...], taps, preferred_element_type=F32)
        for n, c in enumerate(pair):
            p = pre[:, n * ROWS : (n + 1) * ROWS]
            first_done(jnp.concatenate([p, p], axis=1), c)

    def second(c):
        h = jnp.dot(w2_ref[...], taps_of(fh_ref, c + 1), preferred_element_type=F32)
        store_both(sh_ref, inside(silu_of_half(h), c).astype(BF), c + 1)

    def block(c):
        h = silu_of_half(jnp.dot(w3_ref[...], taps_of(sh_ref, c), preferred_element_type=F32))
        h = (h + fh_ref[128:256, pl.ds((c + 2) * 2 * ROWS, 2 * ROWS)].astype(F32)).astype(BF)
        for s in range(2):
            at = (s * half + c % half) * 128
            bo_ref[at : at + 128, pl.ds((c // half) * ROWS, ROWS)] = h[:, s * ROWS : (s + 1) * ROWS]

    def project(h):
        p = jnp.dot(wo_ref[...], bo_ref[:, lanes(h)], preferred_element_type=F32)
        return p[:rim] + nz_ref[0, halves[h], :], p[rim:] + nz_ref[1, halves[h], :]

    def inputs_first(c):
        store_taps(x1_ref, xb_ref[:, lanes(place(c))], c + HALO)

    for c in range(cols):
        inputs_first(c)
    for c in range(1, cols - 1, 2):
        first_pair((c, c + 1))
    hear(0)
    pass_on(1)
    for c in weights[0]:
        c.wait()
    w2_ref[...] = w2_ref[...] * BF(0.5)
    for c in range(2, cols - 2):
        second(c)
    hear(1)
    pass_on(2)
    for c in weights[1]:
        c.wait()
    w3_ref[...] = w3_ref[...] * BF(0.5)
    for c in range(3, cols - 3):
        block(c)
    get_wout.wait()
    wo = wout_ref[...].astype(F32) * (1.0 / STEPS)
    none = jnp.zeros((CH, 128), F32)
    lhs = []
    for sums in range(2):
        for j in range(half):
            parts = [wo if s <= sums and i == j else none for s in range(2) for i in range(half)]
            lhs.append(jnp.concatenate(parts, axis=1))
    wo_ref[...] = jnp.concatenate(lhs, axis=0).astype(BF)
    get_noise.wait()

    def put_noise(c, i):
        n0 = 0.3 * noise_ref[0, :, c, :]
        nz_ref[0, CH * i : CH * (i + 1), :] = n0
        nz_ref[1, CH * i : CH * (i + 1), :] = n0 + 0.3 * noise_ref[1, :, c, :]

    either_way(put_noise)

    halo_fast.wait_recv()
    for c in (-1, -2, -3):
        inputs_first(c)
    first_pair((0, -1))
    first_pair((-2,))
    for c in (1, 0, -1):
        second(c)
    for c in (2, 1, 0):
        block(c)
    for n in range(2, groups - 1):
        hear(n)
        pass_on(n + 1)

    def mids(d):
        def send(n, src, dst, tile):
            return remote(
                pg_ref.at[src],
                rx_ref.at[d - 1, dst],
                mid_send.at[d - 1, n],
                mid_recv.at[d - 1, n],
                k + d,
                tile,
            )

        return (
            send(0, halves[0], at_fast, fast),
            send(1, halves[0], own_fast, t),
            send(2, halves[1], at_slow, slow),
            send(3, halves[1], own_slow, t),
        )

    mid = {d: mids(d) for d in range(1, groups)}
    near_fast = remote(
        pa_ref.at[halves[0]], rxs_ref.at[at_fast], near_send.at[0], near_recv.at[0], k, fast
    )
    near_slow = remote(
        pa_ref.at[halves[1]], rxs_ref.at[at_slow], near_send.at[1], near_recv.at[1], k, slow
    )
    far = sorted(range(1, groups), key=lambda d: -min(d, groups - d))

    def put_sums(h):
        a, g = project(h)
        pg_ref[halves[h], :] = g.astype(BF)
        pa_ref[halves[h], :] = a.astype(BF)
        return a

    a_fast = put_sums(0)
    for d in far:

        @pl.when(k + d < groups)
        def _():
            mid[d][0].start()
            mid[d][1].start()

    near_fast.start()

    pl.when(has_slow)(halo_slow.wait_recv)
    for c in (cols, cols + 1, cols + 2):
        inputs_first(c)
    first_pair((cols - 1, cols))
    first_pair((cols + 1,))
    for c in (cols - 2, cols - 1, cols):
        second(c)
    for c in (cols - 3, cols - 2, cols - 1):
        block(c)
    a_slow = put_sums(1)
    for d in far:
        pl.when((k + d < groups) & has_slow)(mid[d][2].start)
        pl.when(k + d < groups)(mid[d][3].start)
    pl.when(has_slow)(near_slow.start)

    rim_fast.wait_recv()
    near_fast.wait_recv()
    for d in range(1, groups):

        @pl.when(k >= d)
        def _():
            mid[d][0].wait_recv()
            mid[d][1].wait_recv()
            mid[d][3].wait_recv()

    def base_of(rows):
        base = st_ref[rows, :]
        for d in range(groups - 1):
            base = base + rx_ref[d, rows, :].astype(F32)
        return base

    def inputs_next(c, base, step, row):
        cov = xb_ref[:, lanes(place(c))].astype(F32)[CH:]
        for s, state in enumerate((base, base + step)):
            v = jnp.concatenate([state[row : row + CH], cov], axis=0)
            store_taps(x2_ref, v.astype(BF), 2 * (c + HALO) + s)

    base = base_of(pl.ds(0, 3 * rim))
    base_ref[...] = base[rim:]
    step = jnp.concatenate([rxs_ref[at_fast, :].astype(F32), a_fast, a_slow], axis=0)
    for c in range(-HALO, cols):
        inputs_next(c, base, step, row_of(c))
    for c in range(-2, cols - 1):
        first(c)
    for c in range(-1, cols - 2):
        second(c)
    for c in range(cols - 3):
        block(c)

    def lasts(d):
        return [
            remote(
                pd_ref.at[at],
                rxf_ref.at[d - 1, at],
                last_send.at[d - 1, h],
                last_recv.at[d - 1, h],
                k + d,
                t,
            )
            for h, at in enumerate(halves)
        ]

    last = {d: lasts(d) for d in range(1, groups)}

    def put_last(h):
        a, g = project(h)
        pd_ref[halves[h], :] = (g - pg_ref[halves[h], :].astype(F32)).astype(BF)
        for d in far:
            pl.when(k + d < groups)(last[d][h].start)
        return a, g

    a_fast, g_fast = put_last(0)

    @pl.when(has_slow)
    def _():
        rim_slow.wait_recv()
        near_slow.wait_recv()

    for d in range(1, groups):
        pl.when((k >= d) & has_slow)(mid[d][2].wait_recv)
    base = base_of(at_slow)
    step = rxs_ref[at_slow, :].astype(F32)
    for c in range(cols, cols + HALO):
        inputs_next(c, base, step, row_of(c) - 3 * rim)
    for c in (cols - 1, cols, cols + 1):
        first(c)
    for c in (cols - 2, cols - 1, cols):
        second(c)
    for c in (cols - 3, cols - 2, cols - 1):
        block(c)
    a_slow, g_slow = put_last(1)

    halo_fast.wait_send()
    rim_fast.wait_send()
    near_fast.wait_send()

    @pl.when(has_slow)
    def _():
        halo_slow.wait_send()
        rim_slow.wait_send()
        near_slow.wait_send()

    for d in range(1, groups):

        @pl.when(k + d < groups)
        def _():
            mid[d][0].wait_send()
            mid[d][1].wait_send()
            mid[d][3].wait_send()

        pl.when((k + d < groups) & has_slow)(mid[d][2].wait_send)

    for d in range(1, groups):

        @pl.when(k >= d)
        def _():
            last[d][0].wait_recv()
            last[d][1].wait_recv()

    base = base_ref[...]
    for d in range(groups - 1):
        base = base + rxf_ref[d].astype(F32)
    sums = [
        base + jnp.concatenate(halves_of, axis=0)
        for halves_of in ((a_fast, a_slow), (g_fast, g_slow))
    ]

    def put_result(c, i):
        for s in range(2):
            out_ref[s, :, c, :] = sums[s][CH * i : CH * (i + 1)]

    either_way(put_result)
    for d in range(1, groups):

        @pl.when(k + d < groups)
        def _():
            last[d][0].wait_send()
            last[d][1].wait_send()


def solution(mesh):
    groups, tiles = mesh.shape["step"], mesh.shape["tile"]

    def local(start_state, covariates, noise, embedding, w_in, w_first, w_second, w_out):
        cols = start_state.shape[1]
        wide = cols + 2 * HALO
        hbm = pl.BlockSpec(memory_space=pltpu.HBM)
        dma = pltpu.SemaphoreType.DMA
        w_in = jnp.swapaxes(w_in, 1, 2).reshape(144, 128)

        def body(*refs):
            kernel(groups, tiles, *refs)

        args = [
            pltpu.with_memory_space_constraint(v, pltpu.HBM)
            for v in (start_state, covariates, noise, embedding, w_in, w_first, w_second, w_out)
        ]
        return pl.pallas_call(
            body,
            out_shape=pltpu.VMEM((2, 4, cols, ROWS), F32),
            in_specs=[hbm] * 8,
            out_specs=pl.BlockSpec(memory_space=pltpu.VMEM),
            scratch_shapes=[
                pltpu.VMEM((CH, cols, ROWS), F32),
                pltpu.VMEM((12, cols, ROWS), BF),
                pltpu.VMEM((2, CH, cols, ROWS), F32),
                pltpu.VMEM((2, 128), F32),
                pltpu.VMEM((144, 128), BF),
                pltpu.VMEM((CH, 128), BF),
                pltpu.VMEM((12, cols, ROWS), F32),
                pltpu.VMEM((2 * CH * cols, ROWS), F32),
                pltpu.VMEM((CH * cols, ROWS), F32),
                pltpu.VMEM((16, wide * ROWS), BF),
                pltpu.VMEM((48, wide * ROWS), BF),
                pltpu.VMEM((48, wide * 2 * ROWS), BF),
                pltpu.VMEM((128, 144), BF),
                pltpu.VMEM((128, 1152), BF),
                pltpu.VMEM((128, 1152), BF),
                pltpu.VMEM((CH * cols, 128 * cols), BF),
                pltpu.VMEM((128, 2 * ROWS), F32),
                pltpu.VMEM((2, CH * cols, ROWS), F32),
                pltpu.VMEM((384, (wide - 2) * 2 * ROWS), BF),
                pltpu.VMEM((384, (wide - 4) * 2 * ROWS), BF),
                pltpu.VMEM((128 * cols, 2 * ROWS), BF),
                pltpu.VMEM((CH * cols, ROWS), BF),
                pltpu.VMEM((CH * cols, ROWS), BF),
                pltpu.VMEM((CH * cols, ROWS), BF),
                pltpu.VMEM((groups - 1, 2 * CH * cols, ROWS), BF),
                pltpu.VMEM((2 * CH * cols, ROWS), BF),
                pltpu.VMEM((groups - 1, CH * cols, ROWS), BF),
                dma((5,)),
                dma((3,)),
                dma((2, 9)),
                dma((2,)),
                dma((2,)),
                dma((2,)),
                dma((2,)),
                dma((2,)),
                dma((2,)),
                dma((groups - 1, 4)),
                dma((groups - 1, 4)),
                dma((groups - 1, 2)),
                dma((groups - 1, 2)),
                pltpu.SemaphoreType.REGULAR((groups - 1,)),
            ],
            compiler_params=pltpu.CompilerParams(
                collective_id=0, has_side_effects=True, vmem_limit_bytes=40 << 20
            ),
        )(*args)

    in_specs = (
        P(None, "tile", None),
        P(None, "tile", None),
        P("step", None, "tile", None),
        P("step", None),
        P(),
        P(),
        P(),
        P(),
    )
    out_specs = P("step", None, "tile", None)
    return jax.shard_map(local, mesh=mesh, in_specs=in_specs, out_specs=out_specs, check_vma=False)
```

```python
import jax
import jax.numpy as jnp
from jax import lax
from jax.experimental import pallas as pl
from jax.experimental.pallas import tpu as pltpu
from jax.sharding import PartitionSpec as P

STEPS = 8
SWEEPS = 2
CH = 4
HALO = 3
ROWS = 128
BF = jnp.bfloat16
F32 = jnp.float32
MESH = pl.DeviceIdType.MESH


def silu_of_half(h):
    return h * jnp.tanh(h) + h


def kernel(
    groups,
    tiles,
    start_hbm,
    cov_hbm,
    noise_hbm,
    embed_hbm,
    win_hbm,
    wfirst_hbm,
    wsecond_hbm,
    wout_hbm,
    out_ref,
    start_ref,
    cov_ref,
    noise_ref,
    embed_ref,
    win_ref,
    wout_ref,
    covf_ref,
    st_ref,
    base_ref,
    xb_ref,
    x1_ref,
    x2_ref,
    w1_ref,
    w2_ref,
    w3_ref,
    wo0_ref,
    wo1_ref,
    eb_ref,
    nz_ref,
    fh_ref,
    sh_ref,
    bo0_ref,
    bo1_ref,
    pa_ref,
    pg_ref,
    pd_ref,
    rx_ref,
    rxs_ref,
    rxf_ref,
    in_sem,
    win_sem,
    w_sem,
    halo_send,
    halo_recv,
    rim_send,
    rim_recv,
    near_send,
    near_recv,
    mid_send,
    mid_recv,
    last_send,
    last_recv,
    chain,
):
    k = lax.axis_index("step")
    t = lax.axis_index("tile")
    cols = start_ref.shape[1]
    soon = cols - HALO
    rim = 16
    early, late = 2 * rim, rim

    even = t % 2 == 0
    fast = jnp.where(even, t + 1, t - 1)
    slow = jnp.where(even, t - 1, t + 1)
    has_slow = (slow >= 0) & (slow < tiles)

    def turned(n, count):
        return jnp.where(even, count - 1 - n, n)

    def either_way(f):
        @pl.when(even)
        def _():
            for c in range(cols):
                f(c, cols - 1 - c)

        @pl.when(jnp.logical_not(even))
        def _():
            for c in range(cols):
                f(c, c)

    get_start, get_cov, get_embed, get_noise, get_wout = [
        pltpu.make_async_copy(src, dst, in_sem.at[n])
        for n, (src, dst) in enumerate(
            (
                (start_hbm, start_ref),
                (cov_hbm, cov_ref),
                (embed_hbm, embed_ref),
                (noise_hbm, noise_ref),
                (wout_hbm, wout_ref),
            )
        )
    ]
    get_win = [
        pltpu.make_async_copy(
            win_hbm.at[pl.ds(a * 48, 48)],
            win_ref.at[pl.ds(pl.multiple_of(turned(a, 3) * 48, 48), 48)],
            win_sem,
        )
        for a in range(3)
    ]
    weights = []
    for n, (src, dst) in enumerate(((wfirst_hbm, w2_ref), (wsecond_hbm, w3_ref))):
        weights.append(
            [
                pltpu.make_async_copy(
                    src.at[3 * a + b],
                    dst.at[:, pl.ds(pl.multiple_of((3 * turned(a, 3) + b) * 128, 128), 128)],
                    w_sem.at[n],
                )
                for a in range(3)
                for b in range(3)
            ]
        )
    get_start.start()
    get_cov.start()

    for ref in (st_ref, xb_ref, rx_ref, rxs_ref, rxf_ref):
        ref[...] = jnp.zeros_like(ref)

    barrier = pltpu.get_barrier_semaphore()

    def signal(sem, step, tile):
        pl.semaphore_signal(sem, inc=1, device_id=(step, tile), device_id_type=MESH)

    pl.when(has_slow)(lambda: signal(barrier, k, slow))
    pl.when(k > 0)(lambda: signal(barrier, k - 1, t))
    pl.when(k < groups - 1)(lambda: signal(barrier, k + 1, t))
    signal(barrier, k, fast)

    for c in (*get_win, get_embed, *weights[0], *weights[1], get_noise, get_wout):
        c.start()

    def lanes(n, width=1):
        return pl.ds(n * ROWS, width * ROWS)

    def place(i):
        if i < 0:
            return -1 - i
        if i >= cols:
            return HALO + cols + HALO - 1 - (i - cols)
        return HALO + i

    def row_of(i):
        if i < 0:
            return CH * (-1 - i)
        if i >= cols:
            return rim + early + late + CH * (HALO - 1 - (i - cols))
        return rim + own_row(i)

    def own_row(i):
        return CH * i if i < soon else early + CH * (i - soon)

    get_cov.wait()
    covf_ref[...] = cov_ref[...].astype(F32)
    get_start.wait()

    def put_inputs(c, i):
        x = jnp.concatenate([start_ref[:, c, :], covf_ref[:, c, :]], axis=0)
        xb_ref[:, lanes(place(i))] = x.astype(BF)

    either_way(put_inputs)

    def one(p):
        return p.astype(jnp.int32)

    pl.semaphore_wait(barrier, 1 + one(has_slow) + one(k > 0) + one(k < groups - 1))

    def remote(src, dst, send, recv, step, tile):
        return pltpu.make_async_remote_copy(
            src_ref=src,
            dst_ref=dst,
            send_sem=send,
            recv_sem=recv,
            device_id=(step, tile),
            device_id_type=MESH,
        )

    def for_later(f):
        def at(d):
            if d < groups:

                @pl.when(k + d < groups)
                def _():
                    f(d)
                    at(d + 1)

        at(1)

    def for_earlier(f):
        def at(d):
            if d < groups:

                @pl.when(k >= d)
                def _():
                    f(d)
                    at(d + 1)

        at(1)

    def to_sides(ref, parts, send, recv):
        at_fast, own_fast, own_slow, at_slow = parts
        return (
            remote(ref.at[own_fast], ref.at[at_fast], send.at[0], recv.at[0], k, fast),
            remote(ref.at[own_slow], ref.at[at_slow], send.at[1], recv.at[1], k, slow),
        )

    strips = [(slice(None), lanes(n, HALO)) for n in (0, HALO, cols, cols + HALO)]
    halo_fast, halo_slow = to_sides(xb_ref, strips, halo_send, halo_recv)
    pl.when(has_slow)(halo_slow.start)
    halo_fast.start()

    at_fast, own_fast = pl.ds(0, rim), pl.ds(rim, rim)
    own_soon, own_late = pl.ds(rim, early), pl.ds(rim + early, late)
    at_slow = pl.ds(rim + early + late, rim)
    facing, parts = pl.ds(0, rim), (pl.ds(0, early), pl.ds(early, late))

    def put_state(c, i):
        st_ref[row_of(i) : row_of(i) + CH, :] = start_ref[:, c, :]

    either_way(put_state)
    rim_fast, rim_slow = to_sides(st_ref, (at_fast, own_fast, own_late, at_slow), rim_send, rim_recv)
    pl.when(has_slow)(rim_slow.start)
    rim_fast.start()

    def pass_on(n):
        if n < groups - 1:
            pl.when((k > 0) & (k < groups - n))(lambda: signal(chain.at[n], k - 1, t))

    def hear(n):
        pl.when(k < groups - 1 - n)(lambda: pl.semaphore_wait(chain.at[n], 1))

    pass_on(0)

    pltpu.make_async_copy(win_ref, win_ref, win_sem).wait()
    w1_ref[...] = jnp.transpose(win_ref[...].astype(F32) * 0.5).astype(BF)
    get_embed.wait()
    et = 0.5 * jnp.transpose(jnp.concatenate([embed_ref[...], jnp.zeros((6, 128), F32)], axis=0))
    for s in range(2):
        eb_ref[:, pl.ds(s * ROWS, ROWS)] = jnp.broadcast_to(et[:, s : s + 1], (128, ROWS))

    lane = lax.broadcasted_iota(jnp.int32, (1, ROWS), 1)
    keep_first = (lane > 0).astype(F32).astype(BF)
    keep_last = (lane < ROWS - 1).astype(F32).astype(BF)
    slow_one = has_slow.astype(F32)
    bo_refs = (bo0_ref, bo1_ref)
    wo_refs = (wo0_ref, wo1_ref)

    def store_taps(ref, x, at):
        n = x.shape[0]
        at = pl.ds(at * ROWS, ROWS)
        ref[0:n, at] = pltpu.roll(x, 1, 1) * keep_first
        ref[n : 2 * n, at] = x
        ref[2 * n : 3 * n, at] = pltpu.roll(x, ROWS - 1, 1) * keep_last

    def store_both(ref, h, at):
        for s in range(2):
            store_taps(ref, h[:, s * ROWS : (s + 1) * ROWS], 2 * at + s)

    def taps_of(ref, at):
        return jnp.concatenate(
            [ref[:, pl.ds((at + a) * 2 * ROWS, 2 * ROWS)] for a in range(3)], axis=0
        )

    def inside(h, c):
        return h * slow_one if c >= cols else h

    def first_done(pre, c):
        h = inside(silu_of_half(pre + eb_ref[...]), c)
        store_both(fh_ref, h.astype(BF), c + 2)

    def first(c):
        first_done(jnp.dot(w1_ref[...], taps_of(x2_ref, c + 2), preferred_element_type=F32), c)

    def first_pair(pair):
        taps = jnp.concatenate(
            [
                jnp.concatenate([x1_ref[:, lanes(c + 2 + a)] for c in pair], axis=1)
                for a in range(3)
            ],
            axis=0,
        )
        pre = jnp.dot(w1_ref[...], taps, preferred_element_type=F32)
        for n, c in enumerate(pair):
            p = pre[:, n * ROWS : (n + 1) * ROWS]
            first_done(jnp.concatenate([p, p], axis=1), c)

    def second(c):
        h = jnp.dot(w2_ref[...], taps_of(fh_ref, c + 1), preferred_element_type=F32)
        store_both(sh_ref, inside(silu_of_half(h), c).astype(BF), c + 1)

    def block(c):
        h = silu_of_half(jnp.dot(w3_ref[...], taps_of(sh_ref, c), preferred_element_type=F32))
        h = (h + fh_ref[128:256, pl.ds((c + 2) * 2 * ROWS, 2 * ROWS)].astype(F32)).astype(BF)
        n, j = (0, c) if c < soon else (1, c - soon)
        count = (soon, HALO)[n]
        for s in range(2):
            at = (s * count + j) * 128
            bo_refs[n][at : at + 128, :] = h[:, s * ROWS : (s + 1) * ROWS]

    def project(n):
        p = jnp.dot(wo_refs[n][...], bo_refs[n][...], preferred_element_type=F32)
        size = (early, late)[n]
        return p[:size] + nz_ref[0, parts[n], :], p[size:] + nz_ref[1, parts[n], :]

    def inputs_first(c):
        x = xb_ref[:, lanes(place(c))]
        store_taps(x1_ref, x, c + HALO)

    for c in range(cols):
        inputs_first(c)
    for c in range(1, cols - 1, 2):
        first_pair((c, c + 1))
    hear(0)
    pass_on(1)
    pltpu.make_async_copy(w2_ref, w2_ref, w_sem.at[0]).wait()
    w2_ref[...] = w2_ref[...] * BF(0.5)
    for c in range(2, cols - 2):
        second(c)
    hear(1)
    pass_on(2)
    pltpu.make_async_copy(w3_ref, w3_ref, w_sem.at[1]).wait()
    w3_ref[...] = w3_ref[...] * BF(0.5)
    for c in range(3, cols - 3):
        block(c)
    get_wout.wait()
    wo = wout_ref[...].astype(F32) * (1.0 / STEPS)
    none = jnp.zeros((CH, 128), F32)
    for n, (count, size) in enumerate(((soon, early), (HALO, late))):
        lhs = []
        for sums in range(2):
            for j in range(count):
                blocks = [wo if s <= sums and i == j else none for s in range(2) for i in range(count)]
                lhs.append(jnp.concatenate(blocks, axis=1))
            lhs.append(jnp.zeros((size - CH * count, 2 * 128 * count), F32))
        wo_refs[n][...] = jnp.concatenate(lhs, axis=0).astype(BF)
    get_noise.wait()
    nz_ref[...] = jnp.zeros_like(nz_ref)

    def put_noise(c, i):
        at = own_row(i)
        n0 = 0.3 * noise_ref[0, :, c, :]
        nz_ref[0, at : at + CH, :] = n0
        nz_ref[1, at : at + CH, :] = n0 + 0.3 * noise_ref[1, :, c, :]

    either_way(put_noise)

    halo_fast.wait_recv()
    for c in (-1, -2, -3):
        inputs_first(c)
    first_pair((0, -1))
    first_pair((-2,))
    for c in (1, 0, -1):
        second(c)
    for c in (2, 1, 0):
        block(c)
    for n in range(2, groups - 1):
        hear(n)
        pass_on(n + 1)

    def mids(d):
        def send(n, src, dst, tile):
            return remote(
                pg_ref.at[src],
                rx_ref.at[d - 1, dst],
                mid_send.at[d - 1, n],
                mid_recv.at[d - 1, n],
                k + d,
                tile,
            )

        return (
            send(0, facing, at_fast, fast),
            send(1, parts[0], own_soon, t),
            send(2, parts[1], at_slow, slow),
            send(3, parts[1], own_late, t),
        )

    mid = {d: mids(d) for d in range(1, groups)}
    near_fast = remote(
        pa_ref.at[facing], rxs_ref.at[at_fast], near_send.at[0], near_recv.at[0], k, fast
    )
    near_slow = remote(
        pa_ref.at[parts[1]], rxs_ref.at[at_slow], near_send.at[1], near_recv.at[1], k, slow
    )

    def put_sums(n):
        a, g = project(n)
        pg_ref[parts[n], :] = g.astype(BF)
        pa_ref[parts[n], :] = a.astype(BF)
        return a

    def start_mid(*ns):
        def f(d):
            for n in ns:
                mid[d][n].start()

        return f

    def wait_mid(*ns):
        def f(d):
            for n in ns:
                mid[d][n].wait_recv()

        return f

    a_soon = put_sums(0)
    for_later(start_mid(1, 0))
    near_fast.start()

    pl.when(has_slow)(halo_slow.wait_recv)
    for c in (cols, cols + 1, cols + 2):
        inputs_first(c)
    first_pair((cols - 1, cols))
    first_pair((cols + 1,))
    for c in (cols - 2, cols - 1, cols):
        second(c)
    for c in (cols - 3, cols - 2, cols - 1):
        block(c)
    a_late = put_sums(1)

    @pl.when(has_slow)
    def _():
        for_later(start_mid(2, 3))
        near_slow.start()

    pl.when(jnp.logical_not(has_slow))(lambda: for_later(start_mid(3)))

    rim_fast.wait_recv()
    near_fast.wait_recv()
    for_earlier(wait_mid(0, 1))

    def base_of(rows):
        base = st_ref[rows, :]
        for d in range(groups - 1):
            base = base + rx_ref[d, rows, :].astype(F32)
        return base

    def inputs_next(c, base, step, row):
        cov = xb_ref[:, lanes(place(c))].astype(F32)[CH:]
        for s, state in enumerate((base, base + step)):
            v = jnp.concatenate([state[row : row + CH], cov], axis=0)
            store_taps(x2_ref, v.astype(BF), 2 * (c + HALO) + s)

    def next_columns(columns, rows, step, firsts, seconds, blocks):
        base = base_of(rows)
        for c in columns:
            inputs_next(c, base, step, row_of(c) - rows.start)
        for c in firsts:
            first(c)
        for c in seconds:
            second(c)
        for c in blocks:
            block(c)
        return base

    step = jnp.concatenate([rxs_ref[at_fast, :].astype(F32), a_soon], axis=0)
    base = next_columns(
        range(-HALO, soon), pl.ds(0, rim + early), step, range(-2, soon - 1), range(-1, soon - 2), range(soon - 3)
    )
    base_ref[parts[0], :] = base[rim:]

    for_earlier(wait_mid(3))
    base_ref[parts[1], :] = next_columns(
        range(soon, cols), own_late, a_late, range(soon - 1, cols - 1), range(soon - 2, cols - 2), range(soon - 3, soon)
    )

    def lasts(d):
        return [
            remote(
                pd_ref.at[at],
                rxf_ref.at[d - 1, at],
                last_send.at[d - 1, n],
                last_recv.at[d - 1, n],
                k + d,
                t,
            )
            for n, at in enumerate(parts)
        ]

    last = {d: lasts(d) for d in range(1, groups)}

    def put_last(n):
        a, g = project(n)
        pd_ref[parts[n], :] = (g - pg_ref[parts[n], :].astype(F32)).astype(BF)
        for_later(lambda d: last[d][n].start())
        return a, g

    a_soon, g_soon = put_last(0)

    @pl.when(has_slow)
    def _():
        rim_slow.wait_recv()
        near_slow.wait_recv()
        for_earlier(wait_mid(2))

    next_columns(
        range(cols, cols + HALO),
        at_slow,
        rxs_ref[at_slow, :].astype(F32),
        range(cols - 1, cols + 2),
        range(cols - 2, cols + 1),
        range(soon, cols),
    )
    a_late, g_late = put_last(1)

    def all_sent(*copies):
        for c in copies:
            c.wait_send()

    all_sent(halo_fast, rim_fast, near_fast)
    for_later(lambda d: all_sent(mid[d][0], mid[d][1], mid[d][3]))

    @pl.when(has_slow)
    def _():
        all_sent(halo_slow, rim_slow, near_slow)
        for_later(lambda d: all_sent(mid[d][2]))

    def got(d):
        for c in last[d]:
            c.wait_recv()

    for_earlier(got)
    base = base_ref[...]
    for d in range(groups - 1):
        base = base + rxf_ref[d].astype(F32)
    sums = [
        base + jnp.concatenate(both, axis=0) for both in ((a_soon, a_late), (g_soon, g_late))
    ]

    def put_result(c, i):
        at = own_row(i)
        for s in range(2):
            out_ref[s, :, c, :] = sums[s][at : at + CH]

    either_way(put_result)

    for_later(lambda d: all_sent(*last[d]))


def solution(mesh):
    groups, tiles = mesh.shape["step"], mesh.shape["tile"]

    def local(start_state, covariates, noise, embedding, w_in, w_first, w_second, w_out):
        cols = start_state.shape[1]
        wide = cols + 2 * HALO
        own = 48
        hbm = pl.BlockSpec(memory_space=pltpu.HBM)
        dma = pltpu.SemaphoreType.DMA
        w_in = jnp.swapaxes(w_in, 1, 2).reshape(144, 128)

        def body(*refs):
            kernel(groups, tiles, *refs)

        args = [
            pltpu.with_memory_space_constraint(v, pltpu.HBM)
            for v in (start_state, covariates, noise, embedding, w_in, w_first, w_second, w_out)
        ]
        return pl.pallas_call(
            body,
            out_shape=pltpu.VMEM((2, 4, cols, ROWS), F32),
            in_specs=[hbm] * 8,
            out_specs=pl.BlockSpec(memory_space=pltpu.VMEM),
            scratch_shapes=[
                pltpu.VMEM((CH, cols, ROWS), F32),
                pltpu.VMEM((12, cols, ROWS), BF),
                pltpu.VMEM((2, CH, cols, ROWS), F32),
                pltpu.VMEM((2, 128), F32),
                pltpu.VMEM((144, 128), BF),
                pltpu.VMEM((CH, 128), BF),
                pltpu.VMEM((12, cols, ROWS), F32),
                pltpu.VMEM((own + 32, ROWS), F32),
                pltpu.VMEM((own, ROWS), F32),
                pltpu.VMEM((16, wide * ROWS), BF),
                pltpu.VMEM((48, wide * ROWS), BF),
                pltpu.VMEM((48, wide * 2 * ROWS), BF),
                pltpu.VMEM((128, 144), BF),
                pltpu.VMEM((128, 1152), BF),
                pltpu.VMEM((128, 1152), BF),
                pltpu.VMEM((64, 256 * (cols - HALO)), BF),
                pltpu.VMEM((32, 256 * HALO), BF),
                pltpu.VMEM((128, 2 * ROWS), F32),
                pltpu.VMEM((2, own, ROWS), F32),
                pltpu.VMEM((384, (wide - 2) * 2 * ROWS), BF),
                pltpu.VMEM((384, (wide - 4) * 2 * ROWS), BF),
                pltpu.VMEM((256 * (cols - HALO), ROWS), BF),
                pltpu.VMEM((256 * HALO, ROWS), BF),
                pltpu.VMEM((own, ROWS), BF),
                pltpu.VMEM((own, ROWS), BF),
                pltpu.VMEM((own, ROWS), BF),
                pltpu.VMEM((groups - 1, own + 32, ROWS), BF),
                pltpu.VMEM((own + 32, ROWS), BF),
                pltpu.VMEM((groups - 1, own, ROWS), BF),
                dma((5,)),
                dma(()),
                dma((2,)),
                dma((2,)),
                dma((2,)),
                dma((2,)),
                dma((2,)),
                dma((2,)),
                dma((2,)),
                dma((groups - 1, 4)),
                dma((groups - 1, 4)),
                dma((groups - 1, 2)),
                dma((groups - 1, 2)),
                pltpu.SemaphoreType.REGULAR((groups - 1,)),
            ],
            compiler_params=pltpu.CompilerParams(
                collective_id=0, has_side_effects=True, vmem_limit_bytes=40 << 20
            ),
        )(*args)

    in_specs = (
        P(None, "tile", None),
        P(None, "tile", None),
        P("step", None, "tile", None),
        P("step", None),
        P(),
        P(),
        P(),
        P(),
    )
    out_specs = P("step", None, "tile", None)
    return jax.shard_map(local, mesh=mesh, in_specs=in_specs, out_specs=out_specs, check_vma=False)
```

```python
import jax
import jax.numpy as jnp
from jax import lax
from jax.experimental import pallas as pl
from jax.experimental.pallas import tpu as pltpu
from jax.sharding import PartitionSpec as P

STEPS = 8
SWEEPS = 2
CH = 4
HALO = 3
ROWS = 128
BF = jnp.bfloat16
F32 = jnp.float32
MESH = pl.DeviceIdType.MESH


def silu_of_half(h):
    return h * jnp.tanh(h) + h


def kernel(
    groups,
    tiles,
    start_hbm,
    cov_hbm,
    noise_hbm,
    embed_hbm,
    win_hbm,
    wfirst_hbm,
    wsecond_hbm,
    wout_hbm,
    out_ref,
    start_ref,
    cov_ref,
    noise_ref,
    embed_ref,
    win_ref,
    wout_ref,
    covf_ref,
    st_ref,
    base_ref,
    xb_ref,
    x1_ref,
    x2_ref,
    w1_ref,
    w2_ref,
    w3_ref,
    wo0_ref,
    wo1_ref,
    eb_ref,
    nz_ref,
    fh_ref,
    sh_ref,
    bo0_ref,
    bo1_ref,
    pa_ref,
    pg_ref,
    pd_ref,
    rx_ref,
    rxs_ref,
    rxf_ref,
    in_sem,
    win_sem,
    w_sem,
    halo_send,
    halo_recv,
    rim_send,
    rim_recv,
    near_send,
    near_recv,
    mid_send,
    mid_recv,
    last_send,
    last_recv,
    chain,
):
    k = lax.axis_index("step")
    t = lax.axis_index("tile")
    cols = start_ref.shape[1]
    soon = cols - HALO
    rim = 16
    early, late = 2 * rim, rim

    even = t % 2 == 0
    fast = jnp.where(even, t + 1, t - 1)
    slow = jnp.where(even, t - 1, t + 1)
    has_slow = (slow >= 0) & (slow < tiles)

    def turned(n, count):
        return jnp.where(even, count - 1 - n, n)

    def either_way(f):
        @pl.when(even)
        def _():
            for c in range(cols):
                f(c, cols - 1 - c)

        @pl.when(jnp.logical_not(even))
        def _():
            for c in range(cols):
                f(c, c)

    get_start, get_cov, get_embed, get_noise, get_wout = [
        pltpu.make_async_copy(src, dst, in_sem.at[n])
        for n, (src, dst) in enumerate(
            (
                (start_hbm, start_ref),
                (cov_hbm, cov_ref),
                (embed_hbm, embed_ref),
                (noise_hbm, noise_ref),
                (wout_hbm, wout_ref),
            )
        )
    ]
    get_win = [
        pltpu.make_async_copy(
            win_hbm.at[pl.ds(a * 48, 48)],
            win_ref.at[pl.ds(pl.multiple_of(turned(a, 3) * 48, 48), 48)],
            win_sem,
        )
        for a in range(3)
    ]
    weights = []
    for n, (src, dst) in enumerate(((wfirst_hbm, w2_ref), (wsecond_hbm, w3_ref))):
        weights.append(
            [
                pltpu.make_async_copy(
                    src.at[3 * a + b],
                    dst.at[:, pl.ds(pl.multiple_of((3 * turned(a, 3) + b) * 128, 128), 128)],
                    w_sem.at[n],
                )
                for a in range(3)
                for b in range(3)
            ]
        )
    get_start.start()
    get_cov.start()

    for ref in (st_ref, xb_ref, rx_ref, rxs_ref, rxf_ref):
        ref[...] = jnp.zeros_like(ref)

    barrier = pltpu.get_barrier_semaphore()

    def signal(sem, step, tile):
        pl.semaphore_signal(sem, inc=1, device_id=(step, tile), device_id_type=MESH)

    pl.when(has_slow)(lambda: signal(barrier, k, slow))
    for d in (groups // 2, *[d for d in range(1, groups) if d != groups // 2]):
        signal(barrier, lax.rem(k + d, groups), t)
    signal(barrier, k, fast)

    for c in (*get_win, get_embed, *weights[0], *weights[1], get_noise, get_wout):
        c.start()

    def lanes(n, width=1):
        return pl.ds(n * ROWS, width * ROWS)

    def place(i):
        if i < 0:
            return -1 - i
        if i >= cols:
            return HALO + cols + HALO - 1 - (i - cols)
        return HALO + i

    def row_of(i):
        if i < 0:
            return CH * (-1 - i)
        if i >= cols:
            return rim + early + late + CH * (HALO - 1 - (i - cols))
        return rim + own_row(i)

    def own_row(i):
        return CH * i if i < soon else early + CH * (i - soon)

    get_cov.wait()
    covf_ref[...] = cov_ref[...].astype(F32)
    get_start.wait()

    def put_inputs(c, i):
        x = jnp.concatenate([start_ref[:, c, :], covf_ref[:, c, :]], axis=0)
        xb_ref[:, lanes(place(i))] = x.astype(BF)

    either_way(put_inputs)

    def one(p):
        return p.astype(jnp.int32)

    pl.semaphore_wait(barrier, groups + one(has_slow))

    def remote(src, dst, send, recv, step, tile):
        return pltpu.make_async_remote_copy(
            src_ref=src,
            dst_ref=dst,
            send_sem=send,
            recv_sem=recv,
            device_id=(step, tile),
            device_id_type=MESH,
        )

    def for_later(f):
        def at(d):
            if d < groups:

                @pl.when(k + d < groups)
                def _():
                    f(d)
                    at(d + 1)

        at(1)

    def for_earlier(f):
        def at(d):
            if d < groups:

                @pl.when(k >= d)
                def _():
                    f(d)
                    at(d + 1)

        at(1)

    def to_sides(ref, parts, send, recv):
        at_fast, own_fast, own_slow, at_slow = parts
        return (
            remote(ref.at[own_fast], ref.at[at_fast], send.at[0], recv.at[0], k, fast),
            remote(ref.at[own_slow], ref.at[at_slow], send.at[1], recv.at[1], k, slow),
        )

    strips = [(slice(None), lanes(n, HALO)) for n in (0, HALO, cols, cols + HALO)]
    halo_fast, halo_slow = to_sides(xb_ref, strips, halo_send, halo_recv)
    pl.when(has_slow)(halo_slow.start)
    halo_fast.start()

    at_fast, own_fast = pl.ds(0, rim), pl.ds(rim, rim)
    own_soon, own_late = pl.ds(rim, early), pl.ds(rim + early, late)
    at_slow = pl.ds(rim + early + late, rim)
    facing, parts = pl.ds(0, rim), (pl.ds(0, early), pl.ds(early, late))

    def put_state(c, i):
        st_ref[row_of(i) : row_of(i) + CH, :] = start_ref[:, c, :]

    either_way(put_state)
    rim_fast, rim_slow = to_sides(st_ref, (at_fast, own_fast, own_late, at_slow), rim_send, rim_recv)
    pl.when(has_slow)(rim_slow.start)
    rim_fast.start()

    for_earlier(lambda d: signal(chain, k - d, t))

    pltpu.make_async_copy(win_ref, win_ref, win_sem).wait()
    w1_ref[...] = jnp.transpose(win_ref[...].astype(F32) * 0.5).astype(BF)
    get_embed.wait()
    et = 0.5 * jnp.transpose(jnp.concatenate([embed_ref[...], jnp.zeros((6, 128), F32)], axis=0))
    for s in range(2):
        eb_ref[:, pl.ds(s * ROWS, ROWS)] = jnp.broadcast_to(et[:, s : s + 1], (128, ROWS))

    lane = lax.broadcasted_iota(jnp.int32, (1, ROWS), 1)
    keep_first = (lane > 0).astype(F32).astype(BF)
    keep_last = (lane < ROWS - 1).astype(F32).astype(BF)
    slow_one = has_slow.astype(F32)
    bo_refs = (bo0_ref, bo1_ref)
    wo_refs = (wo0_ref, wo1_ref)

    def store_taps(ref, x, at):
        n = x.shape[0]
        at = pl.ds(at * ROWS, ROWS)
        ref[0:n, at] = pltpu.roll(x, 1, 1) * keep_first
        ref[n : 2 * n, at] = x
        ref[2 * n : 3 * n, at] = pltpu.roll(x, ROWS - 1, 1) * keep_last

    def store_both(ref, h, at):
        for s in range(2):
            store_taps(ref, h[:, s * ROWS : (s + 1) * ROWS], 2 * at + s)

    def taps_of(ref, at):
        return jnp.concatenate(
            [ref[:, pl.ds((at + a) * 2 * ROWS, 2 * ROWS)] for a in range(3)], axis=0
        )

    def inside(h, c):
        return h * slow_one if c >= cols else h

    def first_done(pre, c):
        h = inside(silu_of_half(pre + eb_ref[...]), c)
        store_both(fh_ref, h.astype(BF), c + 2)

    def first(c):
        first_done(jnp.dot(w1_ref[...], taps_of(x2_ref, c + 2), preferred_element_type=F32), c)

    def first_pair(pair):
        taps = jnp.concatenate(
            [
                jnp.concatenate([x1_ref[:, lanes(c + 2 + a)] for c in pair], axis=1)
                for a in range(3)
            ],
            axis=0,
        )
        pre = jnp.dot(w1_ref[...], taps, preferred_element_type=F32)
        for n, c in enumerate(pair):
            p = pre[:, n * ROWS : (n + 1) * ROWS]
            first_done(jnp.concatenate([p, p], axis=1), c)

    def second(c):
        h = jnp.dot(w2_ref[...], taps_of(fh_ref, c + 1), preferred_element_type=F32)
        store_both(sh_ref, inside(silu_of_half(h), c).astype(BF), c + 1)

    def block(c):
        h = silu_of_half(jnp.dot(w3_ref[...], taps_of(sh_ref, c), preferred_element_type=F32))
        h = (h + fh_ref[128:256, pl.ds((c + 2) * 2 * ROWS, 2 * ROWS)].astype(F32)).astype(BF)
        n, j = (0, c) if c < soon else (1, c - soon)
        count = (soon, HALO)[n]
        for s in range(2):
            at = (s * count + j) * 128
            bo_refs[n][at : at + 128, :] = h[:, s * ROWS : (s + 1) * ROWS]

    def project(n):
        p = jnp.dot(wo_refs[n][...], bo_refs[n][...], preferred_element_type=F32)
        size = (early, late)[n]
        return p[:size] + nz_ref[0, parts[n], :], p[size:] + nz_ref[1, parts[n], :]

    def inputs_first(c):
        x = xb_ref[:, lanes(place(c))]
        store_taps(x1_ref, x, c + HALO)

    for c in range(cols):
        inputs_first(c)
    for c in range(1, cols - 1, 2):
        first_pair((c, c + 1))
    pltpu.make_async_copy(w2_ref, w2_ref, w_sem.at[0]).wait()
    w2_ref[...] = w2_ref[...] * BF(0.5)
    for c in range(2, cols - 2):
        second(c)
    pltpu.make_async_copy(w3_ref, w3_ref, w_sem.at[1]).wait()
    w3_ref[...] = w3_ref[...] * BF(0.5)
    for c in range(3, cols - 3):
        block(c)
    get_wout.wait()
    wo = wout_ref[...].astype(F32) * (1.0 / STEPS)
    none = jnp.zeros((CH, 128), F32)
    for n, (count, size) in enumerate(((soon, early), (HALO, late))):
        lhs = []
        for sums in range(2):
            for j in range(count):
                blocks = [wo if s <= sums and i == j else none for s in range(2) for i in range(count)]
                lhs.append(jnp.concatenate(blocks, axis=1))
            lhs.append(jnp.zeros((size - CH * count, 2 * 128 * count), F32))
        wo_refs[n][...] = jnp.concatenate(lhs, axis=0).astype(BF)
    get_noise.wait()
    nz_ref[...] = jnp.zeros_like(nz_ref)

    def put_noise(c, i):
        at = own_row(i)
        n0 = 0.3 * noise_ref[0, :, c, :]
        nz_ref[0, at : at + CH, :] = n0
        nz_ref[1, at : at + CH, :] = n0 + 0.3 * noise_ref[1, :, c, :]

    either_way(put_noise)

    halo_fast.wait_recv()
    for c in (-1, -2, -3):
        inputs_first(c)
    first_pair((0, -1))
    first_pair((-2,))
    for c in (1, 0, -1):
        second(c)
    for c in (2, 1, 0):
        block(c)

    def mids(d):
        def send(n, src, dst, tile):
            return remote(
                pg_ref.at[src],
                rx_ref.at[d - 1, dst],
                mid_send.at[d - 1, n],
                mid_recv.at[d - 1, n],
                k + d,
                tile,
            )

        return (
            send(0, facing, at_fast, fast),
            send(1, parts[0], own_soon, t),
            send(2, parts[1], at_slow, slow),
            send(3, parts[1], own_late, t),
        )

    mid = {d: mids(d) for d in range(1, groups)}
    near_fast = remote(
        pa_ref.at[facing], rxs_ref.at[at_fast], near_send.at[0], near_recv.at[0], k, fast
    )
    near_slow = remote(
        pa_ref.at[parts[1]], rxs_ref.at[at_slow], near_send.at[1], near_recv.at[1], k, slow
    )

    def put_sums(n):
        a, g = project(n)
        pg_ref[parts[n], :] = g.astype(BF)
        pa_ref[parts[n], :] = a.astype(BF)
        return a

    def start_mid(*ns):
        def f(d):
            for n in ns:
                mid[d][n].start()

        return f

    def wait_mid(*ns):
        def f(d):
            for n in ns:
                mid[d][n].wait_recv()

        return f

    a_soon = put_sums(0)
    pl.when(k < groups - 1)(lambda: pl.semaphore_wait(chain, groups - 1 - k))
    for_later(start_mid(1, 0))
    near_fast.start()

    pl.when(has_slow)(halo_slow.wait_recv)
    for c in (cols, cols + 1, cols + 2):
        inputs_first(c)
    first_pair((cols - 1, cols))
    first_pair((cols + 1,))
    for c in (cols - 2, cols - 1, cols):
        second(c)
    for c in (cols - 3, cols - 2, cols - 1):
        block(c)
    a_late = put_sums(1)

    @pl.when(has_slow)
    def _():
        for_later(start_mid(2, 3))
        near_slow.start()

    pl.when(jnp.logical_not(has_slow))(lambda: for_later(start_mid(3)))

    rim_fast.wait_recv()
    near_fast.wait_recv()
    for_earlier(wait_mid(0, 1))

    def base_of(rows):
        base = st_ref[rows, :]
        for d in range(groups - 1):
            base = base + rx_ref[d, rows, :].astype(F32)
        return base

    def inputs_next(c, base, step, row):
        cov = xb_ref[:, lanes(place(c))].astype(F32)[CH:]
        for s, state in enumerate((base, base + step)):
            v = jnp.concatenate([state[row : row + CH], cov], axis=0)
            store_taps(x2_ref, v.astype(BF), 2 * (c + HALO) + s)

    def next_columns(columns, rows, step, firsts, seconds, blocks):
        base = base_of(rows)
        for c in columns:
            inputs_next(c, base, step, row_of(c) - rows.start)
        for c in firsts:
            first(c)
        for c in seconds:
            second(c)
        for c in blocks:
            block(c)
        return base

    step = jnp.concatenate([rxs_ref[at_fast, :].astype(F32), a_soon], axis=0)
    base = next_columns(
        range(-HALO, soon), pl.ds(0, rim + early), step, range(-2, soon - 1), range(-1, soon - 2), range(soon - 3)
    )
    base_ref[parts[0], :] = base[rim:]

    for_earlier(wait_mid(3))
    base_ref[parts[1], :] = next_columns(
        range(soon, cols), own_late, a_late, range(soon - 1, cols - 1), range(soon - 2, cols - 2), range(soon - 3, soon)
    )

    def lasts(d):
        return [
            remote(
                pd_ref.at[at],
                rxf_ref.at[d - 1, at],
                last_send.at[d - 1, n],
                last_recv.at[d - 1, n],
                k + d,
                t,
            )
            for n, at in enumerate(parts)
        ]

    last = {d: lasts(d) for d in range(1, groups)}

    def put_last(n):
        a, g = project(n)
        pd_ref[parts[n], :] = (g - pg_ref[parts[n], :].astype(F32)).astype(BF)
        for_later(lambda d: last[d][n].start())
        return a, g

    a_soon, g_soon = put_last(0)

    @pl.when(has_slow)
    def _():
        rim_slow.wait_recv()
        near_slow.wait_recv()
        for_earlier(wait_mid(2))

    next_columns(
        range(cols, cols + HALO),
        at_slow,
        rxs_ref[at_slow, :].astype(F32),
        range(cols - 1, cols + 2),
        range(cols - 2, cols + 1),
        range(soon, cols),
    )
    a_late, g_late = put_last(1)

    def all_sent(*copies):
        for c in copies:
            c.wait_send()

    all_sent(halo_fast, rim_fast, near_fast)
    for_later(lambda d: all_sent(mid[d][0], mid[d][1], mid[d][3]))

    @pl.when(has_slow)
    def _():
        all_sent(halo_slow, rim_slow, near_slow)
        for_later(lambda d: all_sent(mid[d][2]))

    def got(d):
        for c in last[d]:
            c.wait_recv()

    for_earlier(got)
    base = base_ref[...]
    for d in range(groups - 1):
        base = base + rxf_ref[d].astype(F32)
    sums = [
        base + jnp.concatenate(both, axis=0) for both in ((a_soon, a_late), (g_soon, g_late))
    ]

    def put_result(c, i):
        at = own_row(i)
        for s in range(2):
            out_ref[s, :, c, :] = sums[s][at : at + CH]

    either_way(put_result)

    for_later(lambda d: all_sent(*last[d]))


def solution(mesh):
    groups, tiles = mesh.shape["step"], mesh.shape["tile"]

    def local(start_state, covariates, noise, embedding, w_in, w_first, w_second, w_out):
        cols = start_state.shape[1]
        wide = cols + 2 * HALO
        own = 48
        hbm = pl.BlockSpec(memory_space=pltpu.HBM)
        dma = pltpu.SemaphoreType.DMA
        w_in = jnp.swapaxes(w_in, 1, 2).reshape(144, 128)

        def body(*refs):
            kernel(groups, tiles, *refs)

        args = [
            pltpu.with_memory_space_constraint(v, pltpu.HBM)
            for v in (start_state, covariates, noise, embedding, w_in, w_first, w_second, w_out)
        ]
        return pl.pallas_call(
            body,
            out_shape=pltpu.VMEM((2, 4, cols, ROWS), F32),
            in_specs=[hbm] * 8,
            out_specs=pl.BlockSpec(memory_space=pltpu.VMEM),
            scratch_shapes=[
                pltpu.VMEM((CH, cols, ROWS), F32),
                pltpu.VMEM((12, cols, ROWS), BF),
                pltpu.VMEM((2, CH, cols, ROWS), F32),
                pltpu.VMEM((2, 128), F32),
                pltpu.VMEM((144, 128), BF),
                pltpu.VMEM((CH, 128), BF),
                pltpu.VMEM((12, cols, ROWS), F32),
                pltpu.VMEM((own + 32, ROWS), F32),
                pltpu.VMEM((own, ROWS), F32),
                pltpu.VMEM((16, wide * ROWS), BF),
                pltpu.VMEM((48, wide * ROWS), BF),
                pltpu.VMEM((48, wide * 2 * ROWS), BF),
                pltpu.VMEM((128, 144), BF),
                pltpu.VMEM((128, 1152), BF),
                pltpu.VMEM((128, 1152), BF),
                pltpu.VMEM((64, 256 * (cols - HALO)), BF),
                pltpu.VMEM((32, 256 * HALO), BF),
                pltpu.VMEM((128, 2 * ROWS), F32),
                pltpu.VMEM((2, own, ROWS), F32),
                pltpu.VMEM((384, (wide - 2) * 2 * ROWS), BF),
                pltpu.VMEM((384, (wide - 4) * 2 * ROWS), BF),
                pltpu.VMEM((256 * (cols - HALO), ROWS), BF),
                pltpu.VMEM((256 * HALO, ROWS), BF),
                pltpu.VMEM((own, ROWS), BF),
                pltpu.VMEM((own, ROWS), BF),
                pltpu.VMEM((own, ROWS), BF),
                pltpu.VMEM((groups - 1, own + 32, ROWS), BF),
                pltpu.VMEM((own + 32, ROWS), BF),
                pltpu.VMEM((groups - 1, own, ROWS), BF),
                dma((5,)),
                dma(()),
                dma((2,)),
                dma((2,)),
                dma((2,)),
                dma((2,)),
                dma((2,)),
                dma((2,)),
                dma((2,)),
                dma((groups - 1, 4)),
                dma((groups - 1, 4)),
                dma((groups - 1, 2)),
                dma((groups - 1, 2)),
                pltpu.SemaphoreType.REGULAR,
            ],
            compiler_params=pltpu.CompilerParams(
                collective_id=0, has_side_effects=True, vmem_limit_bytes=40 << 20
            ),
        )(*args)

    in_specs = (
        P(None, "tile", None),
        P(None, "tile", None),
        P("step", None, "tile", None),
        P("step", None),
        P(),
        P(),
        P(),
        P(),
    )
    out_specs = P("step", None, "tile", None)
    return jax.shard_map(local, mesh=mesh, in_specs=in_specs, out_specs=out_specs, check_vma=False)
```

```python
import jax
import jax.numpy as jnp
from jax import lax
from jax.experimental import pallas as pl
from jax.experimental.pallas import tpu as pltpu
from jax.sharding import PartitionSpec as P

STEPS = 8
SWEEPS = 2
CH = 4
HALO = 3
ROWS = 128
BF = jnp.bfloat16
F32 = jnp.float32
MESH = pl.DeviceIdType.MESH


def silu_of_half(h):
    return h * jnp.tanh(h) + h


def kernel(
    groups,
    tiles,
    start_hbm,
    cov_hbm,
    noise_hbm,
    embed_hbm,
    win_hbm,
    wfirst_hbm,
    wsecond_hbm,
    wout_hbm,
    out_ref,
    start_ref,
    cov_ref,
    noise_ref,
    embed_ref,
    win_ref,
    wout_ref,
    covf_ref,
    st_ref,
    base_ref,
    xb_ref,
    x1_ref,
    x2_ref,
    w1_ref,
    w2_ref,
    w3_ref,
    wo0_ref,
    wo1_ref,
    eb_ref,
    nz_ref,
    fh_ref,
    sh_ref,
    bo0_ref,
    bo1_ref,
    pa_ref,
    pg_ref,
    pd_ref,
    rx_ref,
    rxs_ref,
    rxf_ref,
    in_sem,
    win_sem,
    w_sem,
    halo_send,
    halo_recv,
    rim_send,
    rim_recv,
    near_send,
    near_recv,
    mid_send,
    mid_recv,
    last_send,
    last_recv,
    up,
    down,
):
    k = lax.axis_index("step")
    t = lax.axis_index("tile")
    cols = start_ref.shape[1]
    soon = cols - HALO
    rim = 16
    early, late = 2 * rim, rim

    even = t % 2 == 0
    fast = jnp.where(even, t + 1, t - 1)
    slow = jnp.where(even, t - 1, t + 1)
    has_slow = (slow >= 0) & (slow < tiles)

    def turned(n, count):
        return jnp.where(even, count - 1 - n, n)

    def either_way(f):
        @pl.when(even)
        def _():
            for c in range(cols):
                f(c, cols - 1 - c)

        @pl.when(jnp.logical_not(even))
        def _():
            for c in range(cols):
                f(c, c)

    get_start, get_cov, get_embed, get_noise, get_wout = [
        pltpu.make_async_copy(src, dst, in_sem.at[n])
        for n, (src, dst) in enumerate(
            (
                (start_hbm, start_ref),
                (cov_hbm, cov_ref),
                (embed_hbm, embed_ref),
                (noise_hbm, noise_ref),
                (wout_hbm, wout_ref),
            )
        )
    ]
    get_win = [
        pltpu.make_async_copy(
            win_hbm.at[pl.ds(a * 48, 48)],
            win_ref.at[pl.ds(pl.multiple_of(turned(a, 3) * 48, 48), 48)],
            win_sem,
        )
        for a in range(3)
    ]
    weights = []
    for n, (src, dst) in enumerate(((wfirst_hbm, w2_ref), (wsecond_hbm, w3_ref))):
        weights.append(
            [
                pltpu.make_async_copy(
                    src.at[3 * a + b],
                    dst.at[:, pl.ds(pl.multiple_of((3 * turned(a, 3) + b) * 128, 128), 128)],
                    w_sem.at[n],
                )
                for a in range(3)
                for b in range(3)
            ]
        )

    for ref in (st_ref, xb_ref, rx_ref, rxs_ref, rxf_ref):
        ref[...] = jnp.zeros_like(ref)

    barrier = pltpu.get_barrier_semaphore()

    def signal(sem, step, tile):
        pl.semaphore_signal(sem, inc=1, device_id=(step, tile), device_id_type=MESH)

    pl.when(has_slow)(lambda: signal(barrier, k, slow))
    pl.when(k > 0)(lambda: signal(barrier, k - 1, t))
    pl.when(k < groups - 1)(lambda: signal(barrier, k + 1, t))
    signal(barrier, k, fast)

    for c in (get_cov, get_start, *get_win, get_embed, *weights[0], *weights[1], get_noise, get_wout):
        c.start()

    def lanes(n, width=1):
        return pl.ds(n * ROWS, width * ROWS)

    def place(i):
        if i < 0:
            return -1 - i
        if i >= cols:
            return HALO + cols + HALO - 1 - (i - cols)
        return HALO + i

    def row_of(i):
        if i < 0:
            return CH * (-1 - i)
        if i >= cols:
            return rim + early + late + CH * (HALO - 1 - (i - cols))
        return rim + own_row(i)

    def own_row(i):
        return CH * i if i < soon else early + CH * (i - soon)

    get_cov.wait()
    covf_ref[...] = cov_ref[...].astype(F32)
    get_start.wait()

    def put_inputs(c, i):
        x = jnp.concatenate([start_ref[:, c, :], covf_ref[:, c, :]], axis=0)
        xb_ref[:, lanes(place(i))] = x.astype(BF)

    either_way(put_inputs)

    def one(p):
        return p.astype(jnp.int32)

    pl.semaphore_wait(barrier, 1 + one(has_slow) + one(k > 0) + one(k < groups - 1))

    def remote(src, dst, send, recv, step, tile):
        return pltpu.make_async_remote_copy(
            src_ref=src,
            dst_ref=dst,
            send_sem=send,
            recv_sem=recv,
            device_id=(step, tile),
            device_id_type=MESH,
        )

    def for_later(f):
        def at(d):
            if d < groups:

                @pl.when(k + d < groups)
                def _():
                    f(d)
                    at(d + 1)

        at(1)

    def for_earlier(f):
        def at(d):
            if d < groups:

                @pl.when(k >= d)
                def _():
                    f(d)
                    at(d + 1)

        at(1)

    def to_sides(ref, parts, send, recv):
        at_fast, own_fast, own_slow, at_slow = parts
        return (
            remote(ref.at[own_fast], ref.at[at_fast], send.at[0], recv.at[0], k, fast),
            remote(ref.at[own_slow], ref.at[at_slow], send.at[1], recv.at[1], k, slow),
        )

    strips = [(slice(None), lanes(n, HALO)) for n in (0, HALO, cols, cols + HALO)]
    halo_fast, halo_slow = to_sides(xb_ref, strips, halo_send, halo_recv)
    pl.when(has_slow)(halo_slow.start)
    halo_fast.start()

    at_fast, own_fast = pl.ds(0, rim), pl.ds(rim, rim)
    own_soon, own_late = pl.ds(rim, early), pl.ds(rim + early, late)
    at_slow = pl.ds(rim + early + late, rim)
    facing, parts = pl.ds(0, rim), (pl.ds(0, early), pl.ds(early, late))

    def put_state(c, i):
        st_ref[row_of(i) : row_of(i) + CH, :] = start_ref[:, c, :]

    either_way(put_state)
    rim_fast, rim_slow = to_sides(st_ref, (at_fast, own_fast, own_late, at_slow), rim_send, rim_recv)
    pl.when(has_slow)(rim_slow.start)
    rim_fast.start()

    pl.when((k > 0) & (k < groups - 1))(lambda: signal(up.at[0], k + 1, t))
    pl.when(k > 0)(lambda: signal(down.at[0], k - 1, t))

    def tell_earlier():
        for n in range(1, groups - 1):

            @pl.when(k > n)
            def _():
                pl.semaphore_wait(up.at[n - 1], 1)
                if n < groups - 2:
                    pl.when(k < groups - 1)(lambda: signal(up.at[n], k + 1, t))
                signal(down.at[n], k - n - 1, t)

    pltpu.make_async_copy(win_ref, win_ref, win_sem).wait()
    w1_ref[...] = jnp.transpose(win_ref[...].astype(F32) * 0.5).astype(BF)
    get_embed.wait()
    et = 0.5 * jnp.transpose(jnp.concatenate([embed_ref[...], jnp.zeros((6, 128), F32)], axis=0))
    for s in range(2):
        eb_ref[:, pl.ds(s * ROWS, ROWS)] = jnp.broadcast_to(et[:, s : s + 1], (128, ROWS))

    lane = lax.broadcasted_iota(jnp.int32, (1, ROWS), 1)
    keep_first = (lane > 0).astype(F32).astype(BF)
    keep_last = (lane < ROWS - 1).astype(F32).astype(BF)
    slow_one = has_slow.astype(F32)
    bo_refs = (bo0_ref, bo1_ref)
    wo_refs = (wo0_ref, wo1_ref)

    def store_taps(ref, x, at):
        n = x.shape[0]
        at = pl.ds(at * ROWS, ROWS)
        ref[0:n, at] = pltpu.roll(x, 1, 1) * keep_first
        ref[n : 2 * n, at] = x
        ref[2 * n : 3 * n, at] = pltpu.roll(x, ROWS - 1, 1) * keep_last

    def store_both(ref, h, at):
        for s in range(2):
            store_taps(ref, h[:, s * ROWS : (s + 1) * ROWS], 2 * at + s)

    def taps_of(ref, at):
        return jnp.concatenate(
            [ref[:, pl.ds((at + a) * 2 * ROWS, 2 * ROWS)] for a in range(3)], axis=0
        )

    def inside(h, c):
        return h * slow_one if c >= cols else h

    def first_done(pre, c):
        h = inside(silu_of_half(pre + eb_ref[...]), c)
        store_both(fh_ref, h.astype(BF), c + 2)

    def first(c):
        first_done(jnp.dot(w1_ref[...], taps_of(x2_ref, c + 2), preferred_element_type=F32), c)

    def first_pair(pair):
        taps = jnp.concatenate(
            [
                jnp.concatenate([x1_ref[:, lanes(c + 2 + a)] for c in pair], axis=1)
                for a in range(3)
            ],
            axis=0,
        )
        pre = jnp.dot(w1_ref[...], taps, preferred_element_type=F32)
        for n, c in enumerate(pair):
            p = pre[:, n * ROWS : (n + 1) * ROWS]
            first_done(jnp.concatenate([p, p], axis=1), c)

    def second(c):
        h = jnp.dot(w2_ref[...], taps_of(fh_ref, c + 1), preferred_element_type=F32)
        store_both(sh_ref, inside(silu_of_half(h), c).astype(BF), c + 1)

    def block(c):
        h = silu_of_half(jnp.dot(w3_ref[...], taps_of(sh_ref, c), preferred_element_type=F32))
        h = (h + fh_ref[128:256, pl.ds((c + 2) * 2 * ROWS, 2 * ROWS)].astype(F32)).astype(BF)
        n, j = (0, c) if c < soon else (1, c - soon)
        count = (soon, HALO)[n]
        for s in range(2):
            at = (s * count + j) * 128
            bo_refs[n][at : at + 128, :] = h[:, s * ROWS : (s + 1) * ROWS]

    def project(n):
        p = jnp.dot(wo_refs[n][...], bo_refs[n][...], preferred_element_type=F32)
        size = (early, late)[n]
        return p[:size] + nz_ref[0, parts[n], :], p[size:] + nz_ref[1, parts[n], :]

    def inputs_first(c):
        x = xb_ref[:, lanes(place(c))]
        store_taps(x1_ref, x, c + HALO)

    for c in range(cols):
        inputs_first(c)
    for c in range(1, cols - 1, 2):
        first_pair((c, c + 1))
    pltpu.make_async_copy(w2_ref, w2_ref, w_sem.at[0]).wait()
    w2_ref[...] = w2_ref[...] * BF(0.5)
    tell_earlier()
    for c in range(2, cols - 2):
        second(c)
    pltpu.make_async_copy(w3_ref, w3_ref, w_sem.at[1]).wait()
    w3_ref[...] = w3_ref[...] * BF(0.5)
    for c in range(3, cols - 3):
        block(c)
    get_wout.wait()
    wo = wout_ref[...].astype(F32) * (1.0 / STEPS)
    none = jnp.zeros((CH, 128), F32)
    for n, (count, size) in enumerate(((soon, early), (HALO, late))):
        lhs = []
        for sums in range(2):
            for j in range(count):
                blocks = [wo if s <= sums and i == j else none for s in range(2) for i in range(count)]
                lhs.append(jnp.concatenate(blocks, axis=1))
            lhs.append(jnp.zeros((size - CH * count, 2 * 128 * count), F32))
        wo_refs[n][...] = jnp.concatenate(lhs, axis=0).astype(BF)
    get_noise.wait()
    nz_ref[...] = jnp.zeros_like(nz_ref)

    def put_noise(c, i):
        at = own_row(i)
        n0 = 0.3 * noise_ref[0, :, c, :]
        nz_ref[0, at : at + CH, :] = n0
        nz_ref[1, at : at + CH, :] = n0 + 0.3 * noise_ref[1, :, c, :]

    either_way(put_noise)

    halo_fast.wait_recv()
    for c in (-1, -2, -3):
        inputs_first(c)
    first_pair((0, -1))
    first_pair((-2,))
    for c in (1, 0, -1):
        second(c)
    for c in (2, 1, 0):
        block(c)

    def mids(d):
        def send(n, src, dst, tile):
            return remote(
                pg_ref.at[src],
                rx_ref.at[d - 1, dst],
                mid_send.at[d - 1, n],
                mid_recv.at[d - 1, n],
                k + d,
                tile,
            )

        return (
            send(0, facing, at_fast, fast),
            send(1, parts[0], own_soon, t),
            send(2, parts[1], at_slow, slow),
            send(3, parts[1], own_late, t),
        )

    mid = {d: mids(d) for d in range(1, groups)}
    near_fast = remote(
        pa_ref.at[facing], rxs_ref.at[at_fast], near_send.at[0], near_recv.at[0], k, fast
    )
    near_slow = remote(
        pa_ref.at[parts[1]], rxs_ref.at[at_slow], near_send.at[1], near_recv.at[1], k, slow
    )

    def put_sums(n):
        a, g = project(n)
        pg_ref[parts[n], :] = g.astype(BF)
        pa_ref[parts[n], :] = a.astype(BF)
        return a

    def wait_mid(*ns):
        def f(d):
            for n in ns:
                mid[d][n].wait_recv()

        return f

    def start_soon(d):
        pl.semaphore_wait(down.at[d - 1], 1)
        mid[d][1].start()
        mid[d][0].start()

    patient = groups - 1
    a_soon = put_sums(0)
    near_fast.start()
    for_later(lambda d: start_soon(d) if d < patient else None)

    pl.when(has_slow)(halo_slow.wait_recv)
    for c in (cols, cols + 1, cols + 2):
        inputs_first(c)
    first_pair((cols - 1, cols))
    first_pair((cols + 1,))
    for c in (cols - 2, cols - 1, cols):
        second(c)
    for c in (cols - 3, cols - 2, cols - 1):
        block(c)
    a_late = put_sums(1)

    def start_late(d):
        if d == patient:
            start_soon(d)
        pl.when(has_slow)(mid[d][2].start)
        mid[d][3].start()

    pl.when(has_slow)(near_slow.start)
    for_later(start_late)

    rim_fast.wait_recv()
    near_fast.wait_recv()
    for_earlier(wait_mid(0, 1))

    def base_of(rows):
        base = st_ref[rows, :]
        for d in range(groups - 1):
            base = base + rx_ref[d, rows, :].astype(F32)
        return base

    def inputs_next(c, base, step, row):
        cov = xb_ref[:, lanes(place(c))].astype(F32)[CH:]
        for s, state in enumerate((base, base + step)):
            v = jnp.concatenate([state[row : row + CH], cov], axis=0)
            store_taps(x2_ref, v.astype(BF), 2 * (c + HALO) + s)

    def next_columns(columns, rows, step, firsts, seconds, blocks):
        base = base_of(rows)
        for c in columns:
            inputs_next(c, base, step, row_of(c) - rows.start)
        for c in firsts:
            first(c)
        for c in seconds:
            second(c)
        for c in blocks:
            block(c)
        return base

    step = jnp.concatenate([rxs_ref[at_fast, :].astype(F32), a_soon], axis=0)
    base = next_columns(
        range(-HALO, soon), pl.ds(0, rim + early), step, range(-2, soon - 1), range(-1, soon - 2), range(soon - 3)
    )
    base_ref[parts[0], :] = base[rim:]

    for_earlier(wait_mid(3))
    base_ref[parts[1], :] = next_columns(
        range(soon, cols), own_late, a_late, range(soon - 1, cols - 1), range(soon - 2, cols - 2), range(soon - 3, soon)
    )

    def lasts(d):
        return [
            remote(
                pd_ref.at[at],
                rxf_ref.at[d - 1, at],
                last_send.at[d - 1, n],
                last_recv.at[d - 1, n],
                k + d,
                t,
            )
            for n, at in enumerate(parts)
        ]

    last = {d: lasts(d) for d in range(1, groups)}

    def put_last(n):
        a, g = project(n)
        pd_ref[parts[n], :] = (g - pg_ref[parts[n], :].astype(F32)).astype(BF)
        for_later(lambda d: last[d][n].start())
        return a, g

    a_soon, g_soon = put_last(0)

    @pl.when(has_slow)
    def _():
        rim_slow.wait_recv()
        near_slow.wait_recv()
        for_earlier(wait_mid(2))

    next_columns(
        range(cols, cols + HALO),
        at_slow,
        rxs_ref[at_slow, :].astype(F32),
        range(cols - 1, cols + 2),
        range(cols - 2, cols + 1),
        range(soon, cols),
    )
    a_late, g_late = put_last(1)

    def all_sent(*copies):
        for c in copies:
            c.wait_send()

    all_sent(halo_fast, rim_fast, near_fast)
    for_later(lambda d: all_sent(mid[d][0], mid[d][1], mid[d][3]))

    @pl.when(has_slow)
    def _():
        all_sent(halo_slow, rim_slow, near_slow)
        for_later(lambda d: all_sent(mid[d][2]))

    def got(d):
        for c in last[d]:
            c.wait_recv()

    for_earlier(got)
    base = base_ref[...]
    for d in range(groups - 1):
        base = base + rxf_ref[d].astype(F32)
    sums = [
        base + jnp.concatenate(both, axis=0) for both in ((a_soon, a_late), (g_soon, g_late))
    ]

    def put_result(c, i):
        at = own_row(i)
        for s in range(2):
            out_ref[s, :, c, :] = sums[s][at : at + CH]

    either_way(put_result)

    for_later(lambda d: all_sent(*last[d]))


def solution(mesh):
    groups, tiles = mesh.shape["step"], mesh.shape["tile"]

    def local(start_state, covariates, noise, embedding, w_in, w_first, w_second, w_out):
        cols = start_state.shape[1]
        wide = cols + 2 * HALO
        own = 48
        hbm = pl.BlockSpec(memory_space=pltpu.HBM)
        dma = pltpu.SemaphoreType.DMA
        w_in = jnp.swapaxes(w_in, 1, 2).reshape(144, 128)

        def body(*refs):
            kernel(groups, tiles, *refs)

        args = [
            pltpu.with_memory_space_constraint(v, pltpu.HBM)
            for v in (start_state, covariates, noise, embedding, w_in, w_first, w_second, w_out)
        ]
        return pl.pallas_call(
            body,
            out_shape=pltpu.VMEM((2, 4, cols, ROWS), F32),
            in_specs=[hbm] * 8,
            out_specs=pl.BlockSpec(memory_space=pltpu.VMEM),
            scratch_shapes=[
                pltpu.VMEM((CH, cols, ROWS), F32),
                pltpu.VMEM((12, cols, ROWS), BF),
                pltpu.VMEM((2, CH, cols, ROWS), F32),
                pltpu.VMEM((2, 128), F32),
                pltpu.VMEM((144, 128), BF),
                pltpu.VMEM((CH, 128), BF),
                pltpu.VMEM((12, cols, ROWS), F32),
                pltpu.VMEM((own + 32, ROWS), F32),
                pltpu.VMEM((own, ROWS), F32),
                pltpu.VMEM((16, wide * ROWS), BF),
                pltpu.VMEM((48, wide * ROWS), BF),
                pltpu.VMEM((48, wide * 2 * ROWS), BF),
                pltpu.VMEM((128, 144), BF),
                pltpu.VMEM((128, 1152), BF),
                pltpu.VMEM((128, 1152), BF),
                pltpu.VMEM((64, 256 * (cols - HALO)), BF),
                pltpu.VMEM((32, 256 * HALO), BF),
                pltpu.VMEM((128, 2 * ROWS), F32),
                pltpu.VMEM((2, own, ROWS), F32),
                pltpu.VMEM((384, (wide - 2) * 2 * ROWS), BF),
                pltpu.VMEM((384, (wide - 4) * 2 * ROWS), BF),
                pltpu.VMEM((256 * (cols - HALO), ROWS), BF),
                pltpu.VMEM((256 * HALO, ROWS), BF),
                pltpu.VMEM((own, ROWS), BF),
                pltpu.VMEM((own, ROWS), BF),
                pltpu.VMEM((own, ROWS), BF),
                pltpu.VMEM((groups - 1, own + 32, ROWS), BF),
                pltpu.VMEM((own + 32, ROWS), BF),
                pltpu.VMEM((groups - 1, own, ROWS), BF),
                dma((5,)),
                dma(()),
                dma((2,)),
                dma((2,)),
                dma((2,)),
                dma((2,)),
                dma((2,)),
                dma((2,)),
                dma((2,)),
                dma((groups - 1, 4)),
                dma((groups - 1, 4)),
                dma((groups - 1, 2)),
                dma((groups - 1, 2)),
                pltpu.SemaphoreType.REGULAR((groups - 1,)),
                pltpu.SemaphoreType.REGULAR((groups - 1,)),
            ],
            compiler_params=pltpu.CompilerParams(
                collective_id=0, has_side_effects=True, vmem_limit_bytes=40 << 20
            ),
        )(*args)

    in_specs = (
        P(None, "tile", None),
        P(None, "tile", None),
        P("step", None, "tile", None),
        P("step", None),
        P(),
        P(),
        P(),
        P(),
    )
    out_specs = P("step", None, "tile", None)
    return jax.shard_map(local, mesh=mesh, in_specs=in_specs, out_specs=out_specs, check_vma=False)
```

```python
import jax
import jax.numpy as jnp
from jax import lax
from jax.experimental import pallas as pl
from jax.experimental.pallas import tpu as pltpu
from jax.sharding import PartitionSpec as P

STEPS = 8
SWEEPS = 2
CH = 4
HALO = 3
FAR = 2 * HALO
ROWS = 128
BF = jnp.bfloat16
F32 = jnp.float32
MESH = pl.DeviceIdType.MESH


def silu_of_half(h):
    return h * jnp.tanh(h) + h


def kernel(
    groups,
    tiles,
    start_hbm,
    cov_hbm,
    noise_hbm,
    embed_hbm,
    win_hbm,
    wfirst_hbm,
    wsecond_hbm,
    wout_hbm,
    out_ref,
    start_ref,
    cov_ref,
    noise_ref,
    embed_ref,
    win_ref,
    wout_ref,
    covf_ref,
    st_ref,
    base_ref,
    xb_ref,
    x1_ref,
    x2_ref,
    w1_ref,
    w2_ref,
    w3_ref,
    wo0_ref,
    wo1_ref,
    eb_ref,
    nz_ref,
    nzs_ref,
    fh_ref,
    sh_ref,
    bo0_ref,
    bo1_ref,
    bo2_ref,
    pa_ref,
    pg_ref,
    pd_ref,
    rx_ref,
    rxs_ref,
    rxf_ref,
    in_sem,
    win_sem,
    w_sem,
    halo_send,
    halo_recv,
    rim_send,
    rim_recv,
    noise_send,
    noise_recv,
    near_send,
    near_recv,
    mid_send,
    mid_recv,
    last_send,
    last_recv,
    down,
):
    k = lax.axis_index("step")
    t = lax.axis_index("tile")
    cols = start_ref.shape[1]
    soon = cols - HALO
    rim = 16
    early, late = 2 * rim, rim

    even = t % 2 == 0
    fast = jnp.where(even, t + 1, t - 1)
    slow = jnp.where(even, t - 1, t + 1)
    has_slow = (slow >= 0) & (slow < tiles)

    def turned(n, count):
        return jnp.where(even, count - 1 - n, n)

    def for_later(f):
        def at(d):
            if d < groups:

                @pl.when(k + d < groups)
                def _():
                    f(d)
                    at(d + 1)

        at(1)

    def for_earlier(f):
        def at(d):
            if d < groups:

                @pl.when(k >= d)
                def _():
                    f(d)
                    at(d + 1)

        at(1)

    def either_way(f):
        @pl.when(even)
        def _():
            for c in range(cols):
                f(c, cols - 1 - c)

        @pl.when(jnp.logical_not(even))
        def _():
            for c in range(cols):
                f(c, c)

    get_start, get_cov, get_embed, get_noise, get_wout = [
        pltpu.make_async_copy(src, dst, in_sem.at[n])
        for n, (src, dst) in enumerate(
            (
                (start_hbm, start_ref),
                (cov_hbm, cov_ref),
                (embed_hbm, embed_ref),
                (noise_hbm, noise_ref),
                (wout_hbm, wout_ref),
            )
        )
    ]
    get_win = [
        pltpu.make_async_copy(
            win_hbm.at[pl.ds(a * 48, 48)],
            win_ref.at[pl.ds(pl.multiple_of(turned(a, 3) * 48, 48), 48)],
            win_sem,
        )
        for a in range(3)
    ]
    weights = []
    for n, (src, dst) in enumerate(((wfirst_hbm, w2_ref), (wsecond_hbm, w3_ref))):
        weights.append(
            [
                pltpu.make_async_copy(
                    src.at[3 * a + b],
                    dst.at[:, pl.ds(pl.multiple_of((3 * turned(a, 3) + b) * 128, 128), 128)],
                    w_sem.at[n],
                )
                for a in range(3)
                for b in range(3)
            ]
        )

    for ref in (st_ref, xb_ref, nzs_ref, rx_ref, rxs_ref, rxf_ref):
        ref[...] = jnp.zeros_like(ref)

    barrier = pltpu.get_barrier_semaphore()

    def signal(sem, step, tile):
        pl.semaphore_signal(sem, inc=1, device_id=(step, tile), device_id_type=MESH)

    pl.when(has_slow)(lambda: signal(barrier, k, slow))
    signal(barrier, k, fast)
    for_later(lambda d: signal(barrier, k + d, t))

    for c in (get_cov, get_start, *get_win, get_embed, *weights[0], *weights[1], get_noise, get_wout):
        c.start()

    def lanes(n, width=1):
        return pl.ds(n * ROWS, width * ROWS)

    def place(i):
        if i < 0:
            return -1 - i
        if i >= cols:
            return HALO + cols + FAR - 1 - (i - cols)
        return HALO + i

    def row_of(i):
        if i < 0:
            return CH * (-1 - i)
        if i >= cols:
            return rim + early + late + CH * (HALO - 1 - (i - cols))
        return rim + own_row(i)

    def own_row(i):
        return CH * i if i < soon else early + CH * (i - soon)

    get_cov.wait()
    covf_ref[...] = cov_ref[...].astype(F32)
    get_start.wait()

    def put_inputs(c, i):
        x = jnp.concatenate([start_ref[:, c, :], covf_ref[:, c, :]], axis=0)
        xb_ref[:, lanes(place(i))] = x.astype(BF)

    either_way(put_inputs)

    def one(p):
        return p.astype(jnp.int32)

    pl.semaphore_wait(barrier, 1 + one(has_slow) + k)

    def remote(src, dst, send, recv, step, tile):
        return pltpu.make_async_remote_copy(
            src_ref=src,
            dst_ref=dst,
            send_sem=send,
            recv_sem=recv,
            device_id=(step, tile),
            device_id_type=MESH,
        )

    def to_sides(ref, parts, send, recv):
        at_fast, own_fast, own_slow, at_slow = parts
        return (
            remote(ref.at[own_fast], ref.at[at_fast], send.at[0], recv.at[0], k, fast),
            remote(ref.at[own_slow], ref.at[at_slow], send.at[1], recv.at[1], k, slow),
        )

    strips = [
        (slice(None), lanes(n, width))
        for n, width in ((0, HALO), (HALO, HALO), (HALO + cols - FAR, FAR), (HALO + cols, FAR))
    ]
    halo_fast, halo_slow = to_sides(xb_ref, strips, halo_send, halo_recv)
    pl.when(has_slow)(halo_slow.start)
    halo_fast.start()

    at_fast, own_fast = pl.ds(0, rim), pl.ds(rim, rim)
    own_soon, own_late = pl.ds(rim, early), pl.ds(rim + early, late)
    at_slow = pl.ds(rim + early + late, rim)
    facing, parts = pl.ds(0, rim), (pl.ds(0, early), pl.ds(early, late), pl.ds(early + late, late))
    late_out, own_late_out = pl.ds(early, 2 * late), pl.ds(rim + early, 2 * late)

    def put_state(c, i):
        st_ref[row_of(i) : row_of(i) + CH, :] = start_ref[:, c, :]

    either_way(put_state)
    rim_fast, rim_slow = to_sides(st_ref, (at_fast, own_fast, own_late, at_slow), rim_send, rim_recv)
    pl.when(has_slow)(rim_slow.start)
    rim_fast.start()

    for_earlier(lambda d: signal(down.at[d - 1], k - d, t))

    pltpu.make_async_copy(win_ref, win_ref, win_sem).wait()
    w1_ref[...] = jnp.transpose(win_ref[...].astype(F32) * 0.5).astype(BF)
    get_embed.wait()
    et = 0.5 * jnp.transpose(jnp.concatenate([embed_ref[...], jnp.zeros((6, 128), F32)], axis=0))
    for s in range(2):
        eb_ref[:, pl.ds(s * ROWS, ROWS)] = jnp.broadcast_to(et[:, s : s + 1], (128, ROWS))

    lane = lax.broadcasted_iota(jnp.int32, (1, ROWS), 1)
    keep_first = (lane > 0).astype(F32).astype(BF)
    keep_last = (lane < ROWS - 1).astype(F32).astype(BF)
    slow_one = has_slow.astype(F32)
    bo_refs = (bo0_ref, bo1_ref, bo2_ref)
    wo_refs = (wo0_ref, wo1_ref, wo1_ref)

    def store_taps(ref, x, at):
        n = x.shape[0]
        at = pl.ds(at * ROWS, ROWS)
        ref[0:n, at] = pltpu.roll(x, 1, 1) * keep_first
        ref[n : 2 * n, at] = x
        ref[2 * n : 3 * n, at] = pltpu.roll(x, ROWS - 1, 1) * keep_last

    def store_both(ref, h, at):
        for s in range(2):
            store_taps(ref, h[:, s * ROWS : (s + 1) * ROWS], 2 * at + s)

    def taps_of(ref, at):
        return jnp.concatenate(
            [ref[:, pl.ds((at + a) * 2 * ROWS, 2 * ROWS)] for a in range(3)], axis=0
        )

    def inside(h, c):
        return h * slow_one if c >= cols else h

    def first_done(pre, c):
        h = inside(silu_of_half(pre + eb_ref[...]), c)
        store_both(fh_ref, h.astype(BF), c + 2)

    def first(c):
        first_done(jnp.dot(w1_ref[...], taps_of(x2_ref, c + 2), preferred_element_type=F32), c)

    def first_pair(pair):
        taps = jnp.concatenate(
            [
                jnp.concatenate([x1_ref[:, lanes(c + 2 + a)] for c in pair], axis=1)
                for a in range(3)
            ],
            axis=0,
        )
        pre = jnp.dot(w1_ref[...], taps, preferred_element_type=F32)
        for n, c in enumerate(pair):
            p = pre[:, n * ROWS : (n + 1) * ROWS]
            first_done(jnp.concatenate([p, p], axis=1), c)

    def second(c):
        h = jnp.dot(w2_ref[...], taps_of(fh_ref, c + 1), preferred_element_type=F32)
        store_both(sh_ref, inside(silu_of_half(h), c).astype(BF), c + 1)

    def block(c):
        h = silu_of_half(jnp.dot(w3_ref[...], taps_of(sh_ref, c), preferred_element_type=F32))
        h = (h + fh_ref[128:256, pl.ds((c + 2) * 2 * ROWS, 2 * ROWS)].astype(F32)).astype(BF)
        n, j = (0, c) if c < soon else (1, c - soon) if c < cols else (2, cols + HALO - 1 - c)
        count = (soon, HALO, HALO)[n]
        for s in range(2):
            at = (s * count + j) * 128
            bo_refs[n][at : at + 128, :] = h[:, s * ROWS : (s + 1) * ROWS]

    def project(n):
        p = jnp.dot(wo_refs[n][...], bo_refs[n][...], preferred_element_type=F32)
        size = (early, late, late)[n]
        noises = (nzs_ref[0], nzs_ref[1]) if n == 2 else (nz_ref[0, parts[n], :], nz_ref[1, parts[n], :])
        return p[:size] + noises[0], p[size:] + noises[1]

    def inputs_first(c):
        x = xb_ref[:, lanes(place(c))]
        store_taps(x1_ref, x, c + HALO)

    for c in range(cols):
        inputs_first(c)
    for c in range(1, cols - 1, 2):
        first_pair((c, c + 1))
    pltpu.make_async_copy(w2_ref, w2_ref, w_sem.at[0]).wait()
    w2_ref[...] = w2_ref[...] * BF(0.5)
    for c in range(2, cols - 2):
        second(c)
    pltpu.make_async_copy(w3_ref, w3_ref, w_sem.at[1]).wait()
    w3_ref[...] = w3_ref[...] * BF(0.5)
    for c in range(3, cols - 3):
        block(c)
    get_wout.wait()
    wo = wout_ref[...].astype(F32) * (1.0 / STEPS)
    none = jnp.zeros((CH, 128), F32)
    for n, (count, size) in enumerate(((soon, early), (HALO, late))):
        lhs = []
        for sums in range(2):
            for j in range(count):
                blocks = [wo if s <= sums and i == j else none for s in range(2) for i in range(count)]
                lhs.append(jnp.concatenate(blocks, axis=1))
            lhs.append(jnp.zeros((size - CH * count, 2 * 128 * count), F32))
        wo_refs[n][...] = jnp.concatenate(lhs, axis=0).astype(BF)
    get_noise.wait()
    nz_ref[...] = jnp.zeros_like(nz_ref)

    def put_noise(c, i):
        at = own_row(i)
        n0 = 0.3 * noise_ref[0, :, c, :]
        nz_ref[0, at : at + CH, :] = n0
        nz_ref[1, at : at + CH, :] = n0 + 0.3 * noise_ref[1, :, c, :]

    either_way(put_noise)
    noise_slow = remote(nz_ref.at[:, parts[1]], nzs_ref, noise_send, noise_recv, k, slow)
    pl.when(has_slow)(noise_slow.start)

    halo_fast.wait_recv()
    for c in (-1, -2, -3):
        inputs_first(c)
    first_pair((0, -1))
    first_pair((-2,))
    for c in (1, 0, -1):
        second(c)
    for c in (2, 1, 0):
        block(c)

    def mids(d):
        def send(n, src, dst, tile):
            return remote(
                pg_ref.at[src],
                rx_ref.at[d - 1, dst],
                mid_send.at[d - 1, n],
                mid_recv.at[d - 1, n],
                k + d,
                tile,
            )

        return (
            send(0, facing, at_fast, fast),
            send(1, parts[0], own_soon, t),
            send(2, late_out, own_late_out, t),
        )

    mid = {d: mids(d) for d in range(1, groups)}
    near_fast = remote(
        pa_ref, rxs_ref, near_send, near_recv, k, fast
    )

    def put_sums(n):
        a, g = project(n)
        pg_ref[parts[n], :] = g.astype(BF)
        if n == 0:
            pa_ref[...] = a[:rim].astype(BF)
        return a

    def wait_mid(*ns):
        def f(d):
            for n in ns:
                mid[d][n].wait_recv()

        return f

    def start_soon(d):
        pl.semaphore_wait(down.at[d - 1], 1)
        mid[d][1].start()
        mid[d][0].start()

    a_soon = put_sums(0)
    near_fast.start()
    for_later(start_soon)

    pl.when(has_slow)(halo_slow.wait_recv)
    for c in range(cols, cols + FAR):
        inputs_first(c)
    for c in range(cols - 1, cols + 5, 2):
        first_pair((c, c + 1))
    for c in range(cols - 2, cols + 4):
        second(c)
    for c in range(cols - 3, cols + 3):
        block(c)
    a_late = put_sums(1)
    pl.when(has_slow)(noise_slow.wait_recv)
    a_out = put_sums(2)

    for_later(lambda d: mid[d][2].start())

    rim_fast.wait_recv()
    near_fast.wait_recv()
    for_earlier(wait_mid(0, 1))

    def base_of(rows):
        base = st_ref[rows, :]
        for d in range(groups - 1):
            base = base + rx_ref[d, rows, :].astype(F32)
        return base

    def inputs_next(c, base, step, row):
        cov = xb_ref[:, lanes(place(c))].astype(F32)[CH:]
        for s, state in enumerate((base, base + step)):
            v = jnp.concatenate([state[row : row + CH], cov], axis=0)
            if c >= cols:
                v = v * slow_one
            store_taps(x2_ref, v.astype(BF), 2 * (c + HALO) + s)

    def next_columns(columns, rows, step, firsts, seconds, blocks):
        base = base_of(rows)
        for c in columns:
            inputs_next(c, base, step, row_of(c) - rows.start)
        for c in firsts:
            first(c)
        for c in seconds:
            second(c)
        for c in blocks:
            block(c)
        return base

    step = jnp.concatenate([rxs_ref[...].astype(F32), a_soon], axis=0)
    base = next_columns(
        range(-HALO, soon), pl.ds(0, rim + early), step, range(-2, soon - 1), range(-1, soon - 2), range(soon - 3)
    )
    base_ref[parts[0], :] = base[rim:]

    pl.when(has_slow)(rim_slow.wait_recv)
    for_earlier(wait_mid(2))
    base = next_columns(
        range(soon, cols + HALO),
        own_late_out,
        jnp.concatenate([a_late, a_out], axis=0),
        range(soon - 1, cols + 2),
        range(soon - 2, cols + 1),
        range(soon - 3, cols),
    )
    base_ref[parts[1], :] = base[:late]

    last = {
        d: remote(pd_ref, rxf_ref.at[d - 1], last_send.at[d - 1], last_recv.at[d - 1], k + d, t)
        for d in range(1, groups)
    }
    both = [project(n) for n in range(2)]
    for n, (a, g) in enumerate(both):
        pd_ref[parts[n], :] = (g - pg_ref[parts[n], :].astype(F32)).astype(BF)
    for_later(lambda d: last[d].start())
    (a_soon, g_soon), (a_late, g_late) = both

    def all_sent(*copies):
        for c in copies:
            c.wait_send()

    all_sent(halo_fast, rim_fast, near_fast)
    for_later(lambda d: all_sent(*mid[d]))

    pl.when(has_slow)(lambda: all_sent(halo_slow, rim_slow, noise_slow))

    for_earlier(lambda d: last[d].wait_recv())
    base = base_ref[...]
    for d in range(groups - 1):
        base = base + rxf_ref[d].astype(F32)
    sums = [
        base + jnp.concatenate(both, axis=0) for both in ((a_soon, a_late), (g_soon, g_late))
    ]

    def put_result(c, i):
        at = own_row(i)
        for s in range(2):
            out_ref[s, :, c, :] = sums[s][at : at + CH]

    either_way(put_result)

    for_later(lambda d: all_sent(last[d]))


def solution(mesh):
    groups, tiles = mesh.shape["step"], mesh.shape["tile"]

    def local(start_state, covariates, noise, embedding, w_in, w_first, w_second, w_out):
        cols = start_state.shape[1]
        wide = cols + 2 * HALO
        own = 48
        hbm = pl.BlockSpec(memory_space=pltpu.HBM)
        dma = pltpu.SemaphoreType.DMA
        w_in = jnp.swapaxes(w_in, 1, 2).reshape(144, 128)

        def body(*refs):
            kernel(groups, tiles, *refs)

        args = [
            pltpu.with_memory_space_constraint(v, pltpu.HBM)
            for v in (start_state, covariates, noise, embedding, w_in, w_first, w_second, w_out)
        ]
        return pl.pallas_call(
            body,
            out_shape=pltpu.VMEM((2, 4, cols, ROWS), F32),
            in_specs=[hbm] * 8,
            out_specs=pl.BlockSpec(memory_space=pltpu.VMEM),
            scratch_shapes=[
                pltpu.VMEM((CH, cols, ROWS), F32),
                pltpu.VMEM((12, cols, ROWS), BF),
                pltpu.VMEM((2, CH, cols, ROWS), F32),
                pltpu.VMEM((2, 128), F32),
                pltpu.VMEM((144, 128), BF),
                pltpu.VMEM((CH, 128), BF),
                pltpu.VMEM((12, cols, ROWS), F32),
                pltpu.VMEM((own + 32, ROWS), F32),
                pltpu.VMEM((own, ROWS), F32),
                pltpu.VMEM((16, (wide + HALO) * ROWS), BF),
                pltpu.VMEM((48, (wide + HALO) * ROWS), BF),
                pltpu.VMEM((48, wide * 2 * ROWS), BF),
                pltpu.VMEM((128, 144), BF),
                pltpu.VMEM((128, 1152), BF),
                pltpu.VMEM((128, 1152), BF),
                pltpu.VMEM((64, 256 * (cols - HALO)), BF),
                pltpu.VMEM((32, 256 * HALO), BF),
                pltpu.VMEM((128, 2 * ROWS), F32),
                pltpu.VMEM((2, own, ROWS), F32),
                pltpu.VMEM((2, 16, ROWS), F32),
                pltpu.VMEM((384, (wide + 1) * 2 * ROWS), BF),
                pltpu.VMEM((384, (wide - 1) * 2 * ROWS), BF),
                pltpu.VMEM((256 * (cols - HALO), ROWS), BF),
                pltpu.VMEM((256 * HALO, ROWS), BF),
                pltpu.VMEM((256 * HALO, ROWS), BF),
                pltpu.VMEM((16, ROWS), BF),
                pltpu.VMEM((own + 16, ROWS), BF),
                pltpu.VMEM((own, ROWS), BF),
                pltpu.VMEM((groups - 1, own + 32, ROWS), BF),
                pltpu.VMEM((16, ROWS), BF),
                pltpu.VMEM((groups - 1, own, ROWS), BF),
                dma((5,)),
                dma(()),
                dma((2,)),
                dma((2,)),
                dma((2,)),
                dma((2,)),
                dma((2,)),
                dma(()),
                dma(()),
                dma(()),
                dma(()),
                dma((groups - 1, 3)),
                dma((groups - 1, 3)),
                dma((groups - 1,)),
                dma((groups - 1,)),
                pltpu.SemaphoreType.REGULAR((groups - 1,)),
            ],
            compiler_params=pltpu.CompilerParams(
                collective_id=0, has_side_effects=True, vmem_limit_bytes=40 << 20
            ),
        )(*args)

    in_specs = (
        P(None, "tile", None),
        P(None, "tile", None),
        P("step", None, "tile", None),
        P("step", None),
        P(),
        P(),
        P(),
        P(),
    )
    out_specs = P("step", None, "tile", None)
    return jax.shard_map(local, mesh=mesh, in_specs=in_specs, out_specs=out_specs, check_vma=False)
```

```python
import jax
import jax.numpy as jnp
from jax import lax
from jax.experimental import pallas as pl
from jax.experimental.pallas import tpu as pltpu
from jax.sharding import PartitionSpec as P

STEPS = 8
SWEEPS = 2
CH = 4
HALO = 3
FAR = 2 * HALO
ROWS = 128
BF = jnp.bfloat16
F32 = jnp.float32
MESH = pl.DeviceIdType.MESH


def silu_of_half(h):
    return h * jnp.tanh(h) + h


def kernel(
    groups,
    tiles,
    start_hbm,
    cov_hbm,
    noise_hbm,
    embed_hbm,
    win_hbm,
    wfirst_hbm,
    wsecond_hbm,
    wout_hbm,
    out_ref,
    start_ref,
    cov_ref,
    noise_ref,
    embed_ref,
    win_ref,
    wout_ref,
    covf_ref,
    st_ref,
    base_ref,
    xb_ref,
    x1_ref,
    x2_ref,
    w1_ref,
    w2_ref,
    w3_ref,
    wo0_ref,
    wo1_ref,
    eb_ref,
    nz_ref,
    nzb_ref,
    nzs_ref,
    fh_ref,
    sh_ref,
    bo0_ref,
    bo1_ref,
    bo2_ref,
    pa_ref,
    pg_ref,
    pd_ref,
    rx_ref,
    rxs_ref,
    rxf_ref,
    in_sem,
    win_sem,
    w_sem,
    halo_send,
    halo_recv,
    rim_send,
    rim_recv,
    noise_send,
    noise_recv,
    near_send,
    near_recv,
    mid_send,
    mid_recv,
    last_send,
    last_recv,
    down,
):
    k = lax.axis_index("step")
    t = lax.axis_index("tile")
    cols = start_ref.shape[1]
    soon = cols - HALO
    rim = 16
    early, late = 2 * rim, rim

    even = t % 2 == 0
    fast = jnp.where(even, t + 1, t - 1)
    slow = jnp.where(even, t - 1, t + 1)
    has_slow = (slow >= 0) & (slow < tiles)

    def turned(n, count):
        return jnp.where(even, count - 1 - n, n)

    def for_later(f):
        def at(d):
            if d < groups:

                @pl.when(k + d < groups)
                def _():
                    f(d)
                    at(d + 1)

        at(1)

    def for_earlier(f):
        def at(d):
            if d < groups:

                @pl.when(k >= d)
                def _():
                    f(d)
                    at(d + 1)

        at(1)

    def either_way(f):
        @pl.when(even)
        def _():
            for c in range(cols):
                f(c, cols - 1 - c)

        @pl.when(jnp.logical_not(even))
        def _():
            for c in range(cols):
                f(c, c)

    get_start, get_cov, get_embed, get_noise, get_wout = [
        pltpu.make_async_copy(src, dst, in_sem.at[n])
        for n, (src, dst) in enumerate(
            (
                (start_hbm, start_ref),
                (cov_hbm, cov_ref),
                (embed_hbm, embed_ref),
                (noise_hbm, noise_ref),
                (wout_hbm, wout_ref),
            )
        )
    ]
    get_win = [
        pltpu.make_async_copy(
            win_hbm.at[pl.ds(a * 48, 48)],
            win_ref.at[pl.ds(pl.multiple_of(turned(a, 3) * 48, 48), 48)],
            win_sem,
        )
        for a in range(3)
    ]
    weights = []
    for n, (src, dst) in enumerate(((wfirst_hbm, w2_ref), (wsecond_hbm, w3_ref))):
        weights.append(
            [
                pltpu.make_async_copy(
                    src.at[3 * a + b],
                    dst.at[:, pl.ds(pl.multiple_of((3 * turned(a, 3) + b) * 128, 128), 128)],
                    w_sem.at[n],
                )
                for a in range(3)
                for b in range(3)
            ]
        )

    for ref in (st_ref, xb_ref, nzs_ref, rx_ref, rxs_ref, rxf_ref):
        ref[...] = jnp.zeros_like(ref)

    barrier = pltpu.get_barrier_semaphore()

    def signal(sem, step, tile):
        pl.semaphore_signal(sem, inc=1, device_id=(step, tile), device_id_type=MESH)

    pl.when(has_slow)(lambda: signal(barrier, k, slow))
    signal(barrier, k, fast)
    for_later(lambda d: signal(barrier, k + d, t))

    for c in (get_cov, get_start, get_noise, *get_win, get_embed, *weights[0], *weights[1], get_wout):
        c.start()

    def lanes(n, width=1):
        return pl.ds(n * ROWS, width * ROWS)

    def place(i):
        if i < 0:
            return -1 - i
        if i >= cols:
            return HALO + cols + FAR - 1 - (i - cols)
        return HALO + i

    def row_of(i):
        if i < 0:
            return CH * (-1 - i)
        if i >= cols:
            return rim + early + late + CH * (HALO - 1 - (i - cols))
        return rim + own_row(i)

    def own_row(i):
        return CH * i if i < soon else early + CH * (i - soon)

    at_fast, own_fast = pl.ds(0, rim), pl.ds(rim, rim)
    own_soon, own_late = pl.ds(rim, early), pl.ds(rim + early, late)
    at_slow = pl.ds(rim + early + late, rim)
    facing, parts = pl.ds(0, rim), (pl.ds(0, early), pl.ds(early, late), pl.ds(early + late, late))
    late_out, own_late_out = pl.ds(early, 2 * late), pl.ds(rim + early, 2 * late)

    get_cov.wait()
    covf_ref[...] = cov_ref[...].astype(F32)
    get_start.wait()

    def put_inputs(c, i):
        x = jnp.concatenate([start_ref[:, c, :], covf_ref[:, c, :]], axis=0)
        xb_ref[:, lanes(place(i))] = x.astype(BF)

    either_way(put_inputs)
    get_noise.wait()
    nz_ref[...] = jnp.zeros_like(nz_ref)

    def put_noise(c, i):
        at = own_row(i)
        n0 = 0.3 * noise_ref[0, :, c, :]
        nz_ref[0, at : at + CH, :] = n0
        nz_ref[1, at : at + CH, :] = n0 + 0.3 * noise_ref[1, :, c, :]

    either_way(put_noise)
    nzb_ref[...] = nz_ref[:, parts[1], :].astype(BF)

    def one(p):
        return p.astype(jnp.int32)

    pl.semaphore_wait(barrier, 1 + one(has_slow) + k)

    def remote(src, dst, send, recv, step, tile):
        return pltpu.make_async_remote_copy(
            src_ref=src,
            dst_ref=dst,
            send_sem=send,
            recv_sem=recv,
            device_id=(step, tile),
            device_id_type=MESH,
        )

    def to_sides(ref, parts, send, recv):
        at_fast, own_fast, own_slow, at_slow = parts
        return (
            remote(ref.at[own_fast], ref.at[at_fast], send.at[0], recv.at[0], k, fast),
            remote(ref.at[own_slow], ref.at[at_slow], send.at[1], recv.at[1], k, slow),
        )

    strips = [
        (slice(None), lanes(n, width))
        for n, width in ((0, HALO), (HALO, HALO), (HALO + cols - FAR, FAR), (HALO + cols, FAR))
    ]
    halo_fast, halo_slow = to_sides(xb_ref, strips, halo_send, halo_recv)
    noise_slow = remote(nzb_ref, nzs_ref, noise_send, noise_recv, k, slow)

    @pl.when(has_slow)
    def _():
        halo_slow.start()
        noise_slow.start()

    halo_fast.start()

    def put_state(c, i):
        st_ref[row_of(i) : row_of(i) + CH, :] = start_ref[:, c, :]

    either_way(put_state)
    rim_fast, rim_slow = to_sides(st_ref, (at_fast, own_fast, own_late, at_slow), rim_send, rim_recv)
    pl.when(has_slow)(rim_slow.start)
    rim_fast.start()

    for_earlier(lambda d: signal(down.at[d - 1], k - d, t))

    pltpu.make_async_copy(win_ref, win_ref, win_sem).wait()
    w1_ref[...] = jnp.transpose(win_ref[...].astype(F32) * 0.5).astype(BF)
    get_embed.wait()
    et = 0.5 * jnp.transpose(jnp.concatenate([embed_ref[...], jnp.zeros((6, 128), F32)], axis=0))
    for s in range(2):
        eb_ref[:, pl.ds(s * ROWS, ROWS)] = jnp.broadcast_to(et[:, s : s + 1], (128, ROWS))

    lane = lax.broadcasted_iota(jnp.int32, (1, ROWS), 1)
    keep_first = (lane > 0).astype(F32).astype(BF)
    keep_last = (lane < ROWS - 1).astype(F32).astype(BF)
    slow_one = has_slow.astype(F32)
    bo_refs = (bo0_ref, bo1_ref, bo2_ref)
    wo_refs = (wo0_ref, wo1_ref, wo1_ref)

    def store_taps(ref, x, at):
        n = x.shape[0]
        at = pl.ds(at * ROWS, ROWS)
        ref[0:n, at] = pltpu.roll(x, 1, 1) * keep_first
        ref[n : 2 * n, at] = x
        ref[2 * n : 3 * n, at] = pltpu.roll(x, ROWS - 1, 1) * keep_last

    def store_both(ref, h, at):
        for s in range(2):
            store_taps(ref, h[:, s * ROWS : (s + 1) * ROWS], 2 * at + s)

    def taps_of(ref, at):
        return jnp.concatenate(
            [ref[:, pl.ds((at + a) * 2 * ROWS, 2 * ROWS)] for a in range(3)], axis=0
        )

    def inside(h, c):
        return h * slow_one if c >= cols else h

    def first_done(pre, c):
        h = inside(silu_of_half(pre + eb_ref[...]), c)
        store_both(fh_ref, h.astype(BF), c + 2)

    def first(c):
        first_done(jnp.dot(w1_ref[...], taps_of(x2_ref, c + 2), preferred_element_type=F32), c)

    def first_pair(pair):
        taps = jnp.concatenate(
            [
                jnp.concatenate([x1_ref[:, lanes(c + 2 + a)] for c in pair], axis=1)
                for a in range(3)
            ],
            axis=0,
        )
        pre = jnp.dot(w1_ref[...], taps, preferred_element_type=F32)
        for n, c in enumerate(pair):
            p = pre[:, n * ROWS : (n + 1) * ROWS]
            first_done(jnp.concatenate([p, p], axis=1), c)

    def second(c):
        h = jnp.dot(w2_ref[...], taps_of(fh_ref, c + 1), preferred_element_type=F32)
        store_both(sh_ref, inside(silu_of_half(h), c).astype(BF), c + 1)

    def block(c):
        h = silu_of_half(jnp.dot(w3_ref[...], taps_of(sh_ref, c), preferred_element_type=F32))
        h = (h + fh_ref[128:256, pl.ds((c + 2) * 2 * ROWS, 2 * ROWS)].astype(F32)).astype(BF)
        n, j = (0, c) if c < soon else (1, c - soon) if c < cols else (2, cols + HALO - 1 - c)
        count = (soon, HALO, HALO)[n]
        for s in range(2):
            at = (s * count + j) * 128
            bo_refs[n][at : at + 128, :] = h[:, s * ROWS : (s + 1) * ROWS]

    def project(n):
        p = jnp.dot(wo_refs[n][...], bo_refs[n][...], preferred_element_type=F32)
        size = (early, late, late)[n]
        noises = [nzs_ref[m].astype(F32) if n == 2 else nz_ref[m, parts[n], :] for m in range(2)]
        return p[:size] + noises[0], p[size:] + noises[1]

    def inputs_first(c):
        x = xb_ref[:, lanes(place(c))]
        store_taps(x1_ref, x, c + HALO)

    for c in range(cols):
        inputs_first(c)
    for c in range(1, cols - 1, 2):
        first_pair((c, c + 1))
    pltpu.make_async_copy(w2_ref, w2_ref, w_sem.at[0]).wait()
    w2_ref[...] = w2_ref[...] * BF(0.5)
    for c in range(2, cols - 2):
        second(c)
    pltpu.make_async_copy(w3_ref, w3_ref, w_sem.at[1]).wait()
    w3_ref[...] = w3_ref[...] * BF(0.5)
    for c in range(3, cols - 3):
        block(c)
    get_wout.wait()
    wo = wout_ref[...].astype(F32) * (1.0 / STEPS)
    none = jnp.zeros((CH, 128), F32)
    for n, (count, size) in enumerate(((soon, early), (HALO, late))):
        lhs = []
        for sums in range(2):
            for j in range(count):
                blocks = [wo if s <= sums and i == j else none for s in range(2) for i in range(count)]
                lhs.append(jnp.concatenate(blocks, axis=1))
            lhs.append(jnp.zeros((size - CH * count, 2 * 128 * count), F32))
        wo_refs[n][...] = jnp.concatenate(lhs, axis=0).astype(BF)

    halo_fast.wait_recv()
    for c in (-1, -2, -3):
        inputs_first(c)
    first_pair((0, -1))
    first_pair((-2,))
    for c in (1, 0, -1):
        second(c)
    for c in (2, 1, 0):
        block(c)

    def mids(d):
        def send(n, src, dst, tile):
            return remote(
                pg_ref.at[src],
                rx_ref.at[d - 1, dst],
                mid_send.at[d - 1, n],
                mid_recv.at[d - 1, n],
                k + d,
                tile,
            )

        return (
            send(0, facing, at_fast, fast),
            send(1, parts[0], own_soon, t),
            send(2, late_out, own_late_out, t),
        )

    mid = {d: mids(d) for d in range(1, groups)}
    near_fast = remote(
        pa_ref, rxs_ref, near_send, near_recv, k, fast
    )

    def put_sums(n):
        a, g = project(n)
        pg_ref[parts[n], :] = g.astype(BF)
        if n == 0:
            pa_ref[...] = a[:rim].astype(BF)
        return a

    def wait_mid(*ns):
        def f(d):
            for n in ns:
                mid[d][n].wait_recv()

        return f

    def start_soon(d):
        pl.semaphore_wait(down.at[d - 1], 1)
        mid[d][1].start()
        mid[d][0].start()

    a_soon = put_sums(0)
    near_fast.start()
    for_later(start_soon)

    @pl.when(has_slow)
    def _():
        halo_slow.wait_recv()
        noise_slow.wait_recv()

    for c in range(cols, cols + FAR):
        inputs_first(c)
    for c in range(cols - 1, cols + 5, 2):
        first_pair((c, c + 1))
    for c in range(cols - 2, cols + 4):
        second(c)
    for c in range(cols - 3, cols + 3):
        block(c)
    a_late = put_sums(1)
    a_out = put_sums(2)

    for_later(lambda d: mid[d][2].start())

    rim_fast.wait_recv()
    near_fast.wait_recv()
    for_earlier(wait_mid(0, 1))

    def base_of(rows):
        base = st_ref[rows, :]
        for d in range(groups - 1):
            base = base + rx_ref[d, rows, :].astype(F32)
        return base

    def inputs_next(c, base, step, row):
        cov = xb_ref[:, lanes(place(c))].astype(F32)[CH:]
        for s, state in enumerate((base, base + step)):
            v = jnp.concatenate([state[row : row + CH], cov], axis=0)
            if c >= cols:
                v = v * slow_one
            store_taps(x2_ref, v.astype(BF), 2 * (c + HALO) + s)

    def next_columns(columns, rows, step, firsts, seconds, blocks):
        base = base_of(rows)
        for c in columns:
            inputs_next(c, base, step, row_of(c) - rows.start)
        for c in firsts:
            first(c)
        for c in seconds:
            second(c)
        for c in blocks:
            block(c)
        return base

    step = jnp.concatenate([rxs_ref[...].astype(F32), a_soon], axis=0)
    base = next_columns(
        range(-HALO, soon), pl.ds(0, rim + early), step, range(-2, soon - 1), range(-1, soon - 2), range(soon - 3)
    )
    base_ref[parts[0], :] = base[rim:]

    pl.when(has_slow)(rim_slow.wait_recv)
    for_earlier(wait_mid(2))
    base = next_columns(
        range(soon, cols + HALO),
        own_late_out,
        jnp.concatenate([a_late, a_out], axis=0),
        range(soon - 1, cols + 2),
        range(soon - 2, cols + 1),
        range(soon - 3, cols),
    )
    base_ref[parts[1], :] = base[:late]

    last = {
        d: remote(pd_ref, rxf_ref.at[d - 1], last_send.at[d - 1], last_recv.at[d - 1], k + d, t)
        for d in range(1, groups)
    }
    both = [project(n) for n in range(2)]
    for n, (a, g) in enumerate(both):
        pd_ref[parts[n], :] = (g - pg_ref[parts[n], :].astype(F32)).astype(BF)
    for_later(lambda d: last[d].start())
    (a_soon, g_soon), (a_late, g_late) = both

    def all_sent(*copies):
        for c in copies:
            c.wait_send()

    all_sent(halo_fast, rim_fast, near_fast)
    for_later(lambda d: all_sent(*mid[d]))

    pl.when(has_slow)(lambda: all_sent(halo_slow, rim_slow, noise_slow))

    for_earlier(lambda d: last[d].wait_recv())
    base = base_ref[...]
    for d in range(groups - 1):
        base = base + rxf_ref[d].astype(F32)
    sums = [
        base + jnp.concatenate(both, axis=0) for both in ((a_soon, a_late), (g_soon, g_late))
    ]

    def put_result(c, i):
        at = own_row(i)
        for s in range(2):
            out_ref[s, :, c, :] = sums[s][at : at + CH]

    either_way(put_result)

    for_later(lambda d: all_sent(last[d]))


def solution(mesh):
    groups, tiles = mesh.shape["step"], mesh.shape["tile"]

    def local(start_state, covariates, noise, embedding, w_in, w_first, w_second, w_out):
        cols = start_state.shape[1]
        wide = cols + 2 * HALO
        own = 48
        hbm = pl.BlockSpec(memory_space=pltpu.HBM)
        dma = pltpu.SemaphoreType.DMA
        w_in = jnp.swapaxes(w_in, 1, 2).reshape(144, 128)

        def body(*refs):
            kernel(groups, tiles, *refs)

        args = [
            pltpu.with_memory_space_constraint(v, pltpu.HBM)
            for v in (start_state, covariates, noise, embedding, w_in, w_first, w_second, w_out)
        ]
        return pl.pallas_call(
            body,
            out_shape=pltpu.VMEM((2, 4, cols, ROWS), F32),
            in_specs=[hbm] * 8,
            out_specs=pl.BlockSpec(memory_space=pltpu.VMEM),
            scratch_shapes=[
                pltpu.VMEM((CH, cols, ROWS), F32),
                pltpu.VMEM((12, cols, ROWS), BF),
                pltpu.VMEM((2, CH, cols, ROWS), F32),
                pltpu.VMEM((2, 128), F32),
                pltpu.VMEM((144, 128), BF),
                pltpu.VMEM((CH, 128), BF),
                pltpu.VMEM((12, cols, ROWS), F32),
                pltpu.VMEM((own + 32, ROWS), F32),
                pltpu.VMEM((own, ROWS), F32),
                pltpu.VMEM((16, (wide + HALO) * ROWS), BF),
                pltpu.VMEM((48, (wide + HALO) * ROWS), BF),
                pltpu.VMEM((48, wide * 2 * ROWS), BF),
                pltpu.VMEM((128, 144), BF),
                pltpu.VMEM((128, 1152), BF),
                pltpu.VMEM((128, 1152), BF),
                pltpu.VMEM((64, 256 * (cols - HALO)), BF),
                pltpu.VMEM((32, 256 * HALO), BF),
                pltpu.VMEM((128, 2 * ROWS), F32),
                pltpu.VMEM((2, own, ROWS), F32),
                pltpu.VMEM((2, 16, ROWS), BF),
                pltpu.VMEM((2, 16, ROWS), BF),
                pltpu.VMEM((384, (wide + 1) * 2 * ROWS), BF),
                pltpu.VMEM((384, (wide - 1) * 2 * ROWS), BF),
                pltpu.VMEM((256 * (cols - HALO), ROWS), BF),
                pltpu.VMEM((256 * HALO, ROWS), BF),
                pltpu.VMEM((256 * HALO, ROWS), BF),
                pltpu.VMEM((16, ROWS), BF),
                pltpu.VMEM((own + 16, ROWS), BF),
                pltpu.VMEM((own, ROWS), BF),
                pltpu.VMEM((groups - 1, own + 32, ROWS), BF),
                pltpu.VMEM((16, ROWS), BF),
                pltpu.VMEM((groups - 1, own, ROWS), BF),
                dma((5,)),
                dma(()),
                dma((2,)),
                dma((2,)),
                dma((2,)),
                dma((2,)),
                dma((2,)),
                dma(()),
                dma(()),
                dma(()),
                dma(()),
                dma((groups - 1, 3)),
                dma((groups - 1, 3)),
                dma((groups - 1,)),
                dma((groups - 1,)),
                pltpu.SemaphoreType.REGULAR((groups - 1,)),
            ],
            compiler_params=pltpu.CompilerParams(
                collective_id=0, has_side_effects=True, vmem_limit_bytes=40 << 20
            ),
        )(*args)

    in_specs = (
        P(None, "tile", None),
        P(None, "tile", None),
        P("step", None, "tile", None),
        P("step", None),
        P(),
        P(),
        P(),
        P(),
    )
    out_specs = P("step", None, "tile", None)
    return jax.shard_map(local, mesh=mesh, in_specs=in_specs, out_specs=out_specs, check_vma=False)
```

```python
import jax
import jax.numpy as jnp
from jax import lax
from jax.experimental import pallas as pl
from jax.experimental.pallas import tpu as pltpu
from jax.sharding import PartitionSpec as P

STEPS = 8
SWEEPS = 2
CH = 4
HALO = 3
FAR = 2 * HALO
ROWS = 128
BF = jnp.bfloat16
F32 = jnp.float32
MESH = pl.DeviceIdType.MESH


def silu_of_half(h):
    return h * jnp.tanh(h) + h


def kernel(
    groups,
    tiles,
    start_hbm,
    cov_hbm,
    noise_hbm,
    embed_hbm,
    win_hbm,
    wfirst_hbm,
    wsecond_hbm,
    wout_hbm,
    out_ref,
    start_ref,
    cov_ref,
    noise_ref,
    embed_ref,
    win_ref,
    wout_ref,
    covf_ref,
    st_ref,
    base_ref,
    xb_ref,
    x1_ref,
    x2_ref,
    w1_ref,
    w2_ref,
    w3_ref,
    wo0_ref,
    wo1_ref,
    eb_ref,
    nz_ref,
    nzb_ref,
    nzs_ref,
    fh_ref,
    sh_ref,
    pr_ref,
    bo0_ref,
    bo1_ref,
    bo2_ref,
    pa_ref,
    pg_ref,
    pd_ref,
    rx_ref,
    rxs_ref,
    rxf_ref,
    in_sem,
    win_sem,
    w_sem,
    halo_send,
    halo_recv,
    rim_send,
    rim_recv,
    noise_send,
    noise_recv,
    near_send,
    near_recv,
    mid_send,
    mid_recv,
    last_send,
    last_recv,
    down,
):
    k = lax.axis_index("step")
    t = lax.axis_index("tile")
    cols = start_ref.shape[1]
    soon = cols - HALO
    rim = 16
    early, late = 2 * rim, rim

    even = t % 2 == 0
    fast = jnp.where(even, t + 1, t - 1)
    slow = jnp.where(even, t - 1, t + 1)
    has_slow = (slow >= 0) & (slow < tiles)

    def turned(n, count):
        return jnp.where(even, count - 1 - n, n)

    def for_later(f):
        def at(d):
            if d < groups:

                @pl.when(k + d < groups)
                def _():
                    f(d)
                    at(d + 1)

        at(1)

    def for_earlier(f):
        def at(d):
            if d < groups:

                @pl.when(k >= d)
                def _():
                    f(d)
                    at(d + 1)

        at(1)

    def either_way(f):
        @pl.when(even)
        def _():
            for c in range(cols):
                f(c, cols - 1 - c)

        @pl.when(jnp.logical_not(even))
        def _():
            for c in range(cols):
                f(c, c)

    get_start, get_cov, get_embed, get_noise, get_wout = [
        pltpu.make_async_copy(src, dst, in_sem.at[n])
        for n, (src, dst) in enumerate(
            (
                (start_hbm, start_ref),
                (cov_hbm, cov_ref),
                (embed_hbm, embed_ref),
                (noise_hbm, noise_ref),
                (wout_hbm, wout_ref),
            )
        )
    ]
    get_win = [
        pltpu.make_async_copy(
            win_hbm.at[pl.ds(a * 48, 48)],
            win_ref.at[pl.ds(pl.multiple_of(turned(a, 3) * 48, 48), 48)],
            win_sem,
        )
        for a in range(3)
    ]
    weights = []
    for n, (src, dst) in enumerate(((wfirst_hbm, w2_ref), (wsecond_hbm, w3_ref))):
        weights.append(
            [
                pltpu.make_async_copy(
                    src.at[3 * a + b],
                    dst.at[:, pl.ds(pl.multiple_of((3 * turned(a, 3) + b) * 128, 128), 128)],
                    w_sem.at[n],
                )
                for a in range(3)
                for b in range(3)
            ]
        )

    for ref in (st_ref, xb_ref, nzs_ref, rx_ref, rxs_ref, rxf_ref):
        ref[...] = jnp.zeros_like(ref)

    barrier = pltpu.get_barrier_semaphore()

    def signal(sem, step, tile):
        pl.semaphore_signal(sem, inc=1, device_id=(step, tile), device_id_type=MESH)

    pl.when(has_slow)(lambda: signal(barrier, k, slow))
    signal(barrier, k, fast)
    for_later(lambda d: signal(barrier, k + d, t))

    for c in (get_cov, get_start, get_noise, *get_win, get_embed, *weights[0], *weights[1], get_wout):
        c.start()

    def lanes(n, width=1):
        return pl.ds(n * ROWS, width * ROWS)

    def place(i):
        if i < 0:
            return -1 - i
        if i >= cols:
            return HALO + cols + FAR - 1 - (i - cols)
        return HALO + i

    def row_of(i):
        if i < 0:
            return CH * (-1 - i)
        if i >= cols:
            return rim + early + late + CH * (HALO - 1 - (i - cols))
        return rim + own_row(i)

    def own_row(i):
        return CH * i if i < soon else early + CH * (i - soon)

    at_fast, own_fast = pl.ds(0, rim), pl.ds(rim, rim)
    own_soon, own_late = pl.ds(rim, early), pl.ds(rim + early, late)
    at_slow = pl.ds(rim + early + late, rim)
    facing, parts = pl.ds(0, rim), (pl.ds(0, early), pl.ds(early, late), pl.ds(early + late, late))
    late_out, own_late_out = pl.ds(early, 2 * late), pl.ds(rim + early, 2 * late)

    get_cov.wait()
    covf_ref[...] = cov_ref[...].astype(F32)
    get_start.wait()

    def put_inputs(c, i):
        x = jnp.concatenate([start_ref[:, c, :], covf_ref[:, c, :]], axis=0)
        xb_ref[:, lanes(place(i))] = x.astype(BF)

    either_way(put_inputs)
    get_noise.wait()
    nz_ref[...] = jnp.zeros_like(nz_ref)

    def put_noise(c, i):
        at = own_row(i)
        n0 = 0.3 * noise_ref[0, :, c, :]
        nz_ref[0, at : at + CH, :] = n0
        nz_ref[1, at : at + CH, :] = n0 + 0.3 * noise_ref[1, :, c, :]

    either_way(put_noise)
    nzb_ref[...] = nz_ref[:, parts[1], :].astype(BF)

    def one(p):
        return p.astype(jnp.int32)

    pl.semaphore_wait(barrier, 1 + one(has_slow) + k)

    def remote(src, dst, send, recv, step, tile):
        return pltpu.make_async_remote_copy(
            src_ref=src,
            dst_ref=dst,
            send_sem=send,
            recv_sem=recv,
            device_id=(step, tile),
            device_id_type=MESH,
        )

    def to_sides(ref, parts, send, recv):
        at_fast, own_fast, own_slow, at_slow = parts
        return (
            remote(ref.at[own_fast], ref.at[at_fast], send.at[0], recv.at[0], k, fast),
            remote(ref.at[own_slow], ref.at[at_slow], send.at[1], recv.at[1], k, slow),
        )

    strips = [
        (slice(None), lanes(n, width))
        for n, width in ((0, HALO), (HALO, HALO), (HALO + cols - FAR, FAR), (HALO + cols, FAR))
    ]
    halo_fast, halo_slow = to_sides(xb_ref, strips, halo_send, halo_recv)
    noise_slow = remote(nzb_ref, nzs_ref, noise_send, noise_recv, k, slow)

    @pl.when(has_slow)
    def _():
        halo_slow.start()
        noise_slow.start()

    halo_fast.start()

    def put_state(c, i):
        st_ref[row_of(i) : row_of(i) + CH, :] = start_ref[:, c, :]

    either_way(put_state)
    rim_fast, rim_slow = to_sides(st_ref, (at_fast, own_fast, own_late, at_slow), rim_send, rim_recv)
    pl.when(has_slow)(rim_slow.start)
    rim_fast.start()

    for_earlier(lambda d: signal(down.at[d - 1], k - d, t))

    pltpu.make_async_copy(win_ref, win_ref, win_sem).wait()
    w1_ref[...] = jnp.transpose(win_ref[...].astype(F32) * 0.5).astype(BF)
    get_embed.wait()
    et = 0.5 * jnp.transpose(jnp.concatenate([embed_ref[...], jnp.zeros((6, 128), F32)], axis=0))
    for s in range(2):
        eb_ref[:, pl.ds(s * ROWS, ROWS)] = jnp.broadcast_to(et[:, s : s + 1], (128, ROWS))

    lane = lax.broadcasted_iota(jnp.int32, (1, ROWS), 1)
    keep_first = (lane > 0).astype(F32).astype(BF)
    keep_last = (lane < ROWS - 1).astype(F32).astype(BF)
    slow_one = has_slow.astype(F32)
    bo_refs = (bo0_ref, bo1_ref, bo2_ref)
    wo_refs = (wo0_ref, wo1_ref, wo1_ref)

    def store_taps(ref, x, at):
        n = x.shape[0]
        at = pl.ds(at * ROWS, ROWS)
        ref[0:n, at] = pltpu.roll(x, 1, 1) * keep_first
        ref[n : 2 * n, at] = x
        ref[2 * n : 3 * n, at] = pltpu.roll(x, ROWS - 1, 1) * keep_last

    def store_both(ref, h, at):
        for s in range(2):
            store_taps(ref, h[:, s * ROWS : (s + 1) * ROWS], 2 * at + s)

    def taps_of(ref, at, which=range(3)):
        return jnp.concatenate(
            [ref[:, pl.ds((at + a) * 2 * ROWS, 2 * ROWS)] for a in which], axis=0
        )

    def conv(w_ref, ref, at, which):
        w = w_ref[:, pl.ds(which[0] * 384, len(which) * 384)]
        return jnp.dot(w, taps_of(ref, at, which), preferred_element_type=F32)

    def ahead(c):
        for n, (w_ref, ref, at) in enumerate(((w2_ref, fh_ref, c + 2), (w3_ref, sh_ref, c))):
            pr_ref[2 * n] = conv(w_ref, ref, at, range(2))
            pr_ref[2 * n + 1] = conv(w_ref, ref, at + 1, range(1))

    def whole(n, done, w_ref, ref, at):
        if not done:
            return conv(w_ref, ref, at, range(3))
        return conv(w_ref, ref, at, range(done, 3)) + pr_ref[2 * n + 2 - done]

    def inside(h, c):
        return h * slow_one if c >= cols else h

    def first_done(pre, c):
        h = inside(silu_of_half(pre + eb_ref[...]), c)
        store_both(fh_ref, h.astype(BF), c + 2)

    def first(c):
        first_done(jnp.dot(w1_ref[...], taps_of(x2_ref, c + 2), preferred_element_type=F32), c)

    def first_pair(pair):
        taps = jnp.concatenate(
            [
                jnp.concatenate([x1_ref[:, lanes(c + 2 + a)] for c in pair], axis=1)
                for a in range(3)
            ],
            axis=0,
        )
        pre = jnp.dot(w1_ref[...], taps, preferred_element_type=F32)
        for n, c in enumerate(pair):
            p = pre[:, n * ROWS : (n + 1) * ROWS]
            first_done(jnp.concatenate([p, p], axis=1), c)

    def second(c, done=0):
        h = whole(0, done, w2_ref, fh_ref, c + 1)
        store_both(sh_ref, inside(silu_of_half(h), c).astype(BF), c + 1)

    def block(c, done=0):
        h = silu_of_half(whole(1, done, w3_ref, sh_ref, c))
        h = (h + fh_ref[128:256, pl.ds((c + 2) * 2 * ROWS, 2 * ROWS)].astype(F32)).astype(BF)
        n, j = (0, c) if c < soon else (1, c - soon) if c < cols else (2, cols + HALO - 1 - c)
        count = (soon, HALO, HALO)[n]
        for s in range(2):
            at = (s * count + j) * 128
            bo_refs[n][at : at + 128, :] = h[:, s * ROWS : (s + 1) * ROWS]

    def project(n):
        p = jnp.dot(wo_refs[n][...], bo_refs[n][...], preferred_element_type=F32)
        size = (early, late, late)[n]
        noises = [nzs_ref[m].astype(F32) if n == 2 else nz_ref[m, parts[n], :] for m in range(2)]
        return p[:size] + noises[0], p[size:] + noises[1]

    def inputs_first(c):
        x = xb_ref[:, lanes(place(c))]
        store_taps(x1_ref, x, c + HALO)

    for c in range(cols):
        inputs_first(c)
    for c in range(1, cols - 1, 2):
        first_pair((c, c + 1))
    pltpu.make_async_copy(w2_ref, w2_ref, w_sem.at[0]).wait()
    w2_ref[...] = w2_ref[...] * BF(0.5)
    for c in range(2, cols - 2):
        second(c)
    pltpu.make_async_copy(w3_ref, w3_ref, w_sem.at[1]).wait()
    w3_ref[...] = w3_ref[...] * BF(0.5)
    for c in range(3, cols - 3):
        block(c)
    get_wout.wait()
    wo = wout_ref[...].astype(F32) * (1.0 / STEPS)
    none = jnp.zeros((CH, 128), F32)
    for n, (count, size) in enumerate(((soon, early), (HALO, late))):
        lhs = []
        for sums in range(2):
            for j in range(count):
                blocks = [wo if s <= sums and i == j else none for s in range(2) for i in range(count)]
                lhs.append(jnp.concatenate(blocks, axis=1))
            lhs.append(jnp.zeros((size - CH * count, 2 * 128 * count), F32))
        wo_refs[n][...] = jnp.concatenate(lhs, axis=0).astype(BF)

    halo_fast.wait_recv()
    for c in (-1, -2, -3):
        inputs_first(c)
    first_pair((0, -1))
    first_pair((-2,))
    for c in (1, 0, -1):
        second(c)
    for c in (2, 1, 0):
        block(c)

    def mids(d):
        def send(n, src, dst, tile):
            return remote(
                pg_ref.at[src],
                rx_ref.at[d - 1, dst],
                mid_send.at[d - 1, n],
                mid_recv.at[d - 1, n],
                k + d,
                tile,
            )

        return (
            send(0, facing, at_fast, fast),
            send(1, parts[0], own_soon, t),
            send(2, late_out, own_late_out, t),
        )

    mid = {d: mids(d) for d in range(1, groups)}
    near_fast = remote(
        pa_ref, rxs_ref, near_send, near_recv, k, fast
    )

    def put_sums(n):
        a, g = project(n)
        pg_ref[parts[n], :] = g.astype(BF)
        if n == 0:
            pa_ref[...] = a[:rim].astype(BF)
        return a

    def wait_mid(*ns):
        def f(d):
            for n in ns:
                mid[d][n].wait_recv()

        return f

    def start_soon(d):
        pl.semaphore_wait(down.at[d - 1], 1)
        mid[d][1].start()
        mid[d][0].start()

    a_soon = put_sums(0)
    near_fast.start()
    for_later(start_soon)

    ahead(soon)

    @pl.when(has_slow)
    def _():
        halo_slow.wait_recv()
        noise_slow.wait_recv()

    for c in range(cols, cols + FAR):
        inputs_first(c)
    for c in range(cols - 1, cols + 5, 2):
        first_pair((c, c + 1))
    for c in range(cols - 2, cols + 4):
        second(c, max(0, cols - c))
    for c in range(cols - 3, cols + 3):
        block(c, max(0, soon + 2 - c))
    a_late = put_sums(1)
    a_out = put_sums(2)

    for_later(lambda d: mid[d][2].start())

    rim_fast.wait_recv()
    near_fast.wait_recv()
    for_earlier(wait_mid(0, 1))

    def base_of(rows):
        base = st_ref[rows, :]
        for d in range(groups - 1):
            base = base + rx_ref[d, rows, :].astype(F32)
        return base

    def inputs_next(c, base, step, row):
        cov = xb_ref[:, lanes(place(c))].astype(F32)[CH:]
        for s, state in enumerate((base, base + step)):
            v = jnp.concatenate([state[row : row + CH], cov], axis=0)
            if c >= cols:
                v = v * slow_one
            store_taps(x2_ref, v.astype(BF), 2 * (c + HALO) + s)

    def next_columns(columns, rows, step, firsts, seconds, blocks, done):
        base = base_of(rows)
        for c in columns:
            inputs_next(c, base, step, row_of(c) - rows.start)
        for c in firsts:
            first(c)
        for n, c in enumerate(seconds):
            second(c, max(0, done - n))
        for n, c in enumerate(blocks):
            block(c, max(0, done - n))
        return base

    step = jnp.concatenate([rxs_ref[...].astype(F32), a_soon], axis=0)
    base = next_columns(
        range(-HALO, soon), pl.ds(0, rim + early), step, range(-2, soon - 1), range(-1, soon - 2), range(soon - 3), 0
    )
    base_ref[parts[0], :] = base[rim:]
    ahead(soon - 3)

    pl.when(has_slow)(rim_slow.wait_recv)
    for_earlier(wait_mid(2))
    base = next_columns(
        range(soon, cols + HALO),
        own_late_out,
        jnp.concatenate([a_late, a_out], axis=0),
        range(soon - 1, cols + 2),
        range(soon - 2, cols + 1),
        range(soon - 3, cols),
        2,
    )
    base_ref[parts[1], :] = base[:late]

    last = {
        d: remote(pd_ref, rxf_ref.at[d - 1], last_send.at[d - 1], last_recv.at[d - 1], k + d, t)
        for d in range(1, groups)
    }
    both = [project(n) for n in range(2)]
    for n, (a, g) in enumerate(both):
        pd_ref[parts[n], :] = (g - pg_ref[parts[n], :].astype(F32)).astype(BF)
    for_later(lambda d: last[d].start())
    (a_soon, g_soon), (a_late, g_late) = both

    def all_sent(*copies):
        for c in copies:
            c.wait_send()

    all_sent(halo_fast, rim_fast, near_fast)
    for_later(lambda d: all_sent(*mid[d]))

    pl.when(has_slow)(lambda: all_sent(halo_slow, rim_slow, noise_slow))

    for_earlier(lambda d: last[d].wait_recv())
    base = base_ref[...]
    for d in range(groups - 1):
        base = base + rxf_ref[d].astype(F32)
    sums = [
        base + jnp.concatenate(both, axis=0) for both in ((a_soon, a_late), (g_soon, g_late))
    ]

    def put_result(c, i):
        at = own_row(i)
        for s in range(2):
            out_ref[s, :, c, :] = sums[s][at : at + CH]

    either_way(put_result)

    for_later(lambda d: all_sent(last[d]))


def solution(mesh):
    groups, tiles = mesh.shape["step"], mesh.shape["tile"]

    def local(start_state, covariates, noise, embedding, w_in, w_first, w_second, w_out):
        cols = start_state.shape[1]
        wide = cols + 2 * HALO
        own = 48
        hbm = pl.BlockSpec(memory_space=pltpu.HBM)
        dma = pltpu.SemaphoreType.DMA
        w_in = jnp.swapaxes(w_in, 1, 2).reshape(144, 128)

        def body(*refs):
            kernel(groups, tiles, *refs)

        args = [
            pltpu.with_memory_space_constraint(v, pltpu.HBM)
            for v in (start_state, covariates, noise, embedding, w_in, w_first, w_second, w_out)
        ]
        return pl.pallas_call(
            body,
            out_shape=pltpu.VMEM((2, 4, cols, ROWS), F32),
            in_specs=[hbm] * 8,
            out_specs=pl.BlockSpec(memory_space=pltpu.VMEM),
            scratch_shapes=[
                pltpu.VMEM((CH, cols, ROWS), F32),
                pltpu.VMEM((12, cols, ROWS), BF),
                pltpu.VMEM((2, CH, cols, ROWS), F32),
                pltpu.VMEM((2, 128), F32),
                pltpu.VMEM((144, 128), BF),
                pltpu.VMEM((CH, 128), BF),
                pltpu.VMEM((12, cols, ROWS), F32),
                pltpu.VMEM((own + 32, ROWS), F32),
                pltpu.VMEM((own, ROWS), F32),
                pltpu.VMEM((16, (wide + HALO) * ROWS), BF),
                pltpu.VMEM((48, (wide + HALO) * ROWS), BF),
                pltpu.VMEM((48, wide * 2 * ROWS), BF),
                pltpu.VMEM((128, 144), BF),
                pltpu.VMEM((128, 1152), BF),
                pltpu.VMEM((128, 1152), BF),
                pltpu.VMEM((64, 256 * (cols - HALO)), BF),
                pltpu.VMEM((32, 256 * HALO), BF),
                pltpu.VMEM((128, 2 * ROWS), F32),
                pltpu.VMEM((2, own, ROWS), F32),
                pltpu.VMEM((2, 16, ROWS), BF),
                pltpu.VMEM((2, 16, ROWS), BF),
                pltpu.VMEM((384, (wide + 1) * 2 * ROWS), BF),
                pltpu.VMEM((384, (wide - 1) * 2 * ROWS), BF),
                pltpu.VMEM((4, 128, 2 * ROWS), F32),
                pltpu.VMEM((256 * (cols - HALO), ROWS), BF),
                pltpu.VMEM((256 * HALO, ROWS), BF),
                pltpu.VMEM((256 * HALO, ROWS), BF),
                pltpu.VMEM((16, ROWS), BF),
                pltpu.VMEM((own + 16, ROWS), BF),
                pltpu.VMEM((own, ROWS), BF),
                pltpu.VMEM((groups - 1, own + 32, ROWS), BF),
                pltpu.VMEM((16, ROWS), BF),
                pltpu.VMEM((groups - 1, own, ROWS), BF),
                dma((5,)),
                dma(()),
                dma((2,)),
                dma((2,)),
                dma((2,)),
                dma((2,)),
                dma((2,)),
                dma(()),
                dma(()),
                dma(()),
                dma(()),
                dma((groups - 1, 3)),
                dma((groups - 1, 3)),
                dma((groups - 1,)),
                dma((groups - 1,)),
                pltpu.SemaphoreType.REGULAR((groups - 1,)),
            ],
            compiler_params=pltpu.CompilerParams(
                collective_id=0, has_side_effects=True, vmem_limit_bytes=40 << 20
            ),
        )(*args)

    in_specs = (
        P(None, "tile", None),
        P(None, "tile", None),
        P("step", None, "tile", None),
        P("step", None),
        P(),
        P(),
        P(),
        P(),
    )
    out_specs = P("step", None, "tile", None)
    return jax.shard_map(local, mesh=mesh, in_specs=in_specs, out_specs=out_specs, check_vma=False)
```

```python
import jax
import jax.numpy as jnp
from jax import lax
from jax.experimental import pallas as pl
from jax.experimental.pallas import tpu as pltpu
from jax.sharding import PartitionSpec as P

STEPS = 8
SWEEPS = 2
CH = 4
HALO = 3
FAR = 2 * HALO
ROWS = 128
BF = jnp.bfloat16
F32 = jnp.float32
MESH = pl.DeviceIdType.MESH


def silu_of_half(h):
    return h * jnp.tanh(h) + h


def kernel(
    groups,
    tiles,
    start_hbm,
    cov_hbm,
    noise_hbm,
    embed_hbm,
    win_hbm,
    wfirst_hbm,
    wsecond_hbm,
    wout_hbm,
    out_ref,
    start_ref,
    cov_ref,
    noise_ref,
    embed_ref,
    win_ref,
    wout_ref,
    covf_ref,
    st_ref,
    base_ref,
    xb_ref,
    x1_ref,
    x2_ref,
    w1_ref,
    w2_ref,
    w3_ref,
    wo0_ref,
    wo1_ref,
    eb_ref,
    nz_ref,
    nzb_ref,
    nzs_ref,
    fh_ref,
    sh_ref,
    pr_ref,
    bo0_ref,
    bo1_ref,
    bo2_ref,
    pa_ref,
    pg_ref,
    pd_ref,
    rx_ref,
    rxs_ref,
    rxf_ref,
    in_sem,
    win_sem,
    w_sem,
    halo_send,
    halo_recv,
    rim_send,
    rim_recv,
    noise_send,
    noise_recv,
    near_send,
    near_recv,
    mid_send,
    mid_recv,
    last_send,
    last_recv,
    down,
):
    k = lax.axis_index("step")
    t = lax.axis_index("tile")
    cols = start_ref.shape[1]
    soon = cols - HALO
    rim = 16
    early, late = 2 * rim, rim

    even = t % 2 == 0
    fast = jnp.where(even, t + 1, t - 1)
    slow = jnp.where(even, t - 1, t + 1)
    has_slow = (slow >= 0) & (slow < tiles)

    def turned(n, count):
        return jnp.where(even, count - 1 - n, n)

    def for_later(f):
        def at(d):
            if d < groups:

                @pl.when(k + d < groups)
                def _():
                    f(d)
                    at(d + 1)

        at(1)

    def for_earlier(f):
        def at(d):
            if d < groups:

                @pl.when(k >= d)
                def _():
                    f(d)
                    at(d + 1)

        at(1)

    def either_way(f):
        @pl.when(even)
        def _():
            for c in range(cols):
                f(c, cols - 1 - c)

        @pl.when(jnp.logical_not(even))
        def _():
            for c in range(cols):
                f(c, c)

    get_start, get_cov, get_embed, get_noise, get_wout = [
        pltpu.make_async_copy(src, dst, in_sem.at[n])
        for n, (src, dst) in enumerate(
            (
                (start_hbm, start_ref),
                (cov_hbm, cov_ref),
                (embed_hbm, embed_ref),
                (noise_hbm, noise_ref),
                (wout_hbm, wout_ref),
            )
        )
    ]
    get_win = [
        pltpu.make_async_copy(
            win_hbm.at[pl.ds(a * 48, 48)],
            win_ref.at[pl.ds(pl.multiple_of(turned(a, 3) * 48, 48), 48)],
            win_sem,
        )
        for a in range(3)
    ]
    weights = []
    for n, (src, dst) in enumerate(((wfirst_hbm, w2_ref), (wsecond_hbm, w3_ref))):
        weights.append(
            [
                pltpu.make_async_copy(
                    src.at[3 * a + b],
                    dst.at[:, pl.ds(pl.multiple_of((3 * turned(a, 3) + b) * 128, 128), 128)],
                    w_sem.at[n],
                )
                for a in range(3)
                for b in range(3)
            ]
        )

    for ref in (st_ref, xb_ref, nzs_ref, rx_ref, rxs_ref, rxf_ref):
        ref[...] = jnp.zeros_like(ref)

    barrier = pltpu.get_barrier_semaphore()

    def signal(sem, step, tile):
        pl.semaphore_signal(sem, inc=1, device_id=(step, tile), device_id_type=MESH)

    pl.when(has_slow)(lambda: signal(barrier, k, slow))
    signal(barrier, k, fast)
    for_later(lambda d: signal(barrier, k + d, t))

    for c in (get_cov, get_start, get_noise, *get_win, get_embed, *weights[0], *weights[1], get_wout):
        c.start()

    def lanes(n, width=1):
        return pl.ds(n * ROWS, width * ROWS)

    def place(i):
        if i < 0:
            return -1 - i
        if i >= cols:
            return HALO + cols + FAR - 1 - (i - cols)
        return HALO + i

    def row_of(i):
        if i < 0:
            return CH * (-1 - i)
        if i >= cols:
            return rim + early + late + CH * (HALO - 1 - (i - cols))
        return rim + own_row(i)

    def own_row(i):
        return CH * i if i < soon else early + CH * (i - soon)

    at_fast, own_fast = pl.ds(0, rim), pl.ds(rim, rim)
    own_soon, own_late = pl.ds(rim, early), pl.ds(rim + early, late)
    at_slow = pl.ds(rim + early + late, rim)
    facing, parts = pl.ds(0, rim), (pl.ds(0, early), pl.ds(early, late), pl.ds(early + late, late))
    late_out, own_late_out = pl.ds(early, 2 * late), pl.ds(rim + early, 2 * late)

    get_cov.wait()
    covf_ref[...] = cov_ref[...].astype(F32)
    get_start.wait()

    def put_inputs(c, i):
        x = jnp.concatenate([start_ref[:, c, :], covf_ref[:, c, :]], axis=0)
        xb_ref[:, lanes(place(i))] = x.astype(BF)

    either_way(put_inputs)
    get_noise.wait()
    nz_ref[...] = jnp.zeros_like(nz_ref)

    def put_noise(c, i):
        at = own_row(i)
        n0 = 0.3 * noise_ref[0, :, c, :]
        nz_ref[0, at : at + CH, :] = n0
        nz_ref[1, at : at + CH, :] = n0 + 0.3 * noise_ref[1, :, c, :]

    either_way(put_noise)
    nzb_ref[...] = nz_ref[:, parts[1], :].astype(BF)

    def one(p):
        return p.astype(jnp.int32)

    pl.semaphore_wait(barrier, 1 + one(has_slow) + k)

    def remote(src, dst, send, recv, step, tile):
        return pltpu.make_async_remote_copy(
            src_ref=src,
            dst_ref=dst,
            send_sem=send,
            recv_sem=recv,
            device_id=(step, tile),
            device_id_type=MESH,
        )

    def to_sides(ref, parts, send, recv):
        at_fast, own_fast, own_slow, at_slow = parts
        return (
            remote(ref.at[own_fast], ref.at[at_fast], send.at[0], recv.at[0], k, fast),
            remote(ref.at[own_slow], ref.at[at_slow], send.at[1], recv.at[1], k, slow),
        )

    strips = [
        (slice(None), lanes(n, width))
        for n, width in ((0, HALO), (HALO, HALO), (HALO + cols - FAR, FAR), (HALO + cols, FAR))
    ]
    halo_fast, halo_slow = to_sides(xb_ref, strips, halo_send, halo_recv)
    noise_slow = remote(nzb_ref, nzs_ref, noise_send, noise_recv, k, slow)

    @pl.when(has_slow)
    def _():
        halo_slow.start()
        noise_slow.start()

    halo_fast.start()

    def put_state(c, i):
        st_ref[row_of(i) : row_of(i) + CH, :] = start_ref[:, c, :]

    either_way(put_state)
    rim_fast, rim_slow = to_sides(st_ref, (at_fast, own_fast, own_late, at_slow), rim_send, rim_recv)
    pl.when(has_slow)(rim_slow.start)
    rim_fast.start()

    for_earlier(lambda d: signal(down.at[d - 1], k - d, t))

    pltpu.make_async_copy(win_ref, win_ref, win_sem).wait()
    w1_ref[...] = jnp.transpose(win_ref[...].astype(F32) * 0.5).astype(BF)
    get_embed.wait()
    et = 0.5 * jnp.transpose(jnp.concatenate([embed_ref[...], jnp.zeros((6, 128), F32)], axis=0))
    for s in range(2):
        eb_ref[:, pl.ds(s * ROWS, ROWS)] = jnp.broadcast_to(et[:, s : s + 1], (128, ROWS))

    lane = lax.broadcasted_iota(jnp.int32, (1, ROWS), 1)
    keep_first = (lane > 0).astype(F32).astype(BF)
    keep_last = (lane < ROWS - 1).astype(F32).astype(BF)
    slow_one = has_slow.astype(F32)
    bo_refs = (bo0_ref, bo1_ref, bo2_ref)
    wo_refs = (wo0_ref, wo1_ref, wo1_ref)

    def store_taps(ref, x, at):
        n = x.shape[0]
        at = pl.ds(at * ROWS, ROWS)
        ref[0:n, at] = pltpu.roll(x, 1, 1) * keep_first
        ref[n : 2 * n, at] = x
        ref[2 * n : 3 * n, at] = pltpu.roll(x, ROWS - 1, 1) * keep_last

    def store_both(ref, h, at):
        for s in range(2):
            store_taps(ref, h[:, s * ROWS : (s + 1) * ROWS], 2 * at + s)

    def taps_of(ref, at, which=range(3)):
        return jnp.concatenate(
            [ref[:, pl.ds((at + a) * 2 * ROWS, 2 * ROWS)] for a in which], axis=0
        )

    def conv(w_ref, ref, at, which):
        w = w_ref[:, pl.ds(which[0] * 384, len(which) * 384)]
        return jnp.dot(w, taps_of(ref, at, which), preferred_element_type=F32)

    def ahead(c):
        for n, (w_ref, ref, at) in enumerate(((w2_ref, fh_ref, c + 2), (w3_ref, sh_ref, c))):
            pr_ref[2 * n] = conv(w_ref, ref, at, range(2))
            pr_ref[2 * n + 1] = conv(w_ref, ref, at + 1, range(1))

    def whole(n, done, w_ref, ref, at):
        if not done:
            return conv(w_ref, ref, at, range(3))
        return conv(w_ref, ref, at, range(done, 3)) + pr_ref[2 * n + 2 - done]

    def inside(h, c):
        return h * slow_one if c >= cols else h

    def first_done(pre, c):
        h = inside(silu_of_half(pre + eb_ref[...]), c)
        store_both(fh_ref, h.astype(BF), c + 2)

    def first(c):
        first_done(jnp.dot(w1_ref[...], taps_of(x2_ref, c + 2), preferred_element_type=F32), c)

    def first_pair(pair):
        taps = jnp.concatenate(
            [
                jnp.concatenate([x1_ref[:, lanes(c + 2 + a)] for c in pair], axis=1)
                for a in range(3)
            ],
            axis=0,
        )
        pre = jnp.dot(w1_ref[...], taps, preferred_element_type=F32)
        for n, c in enumerate(pair):
            p = pre[:, n * ROWS : (n + 1) * ROWS]
            first_done(jnp.concatenate([p, p], axis=1), c)

    def second(c, done=0):
        h = whole(0, done, w2_ref, fh_ref, c + 1)
        store_both(sh_ref, inside(silu_of_half(h), c).astype(BF), c + 1)

    def block(c, done=0):
        h = silu_of_half(whole(1, done, w3_ref, sh_ref, c))
        h = (h + fh_ref[128:256, pl.ds((c + 2) * 2 * ROWS, 2 * ROWS)].astype(F32)).astype(BF)
        n, j = (0, c) if c < soon else (1, c - soon) if c < cols else (2, cols + HALO - 1 - c)
        count = (soon, HALO, HALO)[n]
        for s in range(2):
            at = (s * count + j) * 128
            bo_refs[n][at : at + 128, :] = h[:, s * ROWS : (s + 1) * ROWS]

    def project(n):
        p = jnp.dot(wo_refs[n][...], bo_refs[n][...], preferred_element_type=F32)
        size = (early, late, late)[n]
        noises = [nzs_ref[m].astype(F32) if n == 2 else nz_ref[m, parts[n], :] for m in range(2)]
        return p[:size] + noises[0], p[size:] + noises[1]

    def inputs_first(c):
        x = xb_ref[:, lanes(place(c))]
        store_taps(x1_ref, x, c + HALO)

    for c in range(cols):
        inputs_first(c)
    for c in range(1, cols - 1, 2):
        first_pair((c, c + 1))
    pltpu.make_async_copy(w2_ref, w2_ref, w_sem.at[0]).wait()
    w2_ref[...] = w2_ref[...] * BF(0.5)
    for c in range(2, cols - 2):
        second(c)
    pltpu.make_async_copy(w3_ref, w3_ref, w_sem.at[1]).wait()
    w3_ref[...] = w3_ref[...] * BF(0.5)
    for c in range(3, cols - 3):
        block(c)
    get_wout.wait()
    wo = wout_ref[...].astype(F32) * (1.0 / STEPS)
    none = jnp.zeros((CH, 128), F32)
    for n, (count, size) in enumerate(((soon, early), (HALO, late))):
        lhs = []
        for sums in range(2):
            for j in range(count):
                blocks = [wo if s <= sums and i == j else none for s in range(2) for i in range(count)]
                lhs.append(jnp.concatenate(blocks, axis=1))
            lhs.append(jnp.zeros((size - CH * count, 2 * 128 * count), F32))
        wo_refs[n][...] = jnp.concatenate(lhs, axis=0).astype(BF)

    halo_fast.wait_recv()
    for c in (-1, -2, -3):
        inputs_first(c)
    first_pair((0, -1))
    first_pair((-2,))
    for c in (1, 0, -1):
        second(c)
    for c in (2, 1, 0):
        block(c)

    def mids(d):
        def send(n, src, dst, tile):
            return remote(
                pg_ref.at[src],
                rx_ref.at[d - 1, dst],
                mid_send.at[d - 1, n],
                mid_recv.at[d - 1, n],
                k + d,
                tile,
            )

        return (
            send(0, facing, at_fast, fast),
            send(1, parts[0], own_soon, t),
            send(2, late_out, own_late_out, t),
        )

    mid = {d: mids(d) for d in range(1, groups)}
    near_fast = remote(
        pa_ref, rxs_ref, near_send, near_recv, k, fast
    )

    def put_sums(n):
        a, g = project(n)
        pg_ref[parts[n], :] = g.astype(BF)
        if n == 0:
            pa_ref[...] = a[:rim].astype(BF)
        return a

    def wait_mid(*ns):
        def f(d):
            for n in ns:
                mid[d][n].wait_recv()

        return f

    def start_soon(d):
        pl.semaphore_wait(down.at[d - 1], 1)
        mid[d][1].start()
        mid[d][0].start()

    a_soon = put_sums(0)
    near_fast.start()
    for_later(start_soon)

    ahead(soon)

    @pl.when(has_slow)
    def _():
        halo_slow.wait_recv()
        noise_slow.wait_recv()

    for c in range(cols, cols + FAR):
        inputs_first(c)
    for c in range(cols - 1, cols + 5, 2):
        first_pair((c, c + 1))
    for c in range(cols - 2, cols + 4):
        second(c, max(0, cols - c))
    for c in range(cols - 3, cols + 3):
        block(c, max(0, soon + 2 - c))
    a_late = put_sums(1)
    a_out = put_sums(2)

    for d in sorted(range(1, groups), key=lambda d: -min(d, groups - d)):
        pl.when(k + d < groups)(mid[d][2].start)

    rim_fast.wait_recv()
    near_fast.wait_recv()
    for_earlier(wait_mid(0, 1))

    def base_of(rows):
        base = st_ref[rows, :]
        for d in range(groups - 1):
            base = base + rx_ref[d, rows, :].astype(F32)
        return base

    def inputs_next(c, base, step, row):
        cov = xb_ref[:, lanes(place(c))].astype(F32)[CH:]
        for s, state in enumerate((base, base + step)):
            v = jnp.concatenate([state[row : row + CH], cov], axis=0)
            if c >= cols:
                v = v * slow_one
            store_taps(x2_ref, v.astype(BF), 2 * (c + HALO) + s)

    def next_columns(columns, rows, step, firsts, seconds, blocks, done):
        base = base_of(rows)
        for c in columns:
            inputs_next(c, base, step, row_of(c) - rows.start)
        for c in firsts:
            first(c)
        for n, c in enumerate(seconds):
            second(c, max(0, done - n))
        for n, c in enumerate(blocks):
            block(c, max(0, done - n))
        return base

    step = jnp.concatenate([rxs_ref[...].astype(F32), a_soon], axis=0)
    base = next_columns(
        range(-HALO, soon), pl.ds(0, rim + early), step, range(-2, soon - 1), range(-1, soon - 2), range(soon - 3), 0
    )
    base_ref[parts[0], :] = base[rim:]
    ahead(soon - 3)

    pl.when(has_slow)(rim_slow.wait_recv)
    for_earlier(wait_mid(2))
    base = next_columns(
        range(soon, cols + HALO),
        own_late_out,
        jnp.concatenate([a_late, a_out], axis=0),
        range(soon - 1, cols + 2),
        range(soon - 2, cols + 1),
        range(soon - 3, cols),
        2,
    )
    base_ref[parts[1], :] = base[:late]

    last = {
        d: remote(pd_ref, rxf_ref.at[d - 1], last_send.at[d - 1], last_recv.at[d - 1], k + d, t)
        for d in range(1, groups)
    }
    both = [project(n) for n in range(2)]
    for n, (a, g) in enumerate(both):
        pd_ref[parts[n], :] = (g - pg_ref[parts[n], :].astype(F32)).astype(BF)
    for_later(lambda d: last[d].start())
    (a_soon, g_soon), (a_late, g_late) = both

    def all_sent(*copies):
        for c in copies:
            c.wait_send()

    all_sent(halo_fast, rim_fast, near_fast)
    for_later(lambda d: all_sent(*mid[d]))

    pl.when(has_slow)(lambda: all_sent(halo_slow, rim_slow, noise_slow))

    for_earlier(lambda d: last[d].wait_recv())
    base = base_ref[...]
    for d in range(groups - 1):
        base = base + rxf_ref[d].astype(F32)
    sums = [
        base + jnp.concatenate(both, axis=0) for both in ((a_soon, a_late), (g_soon, g_late))
    ]

    def put_result(c, i):
        at = own_row(i)
        for s in range(2):
            out_ref[s, :, c, :] = sums[s][at : at + CH]

    either_way(put_result)

    for_later(lambda d: all_sent(last[d]))


def solution(mesh):
    groups, tiles = mesh.shape["step"], mesh.shape["tile"]

    def local(start_state, covariates, noise, embedding, w_in, w_first, w_second, w_out):
        cols = start_state.shape[1]
        wide = cols + 2 * HALO
        own = 48
        hbm = pl.BlockSpec(memory_space=pltpu.HBM)
        dma = pltpu.SemaphoreType.DMA
        w_in = jnp.swapaxes(w_in, 1, 2).reshape(144, 128)

        def body(*refs):
            kernel(groups, tiles, *refs)

        args = [
            pltpu.with_memory_space_constraint(v, pltpu.HBM)
            for v in (start_state, covariates, noise, embedding, w_in, w_first, w_second, w_out)
        ]
        return pl.pallas_call(
            body,
            out_shape=pltpu.VMEM((2, 4, cols, ROWS), F32),
            in_specs=[hbm] * 8,
            out_specs=pl.BlockSpec(memory_space=pltpu.VMEM),
            scratch_shapes=[
                pltpu.VMEM((CH, cols, ROWS), F32),
                pltpu.VMEM((12, cols, ROWS), BF),
                pltpu.VMEM((2, CH, cols, ROWS), F32),
                pltpu.VMEM((2, 128), F32),
                pltpu.VMEM((144, 128), BF),
                pltpu.VMEM((CH, 128), BF),
                pltpu.VMEM((12, cols, ROWS), F32),
                pltpu.VMEM((own + 32, ROWS), F32),
                pltpu.VMEM((own, ROWS), F32),
                pltpu.VMEM((16, (wide + HALO) * ROWS), BF),
                pltpu.VMEM((48, (wide + HALO) * ROWS), BF),
                pltpu.VMEM((48, wide * 2 * ROWS), BF),
                pltpu.VMEM((128, 144), BF),
                pltpu.VMEM((128, 1152), BF),
                pltpu.VMEM((128, 1152), BF),
                pltpu.VMEM((64, 256 * (cols - HALO)), BF),
                pltpu.VMEM((32, 256 * HALO), BF),
                pltpu.VMEM((128, 2 * ROWS), F32),
                pltpu.VMEM((2, own, ROWS), F32),
                pltpu.VMEM((2, 16, ROWS), BF),
                pltpu.VMEM((2, 16, ROWS), BF),
                pltpu.VMEM((384, (wide + 1) * 2 * ROWS), BF),
                pltpu.VMEM((384, (wide - 1) * 2 * ROWS), BF),
                pltpu.VMEM((4, 128, 2 * ROWS), F32),
                pltpu.VMEM((256 * (cols - HALO), ROWS), BF),
                pltpu.VMEM((256 * HALO, ROWS), BF),
                pltpu.VMEM((256 * HALO, ROWS), BF),
                pltpu.VMEM((16, ROWS), BF),
                pltpu.VMEM((own + 16, ROWS), BF),
                pltpu.VMEM((own, ROWS), BF),
                pltpu.VMEM((groups - 1, own + 32, ROWS), BF),
                pltpu.VMEM((16, ROWS), BF),
                pltpu.VMEM((groups - 1, own, ROWS), BF),
                dma((5,)),
                dma(()),
                dma((2,)),
                dma((2,)),
                dma((2,)),
                dma((2,)),
                dma((2,)),
                dma(()),
                dma(()),
                dma(()),
                dma(()),
                dma((groups - 1, 3)),
                dma((groups - 1, 3)),
                dma((groups - 1,)),
                dma((groups - 1,)),
                pltpu.SemaphoreType.REGULAR((groups - 1,)),
            ],
            compiler_params=pltpu.CompilerParams(
                collective_id=0, has_side_effects=True, vmem_limit_bytes=40 << 20
            ),
        )(*args)

    in_specs = (
        P(None, "tile", None),
        P(None, "tile", None),
        P("step", None, "tile", None),
        P("step", None),
        P(),
        P(),
        P(),
        P(),
    )
    out_specs = P("step", None, "tile", None)
    return jax.shard_map(local, mesh=mesh, in_specs=in_specs, out_specs=out_specs, check_vma=False)
```

```python
import jax
import jax.numpy as jnp
from jax import lax
from jax.experimental import pallas as pl
from jax.experimental.pallas import tpu as pltpu
from jax.sharding import PartitionSpec as P

STEPS = 8
SWEEPS = 2
CH = 4
HALO = 3
FAR = 2 * HALO
ROWS = 128
BF = jnp.bfloat16
F32 = jnp.float32
MESH = pl.DeviceIdType.MESH


def silu_of_half(h):
    return h * jnp.tanh(h) + h


def kernel(
    groups,
    tiles,
    start_hbm,
    cov_hbm,
    noise_hbm,
    embed_hbm,
    win_hbm,
    wfirst_hbm,
    wsecond_hbm,
    wout_hbm,
    out_ref,
    start_ref,
    cov_ref,
    noise_ref,
    embed_ref,
    win_ref,
    wout_ref,
    covf_ref,
    st_ref,
    base_ref,
    xb_ref,
    x1_ref,
    x2_ref,
    w1_ref,
    w2_ref,
    w3_ref,
    wo0_ref,
    wo1_ref,
    eb_ref,
    nz_ref,
    nzb_ref,
    nzs_ref,
    fh_ref,
    sh_ref,
    pr_ref,
    bo0_ref,
    bo1_ref,
    bo2_ref,
    pa_ref,
    pg_ref,
    pd_ref,
    rx_ref,
    rxs_ref,
    rxf_ref,
    in_sem,
    win_sem,
    w_sem,
    halo_send,
    halo_recv,
    rim_send,
    rim_recv,
    noise_send,
    noise_recv,
    near_send,
    near_recv,
    mid_send,
    mid_recv,
    last_send,
    last_recv,
    down,
):
    k = lax.axis_index("step")
    t = lax.axis_index("tile")
    cols = start_ref.shape[1]
    soon = cols - HALO
    rim = 16
    early, late = 2 * rim, rim

    even = t % 2 == 0
    fast = jnp.where(even, t + 1, t - 1)
    slow = jnp.where(even, t - 1, t + 1)
    has_slow = (slow >= 0) & (slow < tiles)

    def turned(n, count):
        return jnp.where(even, count - 1 - n, n)

    def for_later(f):
        def at(d):
            if d < groups:

                @pl.when(k + d < groups)
                def _():
                    f(d)
                    at(d + 1)

        at(1)

    def for_earlier(f):
        def at(d):
            if d < groups:

                @pl.when(k >= d)
                def _():
                    f(d)
                    at(d + 1)

        at(1)

    def either_way(f):
        @pl.when(even)
        def _():
            for c in range(cols):
                f(c, cols - 1 - c)

        @pl.when(jnp.logical_not(even))
        def _():
            for c in range(cols):
                f(c, c)

    get_start, get_cov, get_embed, get_noise, get_wout = [
        pltpu.make_async_copy(src, dst, in_sem.at[n])
        for n, (src, dst) in enumerate(
            (
                (start_hbm, start_ref),
                (cov_hbm, cov_ref),
                (embed_hbm, embed_ref),
                (noise_hbm, noise_ref),
                (wout_hbm, wout_ref),
            )
        )
    ]
    get_win = [
        pltpu.make_async_copy(
            win_hbm.at[pl.ds(a * 48, 48)],
            win_ref.at[pl.ds(pl.multiple_of(turned(a, 3) * 48, 48), 48)],
            win_sem,
        )
        for a in range(3)
    ]
    weights = []
    for n, (src, dst) in enumerate(((wfirst_hbm, w2_ref), (wsecond_hbm, w3_ref))):
        weights.append(
            [
                pltpu.make_async_copy(
                    src.at[3 * a + b],
                    dst.at[:, pl.ds(pl.multiple_of((3 * turned(a, 3) + b) * 128, 128), 128)],
                    w_sem.at[n],
                )
                for a in range(3)
                for b in range(3)
            ]
        )

    for ref in (st_ref, xb_ref, nzs_ref, rx_ref, rxs_ref, rxf_ref):
        ref[...] = jnp.zeros_like(ref)

    barrier = pltpu.get_barrier_semaphore()

    def signal(sem, step, tile):
        pl.semaphore_signal(sem, inc=1, device_id=(step, tile), device_id_type=MESH)

    pl.when(has_slow)(lambda: signal(barrier, k, slow))
    signal(barrier, k, fast)
    for_later(lambda d: signal(barrier, k + d, t))

    for c in (get_cov, get_start, get_noise, *get_win, get_embed, *weights[0], *weights[1], get_wout):
        c.start()

    def lanes(n, width=1):
        return pl.ds(n * ROWS, width * ROWS)

    def place(i):
        if i < 0:
            return -1 - i
        if i >= cols:
            return HALO + cols + FAR - 1 - (i - cols)
        return HALO + i

    def row_of(i):
        if i < 0:
            return CH * (-1 - i)
        if i >= cols:
            return rim + early + late + CH * (HALO - 1 - (i - cols))
        return rim + own_row(i)

    def own_row(i):
        return CH * i if i < soon else early + CH * (i - soon)

    at_fast, own_fast = pl.ds(0, rim), pl.ds(rim, rim)
    own_soon, own_late = pl.ds(rim, early), pl.ds(rim + early, late)
    at_slow = pl.ds(rim + early + late, rim)
    facing, parts = pl.ds(0, rim), (pl.ds(0, early), pl.ds(early, late), pl.ds(early + late, late))
    late_out, own_late_out = pl.ds(early, 2 * late), pl.ds(rim + early, 2 * late)

    get_cov.wait()
    covf_ref[...] = cov_ref[...].astype(F32)
    get_start.wait()

    def put_inputs(c, i):
        x = jnp.concatenate([start_ref[:, c, :], covf_ref[:, c, :]], axis=0)
        xb_ref[:, lanes(place(i))] = x.astype(BF)

    either_way(put_inputs)
    get_noise.wait()
    nz_ref[...] = jnp.zeros_like(nz_ref)

    def put_noise(c, i):
        at = own_row(i)
        n0 = 0.3 * noise_ref[0, :, c, :]
        nz_ref[0, at : at + CH, :] = n0
        nz_ref[1, at : at + CH, :] = n0 + 0.3 * noise_ref[1, :, c, :]

    either_way(put_noise)
    nzb_ref[...] = nz_ref[:, parts[1], :].astype(BF)

    def one(p):
        return p.astype(jnp.int32)

    pl.semaphore_wait(barrier, 1 + one(has_slow) + k)

    def remote(src, dst, send, recv, step, tile):
        return pltpu.make_async_remote_copy(
            src_ref=src,
            dst_ref=dst,
            send_sem=send,
            recv_sem=recv,
            device_id=(step, tile),
            device_id_type=MESH,
        )

    def to_sides(ref, parts, send, recv):
        at_fast, own_fast, own_slow, at_slow = parts
        return (
            remote(ref.at[own_fast], ref.at[at_fast], send.at[0], recv.at[0], k, fast),
            remote(ref.at[own_slow], ref.at[at_slow], send.at[1], recv.at[1], k, slow),
        )

    strips = [
        (slice(None), lanes(n, width))
        for n, width in ((0, HALO), (HALO, HALO), (HALO + cols - FAR, FAR), (HALO + cols, FAR))
    ]
    halo_fast, halo_slow = to_sides(xb_ref, strips, halo_send, halo_recv)
    noise_slow = remote(nzb_ref, nzs_ref, noise_send, noise_recv, k, slow)

    @pl.when(has_slow)
    def _():
        halo_slow.start()
        noise_slow.start()

    halo_fast.start()

    for_earlier(lambda d: signal(down.at[d - 1], k - d, t))


    def put_state(c, i):
        st_ref[row_of(i) : row_of(i) + CH, :] = start_ref[:, c, :]

    either_way(put_state)
    rim_fast, rim_slow = to_sides(st_ref, (at_fast, own_fast, own_late, at_slow), rim_send, rim_recv)
    pl.when(has_slow)(rim_slow.start)
    rim_fast.start()

    pltpu.make_async_copy(win_ref, win_ref, win_sem).wait()
    w1_ref[...] = jnp.transpose(win_ref[...].astype(F32) * 0.5).astype(BF)
    get_embed.wait()
    et = 0.5 * jnp.transpose(jnp.concatenate([embed_ref[...], jnp.zeros((6, 128), F32)], axis=0))
    for s in range(2):
        eb_ref[:, pl.ds(s * ROWS, ROWS)] = jnp.broadcast_to(et[:, s : s + 1], (128, ROWS))

    lane = lax.broadcasted_iota(jnp.int32, (1, ROWS), 1)
    keep_first = (lane > 0).astype(F32).astype(BF)
    keep_last = (lane < ROWS - 1).astype(F32).astype(BF)
    slow_one = has_slow.astype(F32)
    bo_refs = (bo0_ref, bo1_ref, bo2_ref)
    wo_refs = (wo0_ref, wo1_ref, wo1_ref)

    def store_taps(ref, x, at):
        n = x.shape[0]
        at = pl.ds(at * ROWS, ROWS)
        ref[0:n, at] = pltpu.roll(x, 1, 1) * keep_first
        ref[n : 2 * n, at] = x
        ref[2 * n : 3 * n, at] = pltpu.roll(x, ROWS - 1, 1) * keep_last

    def store_both(ref, h, at):
        for s in range(2):
            store_taps(ref, h[:, s * ROWS : (s + 1) * ROWS], 2 * at + s)

    def taps_of(ref, at, which=range(3)):
        return jnp.concatenate(
            [ref[:, pl.ds((at + a) * 2 * ROWS, 2 * ROWS)] for a in which], axis=0
        )

    def conv(w_ref, ref, at, which):
        w = w_ref[:, pl.ds(which[0] * 384, len(which) * 384)]
        return jnp.dot(w, taps_of(ref, at, which), preferred_element_type=F32)

    def ahead(c):
        for n, (w_ref, ref, at) in enumerate(((w2_ref, fh_ref, c + 2), (w3_ref, sh_ref, c))):
            pr_ref[2 * n] = conv(w_ref, ref, at, range(2))
            pr_ref[2 * n + 1] = conv(w_ref, ref, at + 1, range(1))

    def whole(n, done, w_ref, ref, at):
        if not done:
            return conv(w_ref, ref, at, range(3))
        return conv(w_ref, ref, at, range(done, 3)) + pr_ref[2 * n + 2 - done]

    def inside(h, c):
        return h * slow_one if c >= cols else h

    def first_done(pre, c):
        h = inside(silu_of_half(pre + eb_ref[...]), c)
        store_both(fh_ref, h.astype(BF), c + 2)

    def first(c):
        first_done(jnp.dot(w1_ref[...], taps_of(x2_ref, c + 2), preferred_element_type=F32), c)

    def first_pair(pair):
        taps = jnp.concatenate(
            [
                jnp.concatenate([x1_ref[:, lanes(c + 2 + a)] for c in pair], axis=1)
                for a in range(3)
            ],
            axis=0,
        )
        pre = jnp.dot(w1_ref[...], taps, preferred_element_type=F32)
        for n, c in enumerate(pair):
            p = pre[:, n * ROWS : (n + 1) * ROWS]
            first_done(jnp.concatenate([p, p], axis=1), c)

    def second(c, done=0):
        h = whole(0, done, w2_ref, fh_ref, c + 1)
        store_both(sh_ref, inside(silu_of_half(h), c).astype(BF), c + 1)

    def block(c, done=0):
        h = silu_of_half(whole(1, done, w3_ref, sh_ref, c))
        h = (h + fh_ref[128:256, pl.ds((c + 2) * 2 * ROWS, 2 * ROWS)].astype(F32)).astype(BF)
        n, j = (0, c) if c < soon else (1, c - soon) if c < cols else (2, cols + HALO - 1 - c)
        count = (soon, HALO, HALO)[n]
        for s in range(2):
            at = (s * count + j) * 128
            bo_refs[n][at : at + 128, :] = h[:, s * ROWS : (s + 1) * ROWS]

    def project(n):
        p = jnp.dot(wo_refs[n][...], bo_refs[n][...], preferred_element_type=F32)
        size = (early, late, late)[n]
        noises = [nzs_ref[m].astype(F32) if n == 2 else nz_ref[m, parts[n], :] for m in range(2)]
        return p[:size] + noises[0], p[size:] + noises[1]

    def inputs_first(c):
        x = xb_ref[:, lanes(place(c))]
        store_taps(x1_ref, x, c + HALO)

    for c in range(cols):
        inputs_first(c)
    for c in range(1, cols - 1, 2):
        first_pair((c, c + 1))
    pltpu.make_async_copy(w2_ref, w2_ref, w_sem.at[0]).wait()
    w2_ref[...] = w2_ref[...] * BF(0.5)
    for c in range(2, cols - 2):
        second(c)
    pltpu.make_async_copy(w3_ref, w3_ref, w_sem.at[1]).wait()
    w3_ref[...] = w3_ref[...] * BF(0.5)
    for c in range(3, cols - 3):
        block(c)
    get_wout.wait()
    wo = wout_ref[...].astype(F32) * (1.0 / STEPS)
    none = jnp.zeros((CH, 128), F32)
    for n, (count, size) in enumerate(((soon, early), (HALO, late))):
        lhs = []
        for sums in range(2):
            for j in range(count):
                blocks = [wo if s <= sums and i == j else none for s in range(2) for i in range(count)]
                lhs.append(jnp.concatenate(blocks, axis=1))
            lhs.append(jnp.zeros((size - CH * count, 2 * 128 * count), F32))
        wo_refs[n][...] = jnp.concatenate(lhs, axis=0).astype(BF)

    halo_fast.wait_recv()
    for c in (-1, -2, -3):
        inputs_first(c)
    first_pair((0, -1))
    first_pair((-2,))
    for c in (1, 0, -1):
        second(c)
    for c in (2, 1, 0):
        block(c)

    def mids(d):
        def send(n, src, dst, tile):
            return remote(
                pg_ref.at[src],
                rx_ref.at[d - 1, dst],
                mid_send.at[d - 1, n],
                mid_recv.at[d - 1, n],
                k + d,
                tile,
            )

        return (
            send(0, facing, at_fast, fast),
            send(1, parts[0], own_soon, t),
            send(2, late_out, own_late_out, t),
        )

    mid = {d: mids(d) for d in range(1, groups)}
    near_fast = remote(
        pa_ref, rxs_ref, near_send, near_recv, k, fast
    )

    def put_sums(n):
        a, g = project(n)
        pg_ref[parts[n], :] = g.astype(BF)
        if n == 0:
            pa_ref[...] = a[:rim].astype(BF)
        return a

    def wait_mid(*ns):
        def f(d):
            for n in ns:
                mid[d][n].wait_recv()

        return f

    def start_soon(d):
        pl.semaphore_wait(down.at[d - 1], 1)
        mid[d][1].start()
        mid[d][0].start()

    a_soon = put_sums(0)
    near_fast.start()
    for_later(start_soon)

    ahead(soon)

    @pl.when(has_slow)
    def _():
        halo_slow.wait_recv()
        noise_slow.wait_recv()

    for c in range(cols, cols + FAR):
        inputs_first(c)
    for c in range(cols - 1, cols + 5, 2):
        first_pair((c, c + 1))
    for c in range(cols - 2, cols + 4):
        second(c, max(0, cols - c))
    for c in range(cols - 3, cols + 3):
        block(c, max(0, soon + 2 - c))
    a_late = put_sums(1)
    a_out = put_sums(2)

    for_later(lambda d: mid[d][2].start())

    rim_fast.wait_recv()
    near_fast.wait_recv()
    for_earlier(wait_mid(0, 1))

    def base_of(rows):
        base = st_ref[rows, :]
        for d in range(groups - 1):
            base = base + rx_ref[d, rows, :].astype(F32)
        return base

    def inputs_next(c, base, step, row):
        cov = xb_ref[:, lanes(place(c))].astype(F32)[CH:]
        for s, state in enumerate((base, base + step)):
            v = jnp.concatenate([state[row : row + CH], cov], axis=0)
            if c >= cols:
                v = v * slow_one
            store_taps(x2_ref, v.astype(BF), 2 * (c + HALO) + s)

    def next_columns(columns, rows, step, firsts, seconds, blocks, done):
        base = base_of(rows)
        for c in columns:
            inputs_next(c, base, step, row_of(c) - rows.start)
        for c in firsts:
            first(c)
        for n, c in enumerate(seconds):
            second(c, max(0, done - n))
        for n, c in enumerate(blocks):
            block(c, max(0, done - n))
        return base

    step = jnp.concatenate([rxs_ref[...].astype(F32), a_soon], axis=0)
    base = next_columns(
        range(-HALO, soon), pl.ds(0, rim + early), step, range(-2, soon - 1), range(-1, soon - 2), range(soon - 3), 0
    )
    base_ref[parts[0], :] = base[rim:]
    ahead(soon - 3)

    pl.when(has_slow)(rim_slow.wait_recv)
    for_earlier(wait_mid(2))
    base = next_columns(
        range(soon, cols + HALO),
        own_late_out,
        jnp.concatenate([a_late, a_out], axis=0),
        range(soon - 1, cols + 2),
        range(soon - 2, cols + 1),
        range(soon - 3, cols),
        2,
    )
    base_ref[parts[1], :] = base[:late]

    last = {
        d: remote(pd_ref, rxf_ref.at[d - 1], last_send.at[d - 1], last_recv.at[d - 1], k + d, t)
        for d in range(1, groups)
    }
    both = [project(n) for n in range(2)]
    for n, (a, g) in enumerate(both):
        pd_ref[parts[n], :] = (g - pg_ref[parts[n], :].astype(F32)).astype(BF)
    for_later(lambda d: last[d].start())
    (a_soon, g_soon), (a_late, g_late) = both

    def all_sent(*copies):
        for c in copies:
            c.wait_send()

    all_sent(halo_fast, rim_fast, near_fast)
    for_later(lambda d: all_sent(*mid[d]))

    pl.when(has_slow)(lambda: all_sent(halo_slow, rim_slow, noise_slow))

    for_earlier(lambda d: last[d].wait_recv())
    base = base_ref[...]
    for d in range(groups - 1):
        base = base + rxf_ref[d].astype(F32)
    sums = [
        base + jnp.concatenate(both, axis=0) for both in ((a_soon, a_late), (g_soon, g_late))
    ]

    def put_result(c, i):
        at = own_row(i)
        for s in range(2):
            out_ref[s, :, c, :] = sums[s][at : at + CH]

    either_way(put_result)

    for_later(lambda d: all_sent(last[d]))


def solution(mesh):
    groups, tiles = mesh.shape["step"], mesh.shape["tile"]

    def local(start_state, covariates, noise, embedding, w_in, w_first, w_second, w_out):
        cols = start_state.shape[1]
        wide = cols + 2 * HALO
        own = 48
        hbm = pl.BlockSpec(memory_space=pltpu.HBM)
        dma = pltpu.SemaphoreType.DMA
        w_in = jnp.swapaxes(w_in, 1, 2).reshape(144, 128)

        def body(*refs):
            kernel(groups, tiles, *refs)

        args = [
            pltpu.with_memory_space_constraint(v, pltpu.HBM)
            for v in (start_state, covariates, noise, embedding, w_in, w_first, w_second, w_out)
        ]
        return pl.pallas_call(
            body,
            out_shape=pltpu.VMEM((2, 4, cols, ROWS), F32),
            in_specs=[hbm] * 8,
            out_specs=pl.BlockSpec(memory_space=pltpu.VMEM),
            scratch_shapes=[
                pltpu.VMEM((CH, cols, ROWS), F32),
                pltpu.VMEM((12, cols, ROWS), BF),
                pltpu.VMEM((2, CH, cols, ROWS), F32),
                pltpu.VMEM((2, 128), F32),
                pltpu.VMEM((144, 128), BF),
                pltpu.VMEM((CH, 128), BF),
                pltpu.VMEM((12, cols, ROWS), F32),
                pltpu.VMEM((own + 32, ROWS), F32),
                pltpu.VMEM((own, ROWS), F32),
                pltpu.VMEM((16, (wide + HALO) * ROWS), BF),
                pltpu.VMEM((48, (wide + HALO) * ROWS), BF),
                pltpu.VMEM((48, wide * 2 * ROWS), BF),
                pltpu.VMEM((128, 144), BF),
                pltpu.VMEM((128, 1152), BF),
                pltpu.VMEM((128, 1152), BF),
                pltpu.VMEM((64, 256 * (cols - HALO)), BF),
                pltpu.VMEM((32, 256 * HALO), BF),
                pltpu.VMEM((128, 2 * ROWS), F32),
                pltpu.VMEM((2, own, ROWS), F32),
                pltpu.VMEM((2, 16, ROWS), BF),
                pltpu.VMEM((2, 16, ROWS), BF),
                pltpu.VMEM((384, (wide + 1) * 2 * ROWS), BF),
                pltpu.VMEM((384, (wide - 1) * 2 * ROWS), BF),
                pltpu.VMEM((4, 128, 2 * ROWS), F32),
                pltpu.VMEM((256 * (cols - HALO), ROWS), BF),
                pltpu.VMEM((256 * HALO, ROWS), BF),
                pltpu.VMEM((256 * HALO, ROWS), BF),
                pltpu.VMEM((16, ROWS), BF),
                pltpu.VMEM((own + 16, ROWS), BF),
                pltpu.VMEM((own, ROWS), BF),
                pltpu.VMEM((groups - 1, own + 32, ROWS), BF),
                pltpu.VMEM((16, ROWS), BF),
                pltpu.VMEM((groups - 1, own, ROWS), BF),
                dma((5,)),
                dma(()),
                dma((2,)),
                dma((2,)),
                dma((2,)),
                dma((2,)),
                dma((2,)),
                dma(()),
                dma(()),
                dma(()),
                dma(()),
                dma((groups - 1, 3)),
                dma((groups - 1, 3)),
                dma((groups - 1,)),
                dma((groups - 1,)),
                pltpu.SemaphoreType.REGULAR((groups - 1,)),
            ],
            compiler_params=pltpu.CompilerParams(
                collective_id=0, has_side_effects=True, vmem_limit_bytes=40 << 20
            ),
        )(*args)

    in_specs = (
        P(None, "tile", None),
        P(None, "tile", None),
        P("step", None, "tile", None),
        P("step", None),
        P(),
        P(),
        P(),
        P(),
    )
    out_specs = P("step", None, "tile", None)
    return jax.shard_map(local, mesh=mesh, in_specs=in_specs, out_specs=out_specs, check_vma=False)
```
